256 devices in a mesh: dp: 64 (over y, x, z_hi, core), mp: 4 (over z_lo).
Axes of the slice: x: 4, y: 4, z: 8 (z_hi: 2, z_lo: 4; z = z_hi * 4 + z_lo), core: 2. Of those that a mesh axis runs over, the one named last changes fastest.
Arguments:
- queries: bfloat16 [512, 4096], P('dp', 'mp'), may hold values from -1 to 1
- passages: bfloat16 [512, 4096], P('dp', 'mp'), may hold values from -1 to 1
- negatives: bfloat16 [512, 4096], P('dp', 'mp'), may hold values from -1 to 1
- hard_index: int32 [512], P('dp'), may hold values from 0 to 511
- layer_input: bfloat16 [256, 256, 4096], P('dp'), may hold values from -32 to 32
- lengths: int32 [256], P('dp'), may hold values from 1 to 256, as said below
- in_gain: bfloat16 [4096], replicated, may hold values from 0.5 to 1.5
- out_gain: bfloat16 [4096], replicated, may hold values from 0.5 to 1.5
- w_query: bfloat16 [4096, 2048], P('dp', 'mp'), may hold values from -1 to 1
- w_key: bfloat16 [4096, 512], P('dp', 'mp'), may hold values from -1 to 1
- w_value: bfloat16 [4096, 512], P('dp', 'mp'), may hold values from -0.09375 to 0.09375
- w_out: bfloat16 [2048, 4096], P('mp', 'dp'), may hold values from -0.125 to 0.125
- down_query: bfloat16 [4096, 16], replicated, may hold values from -0.09375 to 0.09375
- query_up_weight: bfloat16 [16, 2048], P(None, 'mp'), may hold values from -1.5 to 1.5
- down_value: bfloat16 [4096, 16], replicated, may hold values from -0.09375 to 0.09375
- value_up_weight: bfloat16 [16, 512], P(None, 'mp'), may hold values from -1.5 to 1.5
Outputs:
- loss: float32 [], replicated
- grad_query: float32 [512, 4096], P('dp', 'mp')
- grad_passage: float32 [512, 4096], P('dp', 'mp')
- grad_negative: float32 [512, 4096], P('dp', 'mp')
- grad_input: bfloat16 [256, 256, 4096], P('dp', 'mp')
- grad_down_query: float32 [4096, 16], replicated
- grad_up_query: float32 [16, 2048], P(None, 'mp')
- grad_down_value: float32 [4096, 16], replicated
- grad_up_value: float32 [16, 512], P(None, 'mp')
The draws below stay inside these ranges and needn't reach their ends.
Inputs may be any that keep to these rules, and one draw needn't show every extreme that they name: `lengths`: every draw has a passage of exactly 256 tokens.
All inputs are finite; a program needn't handle non-finite values.
Results may differ from the reference program's by a relative error of at most 0.02.
The reference program's roundings to bfloat16 on the way count: a program that leaves them out, or rounds other values in their place, can miss the bound.
Values may be sent and summed in bfloat16 or wider, within the bound.
No kernel may reach another device: no remote copies, remote signals or barrier semaphores. Data moves between devices by JAX's collectives and lax.ppermute only.
A program may use at most 192 MiB of HBM per device.

```python
import jax
import jax.numpy as jnp
from jax import lax

D = 4096
HEADS = 16
KVH = 4
HD = 128
RANK = 16
LEN = 256
PAIRS_DEV = 8
PASS_DEV = 4
PAIRS = 512
PASSAGES = 256
HQ = 2048
KV = 512
N_DP = 64
N_MP = 4


def shared_rows(key):
    return jax.random.normal(key, (PAIRS, D), jnp.float32)


def draw_passages(key, part):
    base_rows = shared_rows(key)
    return jnp.clip(base_rows * 0.015625, -1.0, 1.0).astype(jnp.bfloat16)


def draw_queries(key, part):
    key = jax.random.fold_in(key, 12)
    fresh_rows = jax.random.normal(key, (PAIRS, D), jnp.float32)
    return jnp.clip(fresh_rows * 0.015625, -1.0, 1.0).astype(jnp.bfloat16)


def draw_negatives(key, part):
    key = jax.random.fold_in(key, 14)
    fresh_rows = jax.random.normal(key, (PAIRS, D), jnp.float32)
    return jnp.clip(fresh_rows * 0.015625, -0.1, 0.1).astype(jnp.bfloat16)


def draw_layer_input(key, part):
    key = jax.random.fold_in(key, 15)
    fresh_rows = jax.random.normal(key, (PASSAGES, LEN, D), jnp.float32)
    return jnp.clip(fresh_rows, -8.0, 8.0).astype(jnp.bfloat16)


def draw_w_key(key, part):
    key = jax.random.fold_in(key, 16)
    fresh_rows = jax.random.normal(key, (D, KV), jnp.float32)
    return jnp.clip(fresh_rows * D ** (-0.5), -1.0, 1.0).astype(jnp.bfloat16)


def draw_w_query(key, part):
    key = jax.random.fold_in(key, 17)
    fresh_rows = jax.random.normal(key, (D, HQ), jnp.float32)
    return jnp.clip(fresh_rows * D ** (-0.5), -1.0, 1.0).astype(jnp.bfloat16)


def draw_lengths(key, part):
    key = jax.random.fold_in(key, 13)
    drawn = jax.random.randint(key, (PASSAGES,), 1, LEN + 1)
    target = jax.random.randint(jax.random.fold_in(key, 1), (), 0, PASSAGES)
    return jnp.where(jnp.arange(PASSAGES) == target, LEN, drawn).astype(jnp.int32)


def with_ends(values, rng, smallest, top_value):
    longest = values.shape.index(max(values.shape))
    spots = []
    for shift in (0, 1):
        where = [jax.random.randint(jax.random.fold_in(rng, axis), (), 0, length) for axis, length in enumerate(values.shape)]
        where[longest] = (where[longest] + shift) % values.shape[longest]
        spots.append(tuple(where))
    return values.at[spots[0]].set(smallest).at[spots[1]].set(top_value)


def shard_levels(key, dims, pieces, least, top_value):
    level = 1.0
    for axis_at, shards_of in pieces:
        steps = jax.random.uniform(jax.random.fold_in(jax.random.fold_in(key, 6), axis_at), (shards_of,), jnp.float32, least / len(pieces), top_value / len(pieces))
        level = level * jnp.repeat(jnp.exp(steps), dims[axis_at] // shards_of).reshape((-1,) + (1,) * (len(dims) - 1 - axis_at))
    return level


def bell_draw(key, extent, deviation, limit, pieces=(), kind=jnp.bfloat16):
    array = deviation * jax.random.normal(key, extent, jnp.float32)
    if pieces:
        array = array * shard_levels(key, extent, pieces, -0.22, 0.18)
    return jnp.clip(array, -limit, limit).astype(kind)


def setup_inputs(seed: int = 0) -> dict:
    key_list = jax.random.split(jax.random.key(seed), 17)
    return {
        "queries": draw_queries(jax.random.fold_in(key_list[16], 71), 0),
        "passages": draw_passages(jax.random.fold_in(key_list[16], 71), 0),
        "negatives": draw_negatives(jax.random.fold_in(key_list[16], 71), 0),
        "hard_index": with_ends(jax.random.randint(key_list[3], (PAIRS,), 0, PAIRS), jax.random.fold_in(key_list[3], 1), 0, PAIRS - 1).astype(jnp.int32),
        "layer_input": draw_layer_input(jax.random.fold_in(key_list[16], 71), 0),
        "lengths": draw_lengths(jax.random.fold_in(key_list[16], 71), 0),
        "in_gain": jnp.clip(1.0 + 0.1 * jax.random.normal(key_list[6], (D,), jnp.float32), 0.5, 1.5).astype(jnp.bfloat16),
        "out_gain": jnp.clip(1.0 + 0.1 * jax.random.normal(key_list[7], (D,), jnp.float32), 0.5, 1.5).astype(jnp.bfloat16),
        "w_query": draw_w_query(jax.random.fold_in(key_list[16], 71), 0),
        "w_key": draw_w_key(jax.random.fold_in(key_list[16], 71), 0),
        "w_value": bell_draw(key_list[10], (D, KV), D ** -0.5, 0.09375, ((0, 64), (1, 4))),
        "w_out": bell_draw(key_list[11], (HQ, D), HQ ** -0.5, 0.125, ((0, 4), (1, 64))),
        "down_query": bell_draw(key_list[12], (D, RANK), D ** -0.5, 0.09375),
        "query_up_weight": bell_draw(key_list[13], (RANK, HQ), RANK ** -0.5, 1.5, ((1, 4),)),
        "down_value": bell_draw(key_list[14], (D, RANK), D ** -0.5, 0.09375),
        "value_up_weight": bell_draw(key_list[15], (RANK, KV), RANK ** -0.5, 1.5, ((1, 4),)),
    }


EPSILON = 1e-05
SOFTMAX_TEMPER = 0.01
ADAPTER_SCALE = 2.0
ROPE_BASE = 10000.0
MATMUL_ACCURACY = lax.Precision.HIGHEST

def angle_table(seq_len, head_dim):
    half_dim = head_dim // 2
    frequency = ROPE_BASE ** (-(jnp.arange(half_dim, dtype=jnp.float32) * 2.0 / head_dim))
    angles = jnp.arange(seq_len, dtype=jnp.float32)[:, None] * frequency[None, :]
    return (jnp.cos(angles), jnp.sin(angles))

def rotate(field, cosine, sine):
    half_dim = field.shape[-1] // 2
    leading = field[..., :half_dim]
    trailing = field[..., half_dim:]
    return jnp.concatenate([leading * cosine - trailing * sine, trailing * cosine + leading * sine], axis=-1)

def unit_rows(embedded):
    values = embedded.astype(jnp.float32)
    row_length = jnp.sqrt(lax.optimization_barrier(jnp.sum(values * values, axis=1, keepdims=True)))
    return (values / row_length, row_length)

def tangent(d_unit, unit, row_length):
    return (d_unit - lax.optimization_barrier(jnp.sum(d_unit * unit, axis=1, keepdims=True)) * unit) / row_length

def contrast(queries, passages, negatives, hard_index):
    query_unit, query_len = unit_rows(queries)
    passage_unit, passage_len = unit_rows(passages)
    negative_unit, negative_len = unit_rows(negatives)
    query_bfloat_rounded = query_unit.astype(jnp.bfloat16)
    passage_bfloat_rounded = passage_unit.astype(jnp.bfloat16)
    negative_round = negative_unit.astype(jnp.bfloat16)
    similarity_scores = jnp.dot(query_bfloat_rounded, passage_bfloat_rounded.T, preferred_element_type=jnp.float32) / SOFTMAX_TEMPER
    selected_entries = jnp.take(negative_round, hard_index, axis=0)
    hardneg_score = lax.optimization_barrier(jnp.sum(query_bfloat_rounded.astype(jnp.float32) * selected_entries.astype(jnp.float32), axis=1)) / SOFTMAX_TEMPER
    target_labels = jnp.eye(PAIRS, dtype=jnp.float32)
    row_top = jnp.maximum(lax.optimization_barrier(jnp.max(similarity_scores, axis=1)), hardneg_score)
    shifted_logits = jnp.exp(similarity_scores - row_top[:, None])
    hardneg_exponential = jnp.exp(hardneg_score - row_top)
    exponential_total = lax.optimization_barrier(jnp.sum(shifted_logits, axis=1)) + hardneg_exponential
    per_query = row_top + jnp.log(exponential_total) - lax.optimization_barrier(jnp.sum(similarity_scores * target_labels, axis=1))
    loss = jnp.sum(per_query) / PAIRS
    score_gradient = ((shifted_logits / exponential_total[:, None] - target_labels) / SOFTMAX_TEMPER).astype(jnp.bfloat16)
    hardneg_gradient = (hardneg_exponential / exponential_total / SOFTMAX_TEMPER).astype(jnp.bfloat16)
    query_grad = jnp.dot(score_gradient, passage_bfloat_rounded, preferred_element_type=jnp.float32)
    query_grad = query_grad + hardneg_gradient.astype(jnp.float32)[:, None] * selected_entries.astype(jnp.float32)
    passage_grad = jnp.dot(score_gradient.T, query_bfloat_rounded, preferred_element_type=jnp.float32)
    weighted = hardneg_gradient.astype(jnp.float32)[:, None] * query_bfloat_rounded.astype(jnp.float32)
    negative_grad = jax.ops.segment_sum(weighted, hard_index, num_segments=PAIRS)
    return (loss, tangent(query_grad, query_unit, query_len), tangent(passage_grad, passage_unit, passage_len), tangent(negative_grad, negative_unit, negative_len))

def reference(queries, passages, negatives, hard_index, layer_input, lengths, in_gain, out_gain, w_query, w_key, w_value, w_out, down_query, query_up_weight, down_value, value_up_weight):
    loss, grad_query, grad_passage, grad_negative = contrast(queries, passages, negatives, hard_index)
    cotangents = grad_passage.reshape(N_DP, PAIRS_DEV, D)[:, :PASS_DEV].reshape(PASSAGES, D)
    cosine, sine = angle_table(LEN, HD)
    group_size = HEADS // KVH
    query_cols = HQ // N_MP
    kv_cols = KV // N_MP
    score_scale = HD ** (-0.5)
    gain_in = in_gain.astype(jnp.float32)
    gain_out = out_gain.astype(jnp.float32)
    positions = jnp.arange(LEN)

    def rerun_passage(totals, entry):
        layer_rows, length_now, cotangent = entry
        x_float = layer_rows.astype(jnp.float32)
        inv_rms = lax.rsqrt(lax.optimization_barrier(jnp.mean(x_float * x_float, axis=1, keepdims=True)) + EPSILON)
        normed = (x_float * inv_rms * gain_in).astype(jnp.bfloat16)
        keys_pre = jnp.dot(normed, w_key, preferred_element_type=jnp.float32)
        value_lowrank = jnp.dot(normed, down_value, preferred_element_type=jnp.float32).astype(jnp.bfloat16)
        value_before_adapter = jnp.dot(normed, w_value, preferred_element_type=jnp.float32)
        value_before_adapter = value_before_adapter + ADAPTER_SCALE * jnp.dot(value_lowrank, value_up_weight, preferred_element_type=jnp.float32)
        key_rows = rotate(keys_pre.reshape(LEN, KVH, HD), cosine[:, None, :], sine[:, None, :]).astype(jnp.bfloat16)
        value_rows = value_before_adapter.astype(jnp.bfloat16).reshape(LEN, KVH, HD)
        last_pos = length_now - 1
        n_last = lax.dynamic_slice_in_dim(normed, last_pos, 1, 0)
        query_lowrank = jnp.dot(n_last, down_query, preferred_element_type=jnp.float32).astype(jnp.bfloat16)
        query_before_rotation = jnp.dot(n_last, w_query, preferred_element_type=jnp.float32)
        query_before_rotation = query_before_rotation + ADAPTER_SCALE * jnp.dot(query_lowrank, query_up_weight, preferred_element_type=jnp.float32)
        cos_last = lax.dynamic_slice_in_dim(cosine, last_pos, 1, 0)
        sin_last = lax.dynamic_slice_in_dim(sine, last_pos, 1, 0)
        query_heads = rotate(query_before_rotation.reshape(HEADS, HD), cos_last, sin_last).astype(jnp.bfloat16)
        query_group = query_heads.reshape(KVH, group_size, HD).astype(jnp.float32)
        key_float = key_rows.astype(jnp.float32)
        value_float = value_rows.astype(jnp.float32)
        logits = jnp.einsum('kgd,lkd->kgl', query_group, key_float, precision=MATMUL_ACCURACY) * score_scale
        visible = positions <= last_pos
        logits = jnp.where(visible, logits, -1e+30)
        row_peak = lax.optimization_barrier(jnp.max(logits, axis=-1, keepdims=True))
        shifted_logits = jnp.exp(logits - row_peak)
        attention = shifted_logits / lax.optimization_barrier(jnp.sum(shifted_logits, axis=-1, keepdims=True))
        attention_round = attention.astype(jnp.bfloat16).astype(jnp.float32)
        mixed_heads = jnp.einsum('kgl,lkd->kgd', attention_round, value_float, precision=MATMUL_ACCURACY)
        mixed_heads = mixed_heads.astype(jnp.bfloat16).reshape(1, HQ)
        hidden = lax.dynamic_slice_in_dim(x_float, last_pos, 1, 0) + jnp.dot(mixed_heads, w_out, preferred_element_type=jnp.float32)
        inv_hidden = lax.rsqrt(lax.optimization_barrier(jnp.mean(hidden * hidden, axis=1, keepdims=True)) + EPSILON)
        scaled = gain_out * cotangent[None, :]
        d_hidden = scaled * inv_hidden - hidden * inv_hidden ** 3 * lax.optimization_barrier(jnp.mean(hidden * scaled, axis=1, keepdims=True))
        d_mixed = jnp.dot(d_hidden.astype(jnp.bfloat16), w_out.T, preferred_element_type=jnp.float32)
        d_mixed = d_mixed.reshape(KVH, group_size, HD)
        d_attention = jnp.einsum('kgd,lkd->kgl', d_mixed, value_float, precision=MATMUL_ACCURACY)
        d_logits = attention * (d_attention - lax.optimization_barrier(jnp.sum(attention * d_attention, axis=-1, keepdims=True)))
        grad_value_rows = jnp.einsum('kgl,kgd->lkd', attention_round, d_mixed, precision=MATMUL_ACCURACY).reshape(LEN, KV)
        d_query = jnp.einsum('kgl,lkd->kgd', d_logits, key_float, precision=MATMUL_ACCURACY) * score_scale
        d_keys = jnp.einsum('kgl,kgd->lkd', d_logits, query_group, precision=MATMUL_ACCURACY) * score_scale
        grad_query_before_rotation = rotate(d_query.reshape(HEADS, HD), cos_last, -sin_last).reshape(1, HQ)
        d_keys_pre = rotate(d_keys, cosine[:, None, :], -sine[:, None, :]).reshape(LEN, KV)
        query_up_gradient = ADAPTER_SCALE * jnp.dot(query_lowrank.astype(jnp.float32).T, grad_query_before_rotation, precision=MATMUL_ACCURACY)
        value_up_gradient = ADAPTER_SCALE * jnp.dot(value_lowrank.astype(jnp.float32).T, grad_value_rows, precision=MATMUL_ACCURACY)
        grad_query_lowrank = (ADAPTER_SCALE * jnp.dot(grad_query_before_rotation, query_up_weight.astype(jnp.float32).T, precision=MATMUL_ACCURACY)).astype(jnp.bfloat16)
        grad_value_lowrank = (ADAPTER_SCALE * jnp.dot(grad_value_rows, value_up_weight.astype(jnp.float32).T, precision=MATMUL_ACCURACY)).astype(jnp.bfloat16)
        g_down_query = jnp.dot(n_last.T, grad_query_lowrank, preferred_element_type=jnp.float32)
        g_down_value = jnp.dot(normed.T, grad_value_lowrank, preferred_element_type=jnp.float32)
        at_last = (positions == last_pos)[:, None]
        keys_round = d_keys_pre.astype(jnp.bfloat16)
        values_round = grad_value_rows.astype(jnp.bfloat16)
        query_bfloat_rounded = grad_query_before_rotation.astype(jnp.bfloat16)
        d_normed = jnp.zeros((LEN, D), jnp.float32)
        for section in range(N_MP):
            kv_lo = section * kv_cols
            kv_hi = kv_lo + kv_cols
            q_lo = section * query_cols
            q_hi = q_lo + query_cols
            group_term = jnp.dot(keys_round[:, kv_lo:kv_hi], w_key[:, kv_lo:kv_hi].T, preferred_element_type=jnp.float32)
            group_term = group_term + jnp.dot(values_round[:, kv_lo:kv_hi], w_value[:, kv_lo:kv_hi].T, preferred_element_type=jnp.float32)
            query_term = jnp.dot(query_bfloat_rounded[:, q_lo:q_hi], w_query[:, q_lo:q_hi].T, preferred_element_type=jnp.float32)
            group_term = group_term + jnp.where(at_last, query_term, 0.0)
            d_normed = d_normed + lax.optimization_barrier(group_term.astype(jnp.bfloat16)).astype(jnp.float32)
        d_normed = d_normed + jnp.dot(grad_value_lowrank, down_value.T, preferred_element_type=jnp.float32)
        d_normed = d_normed + jnp.where(at_last, jnp.dot(grad_query_lowrank, down_query.T, preferred_element_type=jnp.float32), 0.0)
        d_input = gain_in * d_normed * inv_rms - x_float * inv_rms ** 3 * lax.optimization_barrier(jnp.mean(x_float * gain_in * d_normed, axis=1, keepdims=True))
        d_input = d_input + jnp.where(at_last, d_hidden, 0.0)
        totals = (totals[0] + g_down_query, totals[1] + query_up_gradient, totals[2] + g_down_value, totals[3] + value_up_gradient)
        return (totals, d_input.astype(jnp.bfloat16))
    start_totals = (jnp.zeros((D, RANK), jnp.float32), jnp.zeros((RANK, HQ), jnp.float32), jnp.zeros((D, RANK), jnp.float32), jnp.zeros((RANK, KV), jnp.float32))
    totals, grad_input = lax.scan(rerun_passage, start_totals, (layer_input, lengths, cotangents))
    return (loss, grad_query, grad_passage, grad_negative, grad_input, totals[0], totals[1], totals[2], totals[3])
```

```python
import jax
import jax.numpy as jnp
from jax import lax
from jax.sharding import PartitionSpec as P

HD = 128


EPSILON = 1e-05
SOFTMAX_TEMPER = 0.01
ADAPTER_SCALE = 2.0
ROPE_BASE = 10000.0
MATMUL_ACCURACY = lax.Precision.HIGHEST


def angle_table(seq_len, head_dim):
    half_dim = head_dim // 2
    frequency = ROPE_BASE ** (-(jnp.arange(half_dim, dtype=jnp.float32) * 2.0 / head_dim))
    angles = jnp.arange(seq_len, dtype=jnp.float32)[:, None] * frequency[None, :]
    return (jnp.cos(angles), jnp.sin(angles))


def rotate(field, cosine, sine):
    half_dim = field.shape[-1] // 2
    leading = field[..., :half_dim]
    trailing = field[..., half_dim:]
    return jnp.concatenate(
        [leading * cosine - trailing * sine, trailing * cosine + leading * sine], axis=-1
    )


def shifted(value, axis_name, shift):
    size = lax.axis_size(axis_name)
    return lax.ppermute(value, axis_name, [(i, (i + shift) % size) for i in range(size)])


def ring_sum(value):
    one, two, three = (shifted(value, "mp", k) for k in (1, 2, 3))
    return (value + two) + (one + three)


def ring_gather(value):
    parts = jnp.stack([value] + [shifted(value, "mp", k) for k in (1, 2, 3)])
    place = lax.axis_index("mp")
    order = (place - lax.iota(jnp.int32, 4)) % 4
    return jnp.take(parts, order, axis=0)


def spread(value, axis_name):
    size = lax.axis_size(axis_name)
    return lax.all_to_all(
        jnp.broadcast_to(value[None], (size,) + value.shape), axis_name, 0, 0, tiled=True
    )


def on_device(
    queries,
    passages,
    negatives,
    hard_index,
    layer_input,
    lengths,
    in_gain,
    out_gain,
    w_query,
    w_key,
    w_value,
    w_out,
    down_query,
    query_up_weight,
    down_value,
    value_up_weight,
):
    dp = lax.axis_size("dp")
    mp = lax.axis_size("mp")
    place = lax.axis_index("mp")
    pairs_dev, feature_dev = queries.shape
    total_pairs = pairs_dev * dp
    pass_dev, seq_len, width = layer_input.shape
    kv_cols = w_key.shape[1]
    q_cols = w_query.shape[1]

    kv_shard = jnp.concatenate([w_key, w_value], axis=1)
    kv_rows = lax.all_gather(kv_shard, "mp", axis=1, tiled=True)
    kv_all = lax.all_gather(kv_rows, "dp", axis=0, tiled=True)
    qo_all = lax.all_gather(
        jnp.concatenate([w_query, w_out.T], axis=1), "dp", axis=0, tiled=True
    )
    query_full = qo_all[:, :q_cols]
    out_t = qo_all[:, q_cols:]
    up_value_all = lax.all_gather(value_up_weight, "mp", axis=1, tiled=True)

    embeds = jnp.stack([queries, passages, negatives]).astype(jnp.float32)
    square_sums = ring_sum(jnp.sum(embeds * embeds, axis=2))
    embed_len = jnp.sqrt(square_sums)[:, :, None]
    units = embeds / embed_len
    rounds = units.astype(jnp.bfloat16)
    candidates = spread(rounds[1:].reshape(2 * pairs_dev, feature_dev), "dp")
    queries_all = spread(rounds[0], "dp")
    span = 2 * pairs_dev
    cand_rows = candidates.reshape(dp * span, feature_dev)
    score_part = jnp.einsum(
        "id,jd->ij", rounds[0], cand_rows, preferred_element_type=jnp.float32
    )
    scores = ring_sum(score_part) / SOFTMAX_TEMPER
    column = lax.iota(jnp.int32, dp * span)[None, :]
    is_passage = column % span < pairs_dev
    own_ids = lax.iota(jnp.int32, pairs_dev)
    is_label = column == lax.axis_index("dp") * span + own_ids[:, None]
    hard_column = (hard_index // pairs_dev) * span + pairs_dev + hard_index % pairs_dev
    is_candidate = is_passage | (column == hard_column[:, None])
    masked = jnp.where(is_candidate, scores, -jnp.inf)
    row_top = jnp.max(masked, axis=1)
    exps = jnp.exp(masked - row_top[:, None])
    exp_total = jnp.sum(exps, axis=1)
    per_query = row_top + jnp.log(exp_total) - jnp.sum(jnp.where(is_label, scores, 0.0), axis=1)
    local_total = jnp.sum(per_query)
    score_gradient = (
        (exps / exp_total[:, None] - is_label.astype(jnp.float32)) / SOFTMAX_TEMPER
    ).astype(jnp.bfloat16)
    query_grad = jnp.einsum(
        "ij,jd->id", score_gradient, cand_rows, preferred_element_type=jnp.float32
    )
    by_owner = score_gradient.reshape(pairs_dev, dp, span).transpose(1, 0, 2)
    own_columns = lax.all_to_all(by_owner, "dp", 0, 0, tiled=True)
    both_grads = jnp.einsum(
        "sic,sid->cd", own_columns, queries_all, preferred_element_type=jnp.float32
    )
    grads = jnp.concatenate([query_grad, both_grads], axis=0).reshape(units.shape)
    inner_sums = ring_sum(jnp.sum(grads * units, axis=2))[:, :, None]
    embed_grads = (grads - inner_sums * units) / embed_len
    cotangent = (
        ring_gather(embed_grads[1, :pass_dev]).transpose(1, 0, 2).reshape(pass_dev, width)
    )

    gain_in = in_gain.astype(jnp.float32)
    gain_out = out_gain.astype(jnp.float32)
    x_float = layer_input.astype(jnp.float32)
    inv_rms = lax.rsqrt(jnp.mean(x_float * x_float, axis=-1, keepdims=True) + EPSILON)
    normed = (x_float * inv_rms * gain_in).astype(jnp.bfloat16)
    last_pos = lengths - 1
    n_last = jnp.take_along_axis(normed, last_pos[:, None, None], axis=1)[:, 0]
    x_last = jnp.take_along_axis(layer_input, last_pos[:, None, None], axis=1)[:, 0].astype(
        jnp.float32
    )
    value_lowrank = jnp.einsum(
        "pld,dr->plr", normed, down_value, preferred_element_type=jnp.float32
    ).astype(jnp.bfloat16)
    query_lowrank = jnp.dot(n_last, down_query, preferred_element_type=jnp.float32).astype(
        jnp.bfloat16
    )
    group_cols = 2 * kv_cols
    kv_own = lax.dynamic_slice_in_dim(kv_all, place * group_cols, group_cols, 1)
    group_size = q_cols // kv_cols
    score_scale = HD ** (-0.5)
    cosine, sine = angle_table(seq_len, HD)
    kv_pre = jnp.einsum("pld,dc->plc", normed, kv_own, preferred_element_type=jnp.float32)
    value_rows = (
        kv_pre[:, :, kv_cols:]
        + ADAPTER_SCALE
        * jnp.einsum(
            "plr,rc->plc", value_lowrank, value_up_weight, preferred_element_type=jnp.float32
        )
    ).astype(jnp.bfloat16)
    key_rows = rotate(kv_pre[:, :, :kv_cols], cosine[None], sine[None]).astype(jnp.bfloat16)
    query_before_rotation = jnp.dot(
        n_last, query_full, preferred_element_type=jnp.float32
    ) + ADAPTER_SCALE * jnp.dot(
        query_lowrank, query_up_weight, preferred_element_type=jnp.float32
    )
    cos_last = cosine[last_pos][:, None, :]
    sin_last = sine[last_pos][:, None, :]
    query_rot = rotate(
        query_before_rotation.reshape(pass_dev, group_size, HD), cos_last, sin_last
    ).astype(jnp.bfloat16)
    logits = (
        jnp.einsum("pgd,pld->pgl", query_rot, key_rows, preferred_element_type=jnp.float32)
        * score_scale
    )
    visible = lax.iota(jnp.int32, seq_len)[None, :] <= last_pos[:, None]
    logits = jnp.where(visible[:, None, :], logits, -1e30)
    row_peak = jnp.max(logits, axis=-1, keepdims=True)
    exponent_att = jnp.exp(logits - row_peak)
    attention = exponent_att / jnp.sum(exponent_att, axis=-1, keepdims=True)
    attention_round = attention.astype(jnp.bfloat16)
    mixed_heads = (
        jnp.einsum("pgl,pld->pgd", attention_round, value_rows, preferred_element_type=jnp.float32)
        .astype(jnp.bfloat16)
        .reshape(pass_dev, q_cols)
    )
    out_part = jnp.einsum("pc,dc->pd", mixed_heads, out_t, preferred_element_type=jnp.float32)
    hidden = x_last + ring_sum(out_part)

    inv_hidden = lax.rsqrt(jnp.mean(hidden * hidden, axis=-1, keepdims=True) + EPSILON)
    scaled = gain_out * cotangent
    d_hidden = scaled * inv_hidden - hidden * inv_hidden**3 * jnp.mean(
        hidden * scaled, axis=-1, keepdims=True
    )
    d_mixed = jnp.dot(
        d_hidden.astype(jnp.bfloat16), out_t, preferred_element_type=jnp.float32
    ).reshape(pass_dev, group_size, HD)
    value_float = value_rows.astype(jnp.float32)
    key_float = key_rows.astype(jnp.float32)
    d_attention = jnp.einsum("pgd,pld->pgl", d_mixed, value_float, precision=MATMUL_ACCURACY)
    d_logits = attention * (d_attention - jnp.sum(attention * d_attention, axis=-1, keepdims=True))
    d_values = jnp.einsum(
        "pgl,pgd->pld", attention_round.astype(jnp.float32), d_mixed, precision=MATMUL_ACCURACY
    )
    d_query = (
        jnp.einsum("pgl,pld->pgd", d_logits, key_float, precision=MATMUL_ACCURACY) * score_scale
    )
    d_keys = (
        jnp.einsum(
            "pgl,pgd->pld", d_logits, query_rot.astype(jnp.float32), precision=MATMUL_ACCURACY
        )
        * score_scale
    )
    d_query_pre = rotate(d_query, cos_last, -sin_last).reshape(pass_dev, q_cols)
    d_keys_pre = rotate(d_keys, cosine[None], -sine[None])

    tok_span = seq_len // mp
    first_tok = place * tok_span
    d_kv = jnp.concatenate([d_keys_pre, d_values], axis=2).astype(jnp.bfloat16)
    d_kv_send = d_kv.reshape(pass_dev, mp, tok_span, group_cols).transpose(1, 0, 2, 3)
    d_kv_own = lax.all_to_all(d_kv_send, "mp", 0, 0, tiled=True)
    query_back = jnp.einsum(
        "pc,dc->pd", d_query_pre.astype(jnp.bfloat16), query_full, preferred_element_type=jnp.float32
    )
    du_query_part = ADAPTER_SCALE * jnp.einsum(
        "pc,rc->pr",
        d_query_pre,
        query_up_weight.astype(jnp.float32),
        precision=MATMUL_ACCURACY,
    )
    rank = du_query_part.shape[1]
    shared = ring_gather(jnp.concatenate([query_back, du_query_part], axis=1))
    query_back_all = shared[:, :, :width]
    du_query = jnp.sum(shared[:, :, width:], axis=0).astype(jnp.bfloat16)
    up_query_part = ADAPTER_SCALE * jnp.einsum(
        "pr,pc->rc", query_lowrank.astype(jnp.float32), d_query_pre, precision=MATMUL_ACCURACY
    )
    up_value_part = ADAPTER_SCALE * jnp.einsum(
        "plr,plc->rc", value_lowrank.astype(jnp.float32), d_values, precision=MATMUL_ACCURACY
    )
    d_values_own = d_kv_own[:, :, :, kv_cols:]
    up_value_groups = up_value_all.reshape(rank, mp, kv_cols)
    du_value = (
        ADAPTER_SCALE
        * jnp.einsum(
            "gptc,rgc->ptr", d_values_own, up_value_groups, preferred_element_type=jnp.float32
        )
    ).astype(jnp.bfloat16)

    x_local = lax.dynamic_slice_in_dim(layer_input, first_tok, tok_span, 1).astype(jnp.float32)
    rms_local = lax.dynamic_slice_in_dim(inv_rms, first_tok, tok_span, 1)
    normed_local = lax.dynamic_slice_in_dim(normed, first_tok, tok_span, 1)
    down_value_part = jnp.einsum(
        "ptr,ptd->rd", du_value, normed_local, preferred_element_type=jnp.float32
    )
    mine = (lax.iota(jnp.int32, pass_dev) % mp == place)[:, None]
    down_query_part = jnp.einsum(
        "pr,pd->rd",
        jnp.where(mine, du_query, jnp.zeros_like(du_query)),
        n_last,
        preferred_element_type=jnp.float32,
    )
    down_part = jnp.concatenate([down_query_part, down_value_part], axis=0).reshape(dp, -1)
    head_part = jnp.concatenate(
        [up_query_part.reshape(dp, -1), up_value_part.reshape(dp, -1)], axis=1
    )
    loss_part = jnp.broadcast_to(local_total / dp, (dp, 1))
    parts = jnp.concatenate([down_part, head_part, loss_part], axis=1)
    n_down = down_part.shape[1]
    n_head = head_part.shape[1]
    padded = -(-parts.shape[1] // 1024) * 1024
    parts = jnp.pad(parts, ((0, 0), (0, padded - parts.shape[1]))).reshape(dp, -1, 128)
    reduced = jnp.sum(lax.all_to_all(parts, "dp", 0, 0, tiled=True), axis=0)
    down_rows = n_down // 128
    reduced = jnp.concatenate([ring_sum(reduced[:down_rows]), reduced[down_rows:]], axis=0)
    totals = spread(reduced, "dp").reshape(dp, -1)
    grad_down = totals[:, :n_down].reshape(2 * rank, width)
    grad_down_query = grad_down[:rank].T
    grad_down_value = grad_down[rank:].T
    n_up_query = q_cols * rank // dp
    grad_up_query = totals[:, n_down : n_down + n_up_query].reshape(rank, q_cols)
    grad_up_value = totals[:, n_down + n_up_query : n_down + n_head].reshape(rank, kv_cols)
    loss = jnp.sum(totals[:, n_down + n_head]) / total_pairs

    tok_ids = first_tok + lax.iota(jnp.int32, tok_span)
    at_local = (tok_ids[None, :] == last_pos[:, None])[:, :, None]
    d_normed = jnp.einsum(
        "ptr,dr->ptd", du_value, down_value, preferred_element_type=jnp.float32
    )
    query_adapter = jnp.einsum(
        "pr,dr->pd", du_query, down_query, preferred_element_type=jnp.float32
    )
    d_normed = d_normed + jnp.where(at_local, query_adapter[:, None, :], 0.0)
    for group in range(mp):
        term = jnp.einsum(
            "ptc,dc->ptd",
            d_kv_own[group],
            kv_all[:, group * group_cols : (group + 1) * group_cols],
            preferred_element_type=jnp.float32,
        )
        term = term + jnp.where(at_local, query_back_all[group][:, None, :], 0.0)
        d_normed = d_normed + term.astype(jnp.bfloat16).astype(jnp.float32)
    d_input = gain_in * d_normed * rms_local - x_local * rms_local**3 * jnp.mean(
        x_local * gain_in * d_normed, axis=-1, keepdims=True
    )
    d_input = d_input + jnp.where(at_local, d_hidden[:, None, :], 0.0)
    grad_input = d_input.astype(jnp.bfloat16)
    return (
        loss,
        embed_grads[0],
        embed_grads[1],
        embed_grads[2],
        grad_input,
        grad_down_query,
        grad_up_query,
        grad_down_value,
        grad_up_value,
    )


def solution(mesh):
    in_specs = (
        P("dp", "mp"),
        P("dp", "mp"),
        P("dp", "mp"),
        P("dp"),
        P("dp", None, None),
        P("dp"),
        P(),
        P(),
        P("dp", "mp"),
        P("dp", "mp"),
        P("dp", "mp"),
        P("mp", "dp"),
        P(),
        P(None, "mp"),
        P(),
        P(None, "mp"),
    )
    out_specs = (
        P(),
        P("dp", "mp"),
        P("dp", "mp"),
        P("dp", "mp"),
        P("dp", "mp", None),
        P(),
        P(None, "mp"),
        P(),
        P(None, "mp"),
    )
    return jax.shard_map(
        on_device, mesh=mesh, in_specs=in_specs, out_specs=out_specs, check_vma=False
    )
```

```python
import jax
import jax.numpy as jnp
from jax import lax
from jax.sharding import PartitionSpec as P

HD = 128


EPSILON = 1e-05
SOFTMAX_TEMPER = 0.01
ADAPTER_SCALE = 2.0
ROPE_BASE = 10000.0
MATMUL_ACCURACY = lax.Precision.HIGHEST


def angle_table(seq_len, head_dim):
    half_dim = head_dim // 2
    frequency = ROPE_BASE ** (-(jnp.arange(half_dim, dtype=jnp.float32) * 2.0 / head_dim))
    angles = jnp.arange(seq_len, dtype=jnp.float32)[:, None] * frequency[None, :]
    return (jnp.cos(angles), jnp.sin(angles))


def rotate(field, cosine, sine):
    half_dim = field.shape[-1] // 2
    leading = field[..., :half_dim]
    trailing = field[..., half_dim:]
    return jnp.concatenate(
        [leading * cosine - trailing * sine, trailing * cosine + leading * sine], axis=-1
    )


def shifted(value, axis_name, shift):
    size = lax.axis_size(axis_name)
    return lax.ppermute(value, axis_name, [(i, (i + shift) % size) for i in range(size)])


def ring_sum(value):
    one, two, three = (shifted(value, "mp", k) for k in (1, 2, 3))
    return (value + two) + (one + three)


def ring_gather(value):
    parts = jnp.stack([value] + [shifted(value, "mp", k) for k in (1, 2, 3)])
    place = lax.axis_index("mp")
    order = (place - lax.iota(jnp.int32, 4)) % 4
    return jnp.take(parts, order, axis=0)


def spread(value, axis_name):
    size = lax.axis_size(axis_name)
    return lax.all_to_all(
        jnp.broadcast_to(value[None], (size,) + value.shape), axis_name, 0, 0, tiled=True
    )


def on_device(
    queries,
    passages,
    negatives,
    hard_index,
    layer_input,
    lengths,
    in_gain,
    out_gain,
    w_query,
    w_key,
    w_value,
    w_out,
    down_query,
    query_up_weight,
    down_value,
    value_up_weight,
):
    dp = lax.axis_size("dp")
    mp = lax.axis_size("mp")
    place = lax.axis_index("mp")
    pairs_dev, feature_dev = queries.shape
    total_pairs = pairs_dev * dp
    pass_dev, seq_len, width = layer_input.shape
    kv_cols = w_key.shape[1]
    q_cols = w_query.shape[1]

    kv_rows = ring_gather(jnp.concatenate([w_key, w_value], axis=1))
    shard = jnp.concatenate([w_query, w_out.T, *kv_rows], axis=1)
    weights = lax.all_gather(shard, "dp", axis=0, tiled=True)
    query_full = weights[:, :q_cols]
    out_t = weights[:, q_cols : 2 * q_cols]
    kv_all = weights[:, 2 * q_cols :]

    embeds = jnp.stack([queries, passages, negatives]).astype(jnp.float32)
    square_sums = ring_sum(jnp.sum(embeds * embeds, axis=2))
    embed_len = jnp.sqrt(square_sums)[:, :, None]
    units = embeds / embed_len
    rounds = units.astype(jnp.bfloat16)
    candidates = spread(rounds[1:].reshape(2 * pairs_dev, feature_dev), "dp")
    queries_all = spread(rounds[0], "dp")
    span = 2 * pairs_dev
    cand_rows = candidates.reshape(dp * span, feature_dev)
    score_part = jnp.einsum(
        "id,jd->ij", rounds[0], cand_rows, preferred_element_type=jnp.float32
    )
    scores = ring_sum(score_part) / SOFTMAX_TEMPER
    column = lax.iota(jnp.int32, dp * span)[None, :]
    is_passage = column % span < pairs_dev
    own_ids = lax.iota(jnp.int32, pairs_dev)
    is_label = column == lax.axis_index("dp") * span + own_ids[:, None]
    hard_column = (hard_index // pairs_dev) * span + pairs_dev + hard_index % pairs_dev
    is_candidate = is_passage | (column == hard_column[:, None])
    masked = jnp.where(is_candidate, scores, -jnp.inf)
    row_top = jnp.max(masked, axis=1)
    exps = jnp.exp(masked - row_top[:, None])
    exp_total = jnp.sum(exps, axis=1)
    per_query = row_top + jnp.log(exp_total) - jnp.sum(jnp.where(is_label, scores, 0.0), axis=1)
    local_total = jnp.sum(per_query)
    score_gradient = (
        (exps / exp_total[:, None] - is_label.astype(jnp.float32)) / SOFTMAX_TEMPER
    ).astype(jnp.bfloat16)
    query_grad = jnp.einsum(
        "ij,jd->id", score_gradient, cand_rows, preferred_element_type=jnp.float32
    )
    by_owner = score_gradient.reshape(pairs_dev, dp, span).transpose(1, 0, 2)
    own_columns = lax.all_to_all(by_owner, "dp", 0, 0, tiled=True)
    both_grads = jnp.einsum(
        "sic,sid->cd", own_columns, queries_all, preferred_element_type=jnp.float32
    )
    grads = jnp.concatenate([query_grad, both_grads], axis=0).reshape(units.shape)
    inner_sums = ring_sum(jnp.sum(grads * units, axis=2))[:, :, None]
    embed_grads = (grads - inner_sums * units) / embed_len
    cotangent = (
        ring_gather(embed_grads[1, :pass_dev]).transpose(1, 0, 2).reshape(pass_dev, width)
    )

    gain_in = in_gain.astype(jnp.float32)
    gain_out = out_gain.astype(jnp.float32)
    x_float = layer_input.astype(jnp.float32)
    inv_rms = lax.rsqrt(jnp.mean(x_float * x_float, axis=-1, keepdims=True) + EPSILON)
    normed = (x_float * inv_rms * gain_in).astype(jnp.bfloat16)
    last_pos = lengths - 1
    n_last = jnp.take_along_axis(normed, last_pos[:, None, None], axis=1)[:, 0]
    x_last = jnp.take_along_axis(layer_input, last_pos[:, None, None], axis=1)[:, 0].astype(
        jnp.float32
    )
    value_lowrank = jnp.einsum(
        "pld,dr->plr", normed, down_value, preferred_element_type=jnp.float32
    ).astype(jnp.bfloat16)
    query_lowrank = jnp.dot(n_last, down_query, preferred_element_type=jnp.float32).astype(
        jnp.bfloat16
    )
    group_cols = 2 * kv_cols
    kv_own = lax.dynamic_slice_in_dim(kv_all, place * group_cols, group_cols, 1)
    group_size = q_cols // kv_cols
    score_scale = HD ** (-0.5)
    cosine, sine = angle_table(seq_len, HD)
    kv_pre = jnp.einsum("pld,dc->plc", normed, kv_own, preferred_element_type=jnp.float32)
    value_rows = (
        kv_pre[:, :, kv_cols:]
        + ADAPTER_SCALE
        * jnp.einsum(
            "plr,rc->plc", value_lowrank, value_up_weight, preferred_element_type=jnp.float32
        )
    ).astype(jnp.bfloat16)
    key_rows = rotate(kv_pre[:, :, :kv_cols], cosine[None], sine[None]).astype(jnp.bfloat16)
    query_before_rotation = jnp.dot(
        n_last, query_full, preferred_element_type=jnp.float32
    ) + ADAPTER_SCALE * jnp.dot(
        query_lowrank, query_up_weight, preferred_element_type=jnp.float32
    )
    cos_last = cosine[last_pos][:, None, :]
    sin_last = sine[last_pos][:, None, :]
    query_rot = rotate(
        query_before_rotation.reshape(pass_dev, group_size, HD), cos_last, sin_last
    ).astype(jnp.bfloat16)
    logits = (
        jnp.einsum("pgd,pld->pgl", query_rot, key_rows, preferred_element_type=jnp.float32)
        * score_scale
    )
    visible = lax.iota(jnp.int32, seq_len)[None, :] <= last_pos[:, None]
    logits = jnp.where(visible[:, None, :], logits, -1e30)
    row_peak = jnp.max(logits, axis=-1, keepdims=True)
    exponent_att = jnp.exp(logits - row_peak)
    attention = exponent_att / jnp.sum(exponent_att, axis=-1, keepdims=True)
    attention_round = attention.astype(jnp.bfloat16)
    mixed_heads = (
        jnp.einsum("pgl,pld->pgd", attention_round, value_rows, preferred_element_type=jnp.float32)
        .astype(jnp.bfloat16)
        .reshape(pass_dev, q_cols)
    )
    out_part = jnp.einsum("pc,dc->pd", mixed_heads, out_t, preferred_element_type=jnp.float32)
    hidden = x_last + ring_sum(out_part)

    inv_hidden = lax.rsqrt(jnp.mean(hidden * hidden, axis=-1, keepdims=True) + EPSILON)
    scaled = gain_out * cotangent
    d_hidden = scaled * inv_hidden - hidden * inv_hidden**3 * jnp.mean(
        hidden * scaled, axis=-1, keepdims=True
    )
    d_mixed = jnp.dot(
        d_hidden.astype(jnp.bfloat16), out_t, preferred_element_type=jnp.float32
    ).reshape(pass_dev, group_size, HD)
    value_float = value_rows.astype(jnp.float32)
    key_float = key_rows.astype(jnp.float32)
    d_attention = jnp.einsum("pgd,pld->pgl", d_mixed, value_float, precision=MATMUL_ACCURACY)
    d_logits = attention * (d_attention - jnp.sum(attention * d_attention, axis=-1, keepdims=True))
    d_values = jnp.einsum(
        "pgl,pgd->pld", attention_round.astype(jnp.float32), d_mixed, precision=MATMUL_ACCURACY
    )
    d_query = (
        jnp.einsum("pgl,pld->pgd", d_logits, key_float, precision=MATMUL_ACCURACY) * score_scale
    )
    d_keys = (
        jnp.einsum(
            "pgl,pgd->pld", d_logits, query_rot.astype(jnp.float32), precision=MATMUL_ACCURACY
        )
        * score_scale
    )
    d_query_pre = rotate(d_query, cos_last, -sin_last).reshape(pass_dev, q_cols)
    d_keys_pre = rotate(d_keys, cosine[None], -sine[None])

    tok_span = seq_len // mp
    first_tok = place * tok_span
    d_kv = jnp.concatenate([d_keys_pre, d_values], axis=2).astype(jnp.bfloat16)
    d_kv_send = d_kv.reshape(pass_dev, mp, tok_span, group_cols).transpose(1, 0, 2, 3)
    d_kv_own = lax.all_to_all(d_kv_send, "mp", 0, 0, tiled=True)
    query_back = jnp.einsum(
        "pc,dc->pd", d_query_pre.astype(jnp.bfloat16), query_full, preferred_element_type=jnp.float32
    )
    query_back_all = ring_gather(query_back)
    du_query_part = jnp.einsum(
        "rc,pc->rp",
        query_up_weight.astype(jnp.float32),
        d_query_pre,
        precision=MATMUL_ACCURACY,
    )
    du_value_part = jnp.einsum(
        "rc,nc->rn",
        value_up_weight.astype(jnp.float32),
        d_values.reshape(pass_dev * seq_len, kv_cols),
        precision=MATMUL_ACCURACY,
    )
    du_parts = jnp.pad(
        jnp.concatenate([du_value_part, du_query_part], axis=1), ((0, 0), (0, 128 - pass_dev))
    )
    du = (ADAPTER_SCALE * ring_sum(du_parts)).astype(jnp.bfloat16)
    rank = du.shape[0]
    n_tokens = pass_dev * seq_len
    du_value = du[:, :n_tokens]
    du_query = du[:, n_tokens : n_tokens + pass_dev]
    up_query_part = ADAPTER_SCALE * jnp.einsum(
        "pr,pc->rc", query_lowrank.astype(jnp.float32), d_query_pre, precision=MATMUL_ACCURACY
    )
    up_value_part = ADAPTER_SCALE * jnp.einsum(
        "plr,plc->rc", value_lowrank.astype(jnp.float32), d_values, precision=MATMUL_ACCURACY
    )

    quarter = width // mp
    first_feature = place * quarter
    normed_quarter = lax.dynamic_slice_in_dim(
        normed.reshape(n_tokens, width), first_feature, quarter, 1
    )
    last_quarter = lax.dynamic_slice_in_dim(n_last, first_feature, quarter, 1)
    down_value_part = jnp.einsum(
        "rn,nd->rd", du_value, normed_quarter, preferred_element_type=jnp.float32
    )
    down_query_part = jnp.einsum(
        "rp,pd->rd", du_query, last_quarter, preferred_element_type=jnp.float32
    )
    down_part = jnp.concatenate([down_query_part, down_value_part], axis=0).reshape(dp, -1)
    head_part = jnp.concatenate(
        [up_query_part.reshape(dp, -1), up_value_part.reshape(dp, -1)], axis=1
    )
    loss_part = jnp.broadcast_to(local_total / dp, (dp, 1))
    parts = jnp.concatenate([down_part, head_part, loss_part], axis=1)
    n_down = down_part.shape[1]
    n_head = head_part.shape[1]
    padded = -(-parts.shape[1] // 128) * 128
    parts = jnp.pad(parts, ((0, 0), (0, padded - parts.shape[1]))).reshape(dp, 1, padded)
    reduced = jnp.sum(lax.all_to_all(parts, "dp", 0, 0, tiled=True), axis=0)
    down_all = ring_gather(reduced[:, :n_down]).reshape(1, mp * n_down)
    totals = spread(jnp.concatenate([down_all, reduced[:, n_down:]], axis=1), "dp").reshape(
        dp, -1
    )
    n_all = mp * n_down
    grad_down = (
        totals[:, :n_all]
        .reshape(2 * rank, dp // (2 * rank), mp, n_down)
        .transpose(0, 2, 1, 3)
        .reshape(2 * rank, width)
    )
    grad_down_query = grad_down[:rank].T
    grad_down_value = grad_down[rank:].T
    n_up_query = q_cols * rank // dp
    grad_up_query = totals[:, n_all : n_all + n_up_query].reshape(rank, q_cols)
    grad_up_value = totals[:, n_all + n_up_query : n_all + n_head].reshape(rank, kv_cols)
    loss = jnp.sum(totals[:, n_all + n_head]) / total_pairs

    x_local = lax.dynamic_slice_in_dim(layer_input, first_tok, tok_span, 1).astype(jnp.float32)
    rms_local = lax.dynamic_slice_in_dim(inv_rms, first_tok, tok_span, 1)
    du_local = lax.dynamic_slice_in_dim(
        du_value.reshape(rank, pass_dev, seq_len), first_tok, tok_span, 2
    )
    tok_ids = first_tok + lax.iota(jnp.int32, tok_span)
    at_local = (tok_ids[None, :] == last_pos[:, None])[:, :, None]
    d_normed = jnp.einsum(
        "rpt,dr->ptd", du_local, down_value, preferred_element_type=jnp.float32
    )
    query_adapter = jnp.einsum(
        "rp,dr->pd", du_query, down_query, preferred_element_type=jnp.float32
    )
    d_normed = d_normed + jnp.where(at_local, query_adapter[:, None, :], 0.0)
    for group in range(mp):
        term = jnp.einsum(
            "ptc,dc->ptd",
            d_kv_own[group],
            kv_all[:, group * group_cols : (group + 1) * group_cols],
            preferred_element_type=jnp.float32,
        )
        term = term + jnp.where(at_local, query_back_all[group][:, None, :], 0.0)
        d_normed = d_normed + term.astype(jnp.bfloat16).astype(jnp.float32)
    d_input = gain_in * d_normed * rms_local - x_local * rms_local**3 * jnp.mean(
        x_local * gain_in * d_normed, axis=-1, keepdims=True
    )
    d_input = d_input + jnp.where(at_local, d_hidden[:, None, :], 0.0)
    grad_input = d_input.astype(jnp.bfloat16)
    return (
        loss,
        embed_grads[0],
        embed_grads[1],
        embed_grads[2],
        grad_input,
        grad_down_query,
        grad_up_query,
        grad_down_value,
        grad_up_value,
    )


def solution(mesh):
    in_specs = (
        P("dp", "mp"),
        P("dp", "mp"),
        P("dp", "mp"),
        P("dp"),
        P("dp", None, None),
        P("dp"),
        P(),
        P(),
        P("dp", "mp"),
        P("dp", "mp"),
        P("dp", "mp"),
        P("mp", "dp"),
        P(),
        P(None, "mp"),
        P(),
        P(None, "mp"),
    )
    out_specs = (
        P(),
        P("dp", "mp"),
        P("dp", "mp"),
        P("dp", "mp"),
        P("dp", "mp", None),
        P(),
        P(None, "mp"),
        P(),
        P(None, "mp"),
    )
    return jax.shard_map(
        on_device, mesh=mesh, in_specs=in_specs, out_specs=out_specs, check_vma=False
    )
```

```python
import jax
import jax.numpy as jnp
from jax import lax
from jax.sharding import Mesh
from jax.sharding import PartitionSpec as P

HD = 128
DP = ("y", "x", "zh", "core")


EPSILON = 1e-05
SOFTMAX_TEMPER = 0.01
ADAPTER_SCALE = 2.0
ROPE_BASE = 10000.0
MATMUL_ACCURACY = lax.Precision.HIGHEST


def angle_table(seq_len, head_dim):
    half_dim = head_dim // 2
    frequency = ROPE_BASE ** (-(jnp.arange(half_dim, dtype=jnp.float32) * 2.0 / head_dim))
    angles = jnp.arange(seq_len, dtype=jnp.float32)[:, None] * frequency[None, :]
    return (jnp.cos(angles), jnp.sin(angles))


def rotate(field, cosine, sine):
    half_dim = field.shape[-1] // 2
    leading = field[..., :half_dim]
    trailing = field[..., half_dim:]
    return jnp.concatenate(
        [leading * cosine - trailing * sine, trailing * cosine + leading * sine], axis=-1
    )


def shifted(value, axis_name, shift):
    size = lax.axis_size(axis_name)
    return lax.ppermute(value, axis_name, [(i, (i + shift) % size) for i in range(size)])


def ring_sum(value):
    one, two, three = (shifted(value, "mp", k) for k in (1, 2, 3))
    return (value + two) + (one + three)


def ring_parts(value):
    return [value] + [shifted(value, "mp", k) for k in (1, 2, 3)]


def ring_gather(value):
    parts = jnp.stack(ring_parts(value))
    place = lax.axis_index("mp")
    order = (place - lax.iota(jnp.int32, 4)) % 4
    return jnp.take(parts, order, axis=0)


def spread(value, axis_name):
    size = lax.axis_size(axis_name)
    return lax.all_to_all(
        jnp.broadcast_to(value[None], (size,) + value.shape), axis_name, 0, 0, tiled=True
    )


def core_halves(value):
    rows, columns = value.shape
    halves = value.reshape(rows, 2, columns // 2).transpose(1, 0, 2)
    return lax.all_to_all(halves, "core", 0, 0, tiled=True)


def on_device(
    queries,
    passages,
    negatives,
    hard_index,
    layer_input,
    lengths,
    in_gain,
    out_gain,
    w_query,
    w_key,
    w_value,
    w_out,
    down_query,
    query_up_weight,
    down_value,
    value_up_weight,
):
    dp = lax.axis_size(DP)
    mp = lax.axis_size("mp")
    place = lax.axis_index("mp")
    pairs_dev, feature_dev = queries.shape
    total_pairs = pairs_dev * dp
    pass_dev, seq_len, width = layer_input.shape
    kv_cols = w_key.shape[1]
    q_cols = w_query.shape[1]
    group_cols = 2 * kv_cols

    embeds = jnp.stack([queries, passages, negatives]).astype(jnp.float32)
    square_sums = ring_sum(jnp.sum(embeds * embeds, axis=2))
    embed_len = jnp.sqrt(square_sums)[:, :, None]
    units = embeds / embed_len
    rounds = units.astype(jnp.bfloat16)
    span = 3 * pairs_dev
    by_core = core_halves(rounds.reshape(span, feature_dev))
    by_plane = spread(spread(by_core, "zh"), ("y", "x"))
    embed_all = spread(by_plane.reshape(dp * span, feature_dev // 2), "core")

    shard = jnp.concatenate(
        [w_query, w_out.T, *ring_parts(jnp.concatenate([w_key, w_value], axis=1))], axis=1
    )
    shard = spread(core_halves(shard), "zh")
    piece_rows = shard.shape[0] * shard.shape[1] * shard.shape[2]
    shard = shard.reshape(piece_rows, -1)
    first = spread(spread(shard[:, :q_cols], "x"), "y")
    second = spread(spread(shard[:, q_cols:], "y"), "x").transpose(1, 0, 2, 3)
    first = spread(first.reshape(width, q_cols), "core")
    second = spread(second.reshape(width, q_cols), "core")
    query_full = first[0]
    out_t = second[0]
    kv_parts = (first[1], second[1])

    half = feature_dev // 2
    score_part = sum(
        jnp.einsum(
            "id,jd->ij",
            rounds[0, :, k * half : (k + 1) * half],
            embed_all[k],
            preferred_element_type=jnp.float32,
        )
        for k in range(2)
    )
    passage_unit = ring_gather(units[1, :pass_dev]).transpose(1, 0, 2).reshape(pass_dev, width)
    scores = ring_sum(score_part) / SOFTMAX_TEMPER
    column = lax.iota(jnp.int32, dp * span)[None, :]
    is_passage = (column % span) // pairs_dev == 1
    own_ids = lax.iota(jnp.int32, pairs_dev)
    is_label = column == lax.axis_index(DP) * span + pairs_dev + own_ids[:, None]
    hard_column = (hard_index // pairs_dev) * span + 2 * pairs_dev + hard_index % pairs_dev
    is_candidate = is_passage | (column == hard_column[:, None])
    masked = jnp.where(is_candidate, scores, -jnp.inf)
    row_top = jnp.max(masked, axis=1)
    exps = jnp.exp(masked - row_top[:, None])
    exp_total = jnp.sum(exps, axis=1)
    per_query = row_top + jnp.log(exp_total) - jnp.sum(jnp.where(is_label, scores, 0.0), axis=1)
    local_total = jnp.sum(per_query)
    score_gradient = (
        (exps / exp_total[:, None] - is_label.astype(jnp.float32)) / SOFTMAX_TEMPER
    ).astype(jnp.bfloat16)
    by_owner = score_gradient.reshape(pairs_dev, dp, span).transpose(1, 0, 2)
    own_columns = lax.all_to_all(by_owner, DP, 0, 0, tiled=True)
    own_columns = jnp.pad(own_columns, ((0, 0), (0, span - pairs_dev), (0, 0)))
    own_columns = own_columns.reshape(dp * span, span)
    query_grad = jnp.concatenate(
        [
            jnp.einsum(
                "ij,jd->id", score_gradient, embed_all[k], preferred_element_type=jnp.float32
            )
            for k in range(2)
        ],
        axis=1,
    )
    both_grads = jnp.concatenate(
        [
            jnp.einsum("jc,jd->cd", own_columns, embed_all[k], preferred_element_type=jnp.float32)
            for k in range(2)
        ],
        axis=1,
    )
    passage_grad = both_grads[pairs_dev : pairs_dev + pass_dev]
    passage_grad = ring_gather(passage_grad).transpose(1, 0, 2).reshape(pass_dev, width)
    passage_inner = jnp.sum(passage_grad * passage_unit, axis=1, keepdims=True)
    cotangent = (passage_grad - passage_inner * passage_unit) / embed_len[1, :pass_dev]
    grads = jnp.concatenate([query_grad, both_grads[pairs_dev:]], axis=0).reshape(units.shape)
    inner_sums = ring_sum(jnp.sum(grads * units, axis=2))[:, :, None]
    embed_grads = (grads - inner_sums * units) / embed_len

    gain_in = in_gain.astype(jnp.float32)
    gain_out = out_gain.astype(jnp.float32)
    x_float = layer_input.astype(jnp.float32)
    inv_rms = lax.rsqrt(jnp.mean(x_float * x_float, axis=-1, keepdims=True) + EPSILON)
    normed = (x_float * inv_rms * gain_in).astype(jnp.bfloat16)
    last_pos = lengths - 1
    n_last = jnp.take_along_axis(normed, last_pos[:, None, None], axis=1)[:, 0]
    x_last = jnp.take_along_axis(layer_input, last_pos[:, None, None], axis=1)[:, 0].astype(
        jnp.float32
    )
    value_lowrank = jnp.einsum(
        "pld,dr->plr", normed, down_value, preferred_element_type=jnp.float32
    ).astype(jnp.bfloat16)
    query_lowrank = jnp.dot(n_last, down_query, preferred_element_type=jnp.float32).astype(
        jnp.bfloat16
    )
    kv_own = kv_parts[0][:, :group_cols]
    group_size = q_cols // kv_cols
    score_scale = HD ** (-0.5)
    cosine, sine = angle_table(seq_len, HD)
    kv_pre = jnp.einsum("pld,dc->plc", normed, kv_own, preferred_element_type=jnp.float32)
    value_rows = (
        kv_pre[:, :, kv_cols:]
        + ADAPTER_SCALE
        * jnp.einsum(
            "plr,rc->plc", value_lowrank, value_up_weight, preferred_element_type=jnp.float32
        )
    ).astype(jnp.bfloat16)
    key_rows = rotate(kv_pre[:, :, :kv_cols], cosine[None], sine[None]).astype(jnp.bfloat16)
    query_before_rotation = jnp.dot(
        n_last, query_full, preferred_element_type=jnp.float32
    ) + ADAPTER_SCALE * jnp.dot(
        query_lowrank, query_up_weight, preferred_element_type=jnp.float32
    )
    cos_last = cosine[last_pos][:, None, :]
    sin_last = sine[last_pos][:, None, :]
    query_rot = rotate(
        query_before_rotation.reshape(pass_dev, group_size, HD), cos_last, sin_last
    ).astype(jnp.bfloat16)
    logits = (
        jnp.einsum("pgd,pld->pgl", query_rot, key_rows, preferred_element_type=jnp.float32)
        * score_scale
    )
    visible = lax.iota(jnp.int32, seq_len)[None, :] <= last_pos[:, None]
    logits = jnp.where(visible[:, None, :], logits, -1e30)
    row_peak = jnp.max(logits, axis=-1, keepdims=True)
    exponent_att = jnp.exp(logits - row_peak)
    attention = exponent_att / jnp.sum(exponent_att, axis=-1, keepdims=True)
    attention_round = attention.astype(jnp.bfloat16)
    mixed_heads = (
        jnp.einsum("pgl,pld->pgd", attention_round, value_rows, preferred_element_type=jnp.float32)
        .astype(jnp.bfloat16)
        .reshape(pass_dev, q_cols)
    )
    out_part = jnp.einsum("pc,dc->pd", mixed_heads, out_t, preferred_element_type=jnp.float32)
    hidden = x_last + ring_sum(out_part)

    inv_hidden = lax.rsqrt(jnp.mean(hidden * hidden, axis=-1, keepdims=True) + EPSILON)
    scaled = gain_out * cotangent
    d_hidden = scaled * inv_hidden - hidden * inv_hidden**3 * jnp.mean(
        hidden * scaled, axis=-1, keepdims=True
    )
    d_mixed = jnp.dot(
        d_hidden.astype(jnp.bfloat16), out_t, preferred_element_type=jnp.float32
    ).reshape(pass_dev, group_size, HD)
    value_float = value_rows.astype(jnp.float32)
    key_float = key_rows.astype(jnp.float32)
    d_attention = jnp.einsum("pgd,pld->pgl", d_mixed, value_float, precision=MATMUL_ACCURACY)
    d_logits = attention * (d_attention - jnp.sum(attention * d_attention, axis=-1, keepdims=True))
    d_values = jnp.einsum(
        "pgl,pgd->pld", attention_round.astype(jnp.float32), d_mixed, precision=MATMUL_ACCURACY
    )
    d_query = (
        jnp.einsum("pgl,pld->pgd", d_logits, key_float, precision=MATMUL_ACCURACY) * score_scale
    )
    d_keys = (
        jnp.einsum(
            "pgl,pgd->pld", d_logits, query_rot.astype(jnp.float32), precision=MATMUL_ACCURACY
        )
        * score_scale
    )
    d_query_pre = rotate(d_query, cos_last, -sin_last).reshape(pass_dev, q_cols)
    d_keys_pre = rotate(d_keys, cosine[None], -sine[None])

    tok_span = seq_len // mp
    first_tok = place * tok_span
    d_kv = jnp.concatenate([d_keys_pre, d_values], axis=2).astype(jnp.bfloat16)
    d_kv_send = d_kv.reshape(pass_dev, mp, tok_span, group_cols).transpose(1, 0, 2, 3)
    d_kv_own = lax.all_to_all(d_kv_send, "mp", 0, 0, tiled=True)
    d_kv_own = jnp.take(d_kv_own, (place - lax.iota(jnp.int32, mp)) % mp, axis=0)
    query_back = jnp.einsum(
        "pc,dc->pd", d_query_pre.astype(jnp.bfloat16), query_full, preferred_element_type=jnp.float32
    )
    query_back_all = ring_parts(query_back)
    du_query_part = jnp.einsum(
        "rc,pc->rp",
        query_up_weight.astype(jnp.float32),
        d_query_pre,
        precision=MATMUL_ACCURACY,
    )
    du_value_part = jnp.einsum(
        "rc,nc->rn",
        value_up_weight.astype(jnp.float32),
        d_values.reshape(pass_dev * seq_len, kv_cols),
        precision=MATMUL_ACCURACY,
    )
    du_parts = jnp.pad(
        jnp.concatenate([du_value_part, du_query_part], axis=1), ((0, 0), (0, 128 - pass_dev))
    )
    du = (ADAPTER_SCALE * ring_sum(du_parts)).astype(jnp.bfloat16)
    rank = du.shape[0]
    n_tokens = pass_dev * seq_len
    du_value = du[:, :n_tokens]
    du_query = du[:, n_tokens : n_tokens + pass_dev]
    up_query_part = ADAPTER_SCALE * jnp.einsum(
        "pr,pc->rc", query_lowrank.astype(jnp.float32), d_query_pre, precision=MATMUL_ACCURACY
    )
    up_value_part = ADAPTER_SCALE * jnp.einsum(
        "plr,plc->rc", value_lowrank.astype(jnp.float32), d_values, precision=MATMUL_ACCURACY
    )

    quarter = width // mp
    first_feature = place * quarter
    normed_quarter = lax.dynamic_slice_in_dim(
        normed.reshape(n_tokens, width), first_feature, quarter, 1
    )
    last_quarter = lax.dynamic_slice_in_dim(n_last, first_feature, quarter, 1)
    down_value_part = jnp.einsum(
        "rn,nd->rd", du_value, normed_quarter, preferred_element_type=jnp.float32
    )
    down_query_part = jnp.einsum(
        "rp,pd->rd", du_query, last_quarter, preferred_element_type=jnp.float32
    )
    down_part = jnp.concatenate([down_query_part, down_value_part], axis=0).reshape(dp, -1)
    head_part = jnp.concatenate(
        [up_query_part.reshape(dp, -1), up_value_part.reshape(dp, -1)], axis=1
    )
    loss_part = jnp.broadcast_to(local_total / dp, (dp, 1))
    parts = jnp.concatenate([down_part, head_part, loss_part], axis=1)
    n_down = down_part.shape[1]
    n_head = head_part.shape[1]
    padded = -(-parts.shape[1] // 128) * 128
    parts = jnp.pad(parts, ((0, 0), (0, padded - parts.shape[1]))).reshape(dp, 1, padded)
    reduced = jnp.sum(lax.all_to_all(parts, DP, 0, 0, tiled=True), axis=0)
    down_all = ring_gather(reduced[:, :n_down]).reshape(1, mp * n_down)
    totals = spread(jnp.concatenate([down_all, reduced[:, n_down:]], axis=1), DP).reshape(
        dp, -1
    )
    n_all = mp * n_down
    grad_down = (
        totals[:, :n_all]
        .reshape(2 * rank, dp // (2 * rank), mp, n_down)
        .transpose(0, 2, 1, 3)
        .reshape(2 * rank, width)
    )
    grad_down_query = grad_down[:rank].T
    grad_down_value = grad_down[rank:].T
    n_up_query = q_cols * rank // dp
    grad_up_query = totals[:, n_all : n_all + n_up_query].reshape(rank, q_cols)
    grad_up_value = totals[:, n_all + n_up_query : n_all + n_head].reshape(rank, kv_cols)
    loss = jnp.sum(totals[:, n_all + n_head]) / total_pairs

    x_local = lax.dynamic_slice_in_dim(layer_input, first_tok, tok_span, 1).astype(jnp.float32)
    rms_local = lax.dynamic_slice_in_dim(inv_rms, first_tok, tok_span, 1)
    du_local = lax.dynamic_slice_in_dim(
        du_value.reshape(rank, pass_dev, seq_len), first_tok, tok_span, 2
    )
    tok_ids = first_tok + lax.iota(jnp.int32, tok_span)
    at_local = (tok_ids[None, :] == last_pos[:, None])[:, :, None]
    d_normed = jnp.einsum(
        "rpt,dr->ptd", du_local, down_value, preferred_element_type=jnp.float32
    )
    query_adapter = jnp.einsum(
        "rp,dr->pd", du_query, down_query, preferred_element_type=jnp.float32
    )
    d_normed = d_normed + jnp.where(at_local, query_adapter[:, None, :], 0.0)
    for group in range(mp):
        term = jnp.einsum(
            "ptc,dc->ptd",
            d_kv_own[group],
            kv_parts[group // 2][:, (group % 2) * group_cols : (group % 2 + 1) * group_cols],
            preferred_element_type=jnp.float32,
        )
        term = term + jnp.where(at_local, query_back_all[group][:, None, :], 0.0)
        d_normed = d_normed + term.astype(jnp.bfloat16).astype(jnp.float32)
    d_input = gain_in * d_normed * rms_local - x_local * rms_local**3 * jnp.mean(
        x_local * gain_in * d_normed, axis=-1, keepdims=True
    )
    d_input = d_input + jnp.where(at_local, d_hidden[:, None, :], 0.0)
    grad_input = d_input.astype(jnp.bfloat16)
    return (
        loss,
        embed_grads[0],
        embed_grads[1],
        embed_grads[2],
        grad_input,
        grad_down_query,
        grad_up_query,
        grad_down_value,
        grad_up_value,
    )


def solution(mesh):
    staged = Mesh(mesh.devices.reshape(4, 4, 2, 2, 4), (*DP, "mp"))
    in_specs = (
        P(DP, "mp"),
        P(DP, "mp"),
        P(DP, "mp"),
        P(DP),
        P(DP, None, None),
        P(DP),
        P(),
        P(),
        P(DP, "mp"),
        P(DP, "mp"),
        P(DP, "mp"),
        P("mp", DP),
        P(),
        P(None, "mp"),
        P(),
        P(None, "mp"),
    )
    out_specs = (
        P(),
        P(DP, "mp"),
        P(DP, "mp"),
        P(DP, "mp"),
        P(DP, "mp", None),
        P(),
        P(None, "mp"),
        P(),
        P(None, "mp"),
    )
    return jax.shard_map(
        on_device, mesh=staged, in_specs=in_specs, out_specs=out_specs, check_vma=False
    )
```

```python
import jax
import jax.numpy as jnp
from jax import lax
from jax.experimental import pallas as pl
from jax.experimental.pallas import tpu as pltpu
from jax.sharding import Mesh
from jax.sharding import PartitionSpec as P

HD = 128
DP = ("y", "x", "zh", "core")


EPSILON = 1e-05
SOFTMAX_TEMPER = 0.01
ADAPTER_SCALE = 2.0
ROPE_BASE = 10000.0
MATMUL_ACCURACY = lax.Precision.HIGHEST


def angle_table(seq_len, head_dim):
    half_dim = head_dim // 2
    frequency = ROPE_BASE ** (-(jnp.arange(half_dim, dtype=jnp.float32) * 2.0 / head_dim))
    angles = jnp.arange(seq_len, dtype=jnp.float32)[:, None] * frequency[None, :]
    return (jnp.cos(angles), jnp.sin(angles))


def rotate(field, cosine, sine):
    half_dim = field.shape[-1] // 2
    leading = field[..., :half_dim]
    trailing = field[..., half_dim:]
    return jnp.concatenate(
        [leading * cosine - trailing * sine, trailing * cosine + leading * sine], axis=-1
    )


def shifted(value, axis_name, shift):
    size = lax.axis_size(axis_name)
    return lax.ppermute(value, axis_name, [(i, (i + shift) % size) for i in range(size)])


def ring_sum(value):
    one, two, three = (shifted(value, "mp", k) for k in (1, 2, 3))
    return (value + two) + (one + three)


def ring_parts(value):
    return [value] + [shifted(value, "mp", k) for k in (1, 2, 3)]


def ring_gather(value):
    parts = jnp.stack(ring_parts(value))
    place = lax.axis_index("mp")
    order = (place - lax.iota(jnp.int32, 4)) % 4
    return jnp.take(parts, order, axis=0)


def spread(value, axis_name):
    size = lax.axis_size(axis_name)
    return lax.all_to_all(
        jnp.broadcast_to(value[None], (size,) + value.shape), axis_name, 0, 0, tiled=True
    )


def pair_gather(value, axis_name):
    other = lax.ppermute(value, axis_name, [(0, 1), (1, 0)])
    at_first = lax.axis_index(axis_name) == 0
    return jnp.stack([jnp.where(at_first, value, other), jnp.where(at_first, other, value)])


def core_halves(value):
    half = value.shape[1] // 2
    at_first = lax.axis_index("core") == 0
    left, right = value[:, :half], value[:, half:]
    kept = jnp.where(at_first, left, right)
    other = lax.ppermute(jnp.where(at_first, right, left), "core", [(0, 1), (1, 0)])
    return jnp.stack([jnp.where(at_first, kept, other), jnp.where(at_first, other, kept)])


def ring_blocks(value, axis_name):
    return [value] + [shifted(value, axis_name, k) for k in (1, 2, 3)]


def place_weights(mine, theirs, rows, block):
    n_pieces = len(mine)
    columns = mine[0].shape[1]
    total = 2 * n_pieces * block

    def kernel(rows_ref, core_ref, *refs):
        sources = refs[: 2 * n_pieces]
        outs = refs[2 * n_pieces : -1]
        sems = refs[-1]

        def copies(core):
            moves = []
            for p, source in enumerate(sources):
                owner = core if p < n_pieces else 1 - core
                piece = p % n_pieces
                second = piece >= n_pieces // 2
                for b in range(4):
                    row = pl.multiple_of(rows_ref[piece * 4 + b], block)
                    span = pl.ds(b * block, block)
                    if owner == 0:
                        moves.append((source.at[span], outs[int(second)].at[pl.ds(row, block)]))
                    else:
                        for k in range(2):
                            moves.append(
                                (
                                    source.at[span, pl.ds(k * columns // 2, columns // 2)],
                                    outs[2 + 2 * int(second) + k].at[pl.ds(row, block)],
                                )
                            )
            return [
                pltpu.make_async_copy(src, dst, sems.at[i]) for i, (src, dst) in enumerate(moves)
            ]

        for core in range(2):

            @pl.when(core_ref[0] == core)
            def _():
                moves = copies(core)
                for move in moves:
                    move.start()
                for move in moves:
                    move.wait()

    wide = jax.ShapeDtypeStruct((total, columns), mine[0].dtype)
    slim = jax.ShapeDtypeStruct((total, columns // 2), mine[0].dtype)
    anywhere = pl.BlockSpec(memory_space=pl.ANY)
    scalars = pl.BlockSpec(memory_space=pltpu.SMEM)
    return pl.pallas_call(
        kernel,
        out_shape=[wide] * 2 + [slim] * 4,
        in_specs=[scalars, scalars] + [anywhere] * (2 * n_pieces),
        out_specs=[anywhere] * 6,
        scratch_shapes=[pltpu.SemaphoreType.DMA((n_pieces * 12,))],
    )(rows, lax.axis_index("core").reshape(1), *mine, *theirs)


def on_device(
    queries,
    passages,
    negatives,
    hard_index,
    layer_input,
    lengths,
    in_gain,
    out_gain,
    w_query,
    w_key,
    w_value,
    w_out,
    down_query,
    query_up_weight,
    down_value,
    value_up_weight,
):
    dp = lax.axis_size(DP)
    mp = lax.axis_size("mp")
    place = lax.axis_index("mp")
    pairs_dev, feature_dev = queries.shape
    total_pairs = pairs_dev * dp
    pass_dev, seq_len, width = layer_input.shape
    kv_cols = w_key.shape[1]
    q_cols = w_query.shape[1]
    group_cols = 2 * kv_cols

    embeds = jnp.stack([queries, passages, negatives]).astype(jnp.float32)
    square_sums = ring_sum(jnp.sum(embeds * embeds, axis=2))
    embed_len = jnp.sqrt(square_sums)[:, :, None]
    units = embeds / embed_len
    rounds = units.astype(jnp.bfloat16)
    span = 3 * pairs_dev
    by_core = core_halves(rounds.reshape(span, feature_dev))
    by_plane = spread(pair_gather(by_core, "zh"), ("y", "x"))
    embed_all = pair_gather(by_plane.reshape(dp * span, feature_dev // 2), "core")

    shard = jnp.concatenate(
        [w_query, w_out.T, *ring_parts(jnp.concatenate([w_key, w_value], axis=1))], axis=1
    )
    shard = pair_gather(core_halves(shard), "zh")
    block = 4 * shard.shape[2]
    shard = shard.reshape(block, -1)
    x_first = jnp.concatenate(ring_blocks(shard[:, :q_cols], "x"), axis=0)
    y_first = jnp.concatenate(ring_blocks(shard[:, q_cols:], "y"), axis=0)
    mine = ring_blocks(x_first, "y") + ring_blocks(y_first, "x")
    theirs = [lax.ppermute(piece, "core", [(0, 1), (1, 0)]) for piece in mine]
    back = lax.iota(jnp.int32, 4)
    y_from = (lax.axis_index("y") - back) % 4
    x_from = (lax.axis_index("x") - back) % 4
    rows = jnp.stack(
        [y_from[:, None] * 4 + x_from[None, :], y_from[None, :] * 4 + x_from[:, None]]
    )
    query_full, out_t, *kv_groups = place_weights(mine, theirs, (rows * block).reshape(-1), block)

    half = feature_dev // 2
    score_part = sum(
        jnp.einsum(
            "id,jd->ij",
            rounds[0, :, k * half : (k + 1) * half],
            embed_all[k],
            preferred_element_type=jnp.float32,
        )
        for k in range(2)
    )
    passage_unit = ring_gather(units[1, :pass_dev]).transpose(1, 0, 2).reshape(pass_dev, width)
    scores = ring_sum(score_part) / SOFTMAX_TEMPER
    column = lax.iota(jnp.int32, dp * span)[None, :]
    is_passage = (column % span) // pairs_dev == 1
    own_ids = lax.iota(jnp.int32, pairs_dev)
    is_label = column == lax.axis_index(DP) * span + pairs_dev + own_ids[:, None]
    hard_column = (hard_index // pairs_dev) * span + 2 * pairs_dev + hard_index % pairs_dev
    is_candidate = is_passage | (column == hard_column[:, None])
    masked = jnp.where(is_candidate, scores, -jnp.inf)
    row_top = jnp.max(masked, axis=1)
    exps = jnp.exp(masked - row_top[:, None])
    exp_total = jnp.sum(exps, axis=1)
    per_query = row_top + jnp.log(exp_total) - jnp.sum(jnp.where(is_label, scores, 0.0), axis=1)
    local_total = jnp.sum(per_query)
    score_gradient = (
        (exps / exp_total[:, None] - is_label.astype(jnp.float32)) / SOFTMAX_TEMPER
    ).astype(jnp.bfloat16)
    by_owner = score_gradient.reshape(pairs_dev, dp, span).transpose(1, 0, 2)
    own_columns = lax.all_to_all(by_owner, DP, 0, 0, tiled=True)
    own_columns = jnp.pad(own_columns, ((0, 0), (0, span - pairs_dev), (0, 0)))
    own_columns = own_columns.reshape(dp * span, span)
    query_grad = jnp.concatenate(
        [
            jnp.einsum(
                "ij,jd->id", score_gradient, embed_all[k], preferred_element_type=jnp.float32
            )
            for k in range(2)
        ],
        axis=1,
    )
    both_grads = jnp.concatenate(
        [
            jnp.einsum("jc,jd->cd", own_columns, embed_all[k], preferred_element_type=jnp.float32)
            for k in range(2)
        ],
        axis=1,
    )
    passage_grad = both_grads[pairs_dev : pairs_dev + pass_dev]
    passage_grad = ring_gather(passage_grad).transpose(1, 0, 2).reshape(pass_dev, width)
    passage_inner = jnp.sum(passage_grad * passage_unit, axis=1, keepdims=True)
    cotangent = (passage_grad - passage_inner * passage_unit) / embed_len[1, :pass_dev]
    grads = jnp.concatenate([query_grad, both_grads[pairs_dev:]], axis=0).reshape(units.shape)
    inner_sums = ring_sum(jnp.sum(grads * units, axis=2))[:, :, None]
    embed_grads = (grads - inner_sums * units) / embed_len

    gain_in = in_gain.astype(jnp.float32)
    gain_out = out_gain.astype(jnp.float32)
    x_float = layer_input.astype(jnp.float32)
    inv_rms = lax.rsqrt(jnp.mean(x_float * x_float, axis=-1, keepdims=True) + EPSILON)
    normed = (x_float * inv_rms * gain_in).astype(jnp.bfloat16)
    last_pos = lengths - 1
    n_last = jnp.take_along_axis(normed, last_pos[:, None, None], axis=1)[:, 0]
    x_last = jnp.take_along_axis(layer_input, last_pos[:, None, None], axis=1)[:, 0].astype(
        jnp.float32
    )
    value_lowrank = jnp.einsum(
        "pld,dr->plr", normed, down_value, preferred_element_type=jnp.float32
    ).astype(jnp.bfloat16)
    query_lowrank = jnp.dot(n_last, down_query, preferred_element_type=jnp.float32).astype(
        jnp.bfloat16
    )
    group_size = q_cols // kv_cols
    score_scale = HD ** (-0.5)
    cosine, sine = angle_table(seq_len, HD)
    kv_pre = jnp.einsum("pld,dc->plc", normed, kv_groups[0], preferred_element_type=jnp.float32)
    value_rows = (
        kv_pre[:, :, kv_cols:]
        + ADAPTER_SCALE
        * jnp.einsum(
            "plr,rc->plc", value_lowrank, value_up_weight, preferred_element_type=jnp.float32
        )
    ).astype(jnp.bfloat16)
    key_rows = rotate(kv_pre[:, :, :kv_cols], cosine[None], sine[None]).astype(jnp.bfloat16)
    query_before_rotation = jnp.dot(
        n_last, query_full, preferred_element_type=jnp.float32
    ) + ADAPTER_SCALE * jnp.dot(
        query_lowrank, query_up_weight, preferred_element_type=jnp.float32
    )
    cos_last = cosine[last_pos][:, None, :]
    sin_last = sine[last_pos][:, None, :]
    query_rot = rotate(
        query_before_rotation.reshape(pass_dev, group_size, HD), cos_last, sin_last
    ).astype(jnp.bfloat16)
    logits = (
        jnp.einsum("pgd,pld->pgl", query_rot, key_rows, preferred_element_type=jnp.float32)
        * score_scale
    )
    visible = lax.iota(jnp.int32, seq_len)[None, :] <= last_pos[:, None]
    logits = jnp.where(visible[:, None, :], logits, -1e30)
    row_peak = jnp.max(logits, axis=-1, keepdims=True)
    exponent_att = jnp.exp(logits - row_peak)
    attention = exponent_att / jnp.sum(exponent_att, axis=-1, keepdims=True)
    attention_round = attention.astype(jnp.bfloat16)
    mixed_heads = (
        jnp.einsum("pgl,pld->pgd", attention_round, value_rows, preferred_element_type=jnp.float32)
        .astype(jnp.bfloat16)
        .reshape(pass_dev, q_cols)
    )
    out_part = jnp.einsum("pc,dc->pd", mixed_heads, out_t, preferred_element_type=jnp.float32)
    hidden = x_last + ring_sum(out_part)

    inv_hidden = lax.rsqrt(jnp.mean(hidden * hidden, axis=-1, keepdims=True) + EPSILON)
    scaled = gain_out * cotangent
    d_hidden = scaled * inv_hidden - hidden * inv_hidden**3 * jnp.mean(
        hidden * scaled, axis=-1, keepdims=True
    )
    d_mixed = jnp.dot(
        d_hidden.astype(jnp.bfloat16), out_t, preferred_element_type=jnp.float32
    ).reshape(pass_dev, group_size, HD)
    value_float = value_rows.astype(jnp.float32)
    key_float = key_rows.astype(jnp.float32)
    d_attention = jnp.einsum("pgd,pld->pgl", d_mixed, value_float, precision=MATMUL_ACCURACY)
    d_logits = attention * (d_attention - jnp.sum(attention * d_attention, axis=-1, keepdims=True))
    d_values = jnp.einsum(
        "pgl,pgd->pld", attention_round.astype(jnp.float32), d_mixed, precision=MATMUL_ACCURACY
    )
    d_query = (
        jnp.einsum("pgl,pld->pgd", d_logits, key_float, precision=MATMUL_ACCURACY) * score_scale
    )
    d_keys = (
        jnp.einsum(
            "pgl,pgd->pld", d_logits, query_rot.astype(jnp.float32), precision=MATMUL_ACCURACY
        )
        * score_scale
    )
    d_query_pre = rotate(d_query, cos_last, -sin_last).reshape(pass_dev, q_cols)
    d_keys_pre = rotate(d_keys, cosine[None], -sine[None])

    tok_span = seq_len // mp
    first_tok = place * tok_span
    d_kv = jnp.concatenate([d_keys_pre, d_values], axis=2).astype(jnp.bfloat16)
    d_kv_send = d_kv.reshape(pass_dev, mp, tok_span, group_cols).transpose(1, 0, 2, 3)
    d_kv_own = lax.all_to_all(d_kv_send, "mp", 0, 0, tiled=True)
    d_kv_own = jnp.take(d_kv_own, (place - lax.iota(jnp.int32, mp)) % mp, axis=0)
    query_back = jnp.einsum(
        "pc,dc->pd", d_query_pre.astype(jnp.bfloat16), query_full, preferred_element_type=jnp.float32
    )
    query_back_all = ring_parts(query_back)
    du_query_part = jnp.einsum(
        "rc,pc->rp",
        query_up_weight.astype(jnp.float32),
        d_query_pre,
        precision=MATMUL_ACCURACY,
    )
    du_value_part = jnp.einsum(
        "rc,nc->rn",
        value_up_weight.astype(jnp.float32),
        d_values.reshape(pass_dev * seq_len, kv_cols),
        precision=MATMUL_ACCURACY,
    )
    du_parts = jnp.pad(
        jnp.concatenate([du_value_part, du_query_part], axis=1), ((0, 0), (0, 128 - pass_dev))
    )
    du = (ADAPTER_SCALE * ring_sum(du_parts)).astype(jnp.bfloat16)
    rank = du.shape[0]
    n_tokens = pass_dev * seq_len
    du_value = du[:, :n_tokens]
    du_query = du[:, n_tokens : n_tokens + pass_dev]
    up_query_part = ADAPTER_SCALE * jnp.einsum(
        "pr,pc->rc", query_lowrank.astype(jnp.float32), d_query_pre, precision=MATMUL_ACCURACY
    )
    up_value_part = ADAPTER_SCALE * jnp.einsum(
        "plr,plc->rc", value_lowrank.astype(jnp.float32), d_values, precision=MATMUL_ACCURACY
    )

    quarter = width // mp
    first_feature = place * quarter
    normed_quarter = lax.dynamic_slice_in_dim(
        normed.reshape(n_tokens, width), first_feature, quarter, 1
    )
    last_quarter = lax.dynamic_slice_in_dim(n_last, first_feature, quarter, 1)
    down_value_part = jnp.einsum(
        "rn,nd->rd", du_value, normed_quarter, preferred_element_type=jnp.float32
    )
    down_query_part = jnp.einsum(
        "rp,pd->rd", du_query, last_quarter, preferred_element_type=jnp.float32
    )
    down_part = jnp.concatenate([down_query_part, down_value_part], axis=0).reshape(dp, -1)
    head_part = jnp.concatenate(
        [up_query_part.reshape(dp, -1), up_value_part.reshape(dp, -1)], axis=1
    )
    loss_part = jnp.broadcast_to(local_total / dp, (dp, 1))
    parts = jnp.concatenate([down_part, head_part, loss_part], axis=1)
    n_down = down_part.shape[1]
    n_head = head_part.shape[1]
    padded = -(-parts.shape[1] // 128) * 128
    parts = jnp.pad(parts, ((0, 0), (0, padded - parts.shape[1]))).reshape(dp, 1, padded)
    reduced = jnp.sum(lax.all_to_all(parts, DP, 0, 0, tiled=True), axis=0)
    down_all = ring_gather(reduced[:, :n_down]).reshape(1, mp * n_down)
    totals = spread(jnp.concatenate([down_all, reduced[:, n_down:]], axis=1), DP).reshape(
        dp, -1
    )
    n_all = mp * n_down
    grad_down = (
        totals[:, :n_all]
        .reshape(2 * rank, dp // (2 * rank), mp, n_down)
        .transpose(0, 2, 1, 3)
        .reshape(2 * rank, width)
    )
    grad_down_query = grad_down[:rank].T
    grad_down_value = grad_down[rank:].T
    n_up_query = q_cols * rank // dp
    grad_up_query = totals[:, n_all : n_all + n_up_query].reshape(rank, q_cols)
    grad_up_value = totals[:, n_all + n_up_query : n_all + n_head].reshape(rank, kv_cols)
    loss = jnp.sum(totals[:, n_all + n_head]) / total_pairs

    x_local = lax.dynamic_slice_in_dim(layer_input, first_tok, tok_span, 1).astype(jnp.float32)
    rms_local = lax.dynamic_slice_in_dim(inv_rms, first_tok, tok_span, 1)
    du_local = lax.dynamic_slice_in_dim(
        du_value.reshape(rank, pass_dev, seq_len), first_tok, tok_span, 2
    )
    tok_ids = first_tok + lax.iota(jnp.int32, tok_span)
    at_local = (tok_ids[None, :] == last_pos[:, None])[:, :, None]
    d_normed = jnp.einsum(
        "rpt,dr->ptd", du_local, down_value, preferred_element_type=jnp.float32
    )
    query_adapter = jnp.einsum(
        "rp,dr->pd", du_query, down_query, preferred_element_type=jnp.float32
    )
    d_normed = d_normed + jnp.where(at_local, query_adapter[:, None, :], 0.0)
    for group in range(mp):
        term = jnp.einsum(
            "ptc,dc->ptd",
            d_kv_own[group],
            kv_groups[group],
            preferred_element_type=jnp.float32,
        )
        term = term + jnp.where(at_local, query_back_all[group][:, None, :], 0.0)
        d_normed = d_normed + term.astype(jnp.bfloat16).astype(jnp.float32)
    d_input = gain_in * d_normed * rms_local - x_local * rms_local**3 * jnp.mean(
        x_local * gain_in * d_normed, axis=-1, keepdims=True
    )
    d_input = d_input + jnp.where(at_local, d_hidden[:, None, :], 0.0)
    grad_input = d_input.astype(jnp.bfloat16)
    return (
        loss,
        embed_grads[0],
        embed_grads[1],
        embed_grads[2],
        grad_input,
        grad_down_query,
        grad_up_query,
        grad_down_value,
        grad_up_value,
    )


def solution(mesh):
    staged = Mesh(mesh.devices.reshape(4, 4, 2, 2, 4), (*DP, "mp"))
    in_specs = (
        P(DP, "mp"),
        P(DP, "mp"),
        P(DP, "mp"),
        P(DP),
        P(DP, None, None),
        P(DP),
        P(),
        P(),
        P(DP, "mp"),
        P(DP, "mp"),
        P(DP, "mp"),
        P("mp", DP),
        P(),
        P(None, "mp"),
        P(),
        P(None, "mp"),
    )
    out_specs = (
        P(),
        P(DP, "mp"),
        P(DP, "mp"),
        P(DP, "mp"),
        P(DP, "mp", None),
        P(),
        P(None, "mp"),
        P(),
        P(None, "mp"),
    )
    return jax.shard_map(
        on_device, mesh=staged, in_specs=in_specs, out_specs=out_specs, check_vma=False
    )
```

```python
import jax
import jax.numpy as jnp
from jax import lax
from jax.sharding import Mesh
from jax.sharding import PartitionSpec as P

HD = 128
DP = ("y", "x", "zh", "core")


EPSILON = 1e-05
SOFTMAX_TEMPER = 0.01
ADAPTER_SCALE = 2.0
ROPE_BASE = 10000.0
MATMUL_ACCURACY = lax.Precision.HIGHEST


def angle_table(seq_len, head_dim):
    half_dim = head_dim // 2
    frequency = ROPE_BASE ** (-(jnp.arange(half_dim, dtype=jnp.float32) * 2.0 / head_dim))
    angles = jnp.arange(seq_len, dtype=jnp.float32)[:, None] * frequency[None, :]
    return (jnp.cos(angles), jnp.sin(angles))


def rotate(field, cosine, sine):
    half_dim = field.shape[-1] // 2
    leading = field[..., :half_dim]
    trailing = field[..., half_dim:]
    return jnp.concatenate(
        [leading * cosine - trailing * sine, trailing * cosine + leading * sine], axis=-1
    )


def shifted(value, axis_name, shift):
    size = lax.axis_size(axis_name)
    return lax.ppermute(value, axis_name, [(i, (i + shift) % size) for i in range(size)])


def ring_sum(value):
    one, two, three = (shifted(value, "mp", k) for k in (1, 2, 3))
    return (value + two) + (one + three)


def ring_parts(value):
    return [value] + [shifted(value, "mp", k) for k in (1, 2, 3)]


def ring_gather(value):
    parts = jnp.stack(ring_parts(value))
    place = lax.axis_index("mp")
    order = (place - lax.iota(jnp.int32, 4)) % 4
    return jnp.take(parts, order, axis=0)


def spread(value, axis_name):
    size = lax.axis_size(axis_name)
    return lax.all_to_all(
        jnp.broadcast_to(value[None], (size,) + value.shape), axis_name, 0, 0, tiled=True
    )


def pair_gather(value, axis_name):
    other = lax.ppermute(value, axis_name, [(0, 1), (1, 0)])
    at_first = lax.axis_index(axis_name) == 0
    return jnp.stack([jnp.where(at_first, value, other), jnp.where(at_first, other, value)])


def core_halves(value):
    half = value.shape[1] // 2
    at_first = lax.axis_index("core") == 0
    left, right = value[:, :half], value[:, half:]
    kept = jnp.where(at_first, left, right)
    other = lax.ppermute(jnp.where(at_first, right, left), "core", [(0, 1), (1, 0)])
    return jnp.stack([jnp.where(at_first, kept, other), jnp.where(at_first, other, kept)])


def on_device(
    queries,
    passages,
    negatives,
    hard_index,
    layer_input,
    lengths,
    in_gain,
    out_gain,
    w_query,
    w_key,
    w_value,
    w_out,
    down_query,
    query_up_weight,
    down_value,
    value_up_weight,
):
    dp = lax.axis_size(DP)
    mp = lax.axis_size("mp")
    place = lax.axis_index("mp")
    pairs_dev, feature_dev = queries.shape
    total_pairs = pairs_dev * dp
    pass_dev, seq_len, width = layer_input.shape
    kv_cols = w_key.shape[1]
    q_cols = w_query.shape[1]
    group_cols = 2 * kv_cols

    kv_shards = ring_parts(jnp.concatenate([w_key, w_value], axis=1))
    weights = lax.all_gather(
        jnp.concatenate([w_query, w_out.T, kv_shards[0]], axis=1), DP, axis=0, tiled=True
    )
    others = lax.all_gather(jnp.concatenate(kv_shards[1:], axis=1), DP, axis=0, tiled=True)
    query_full = weights[:, :q_cols]
    out_t = weights[:, q_cols : 2 * q_cols]
    kv_groups = [weights[:, 2 * q_cols :]]
    kv_groups += [others[:, k * group_cols : (k + 1) * group_cols] for k in range(mp - 1)]

    half = feature_dev // 2
    span = 3 * pairs_dev
    first_core = lax.axis_index("core") == 0
    embeds = jnp.stack([queries, passages, negatives])
    by_core = core_halves(embeds.reshape(span, feature_dev))
    mine = spread(pair_gather(by_core, "zh"), ("y", "x")).reshape(dp * span, half)
    theirs = lax.ppermute(mine, "core", [(0, 1), (1, 0)])
    raw_halves = [rows.astype(jnp.float32) for rows in (mine, theirs)]
    square_sums = ring_sum(sum(jnp.sum(rows * rows, axis=1) for rows in raw_halves))
    all_len = jnp.sqrt(square_sums)
    embed_halves = [(rows / all_len[:, None]).astype(jnp.bfloat16) for rows in raw_halves]
    embed_len = lax.dynamic_slice_in_dim(all_len, lax.axis_index(DP) * span, span)
    embed_len = embed_len.reshape(3, pairs_dev, 1)
    units = embeds.astype(jnp.float32) / embed_len
    query_round = units[0].astype(jnp.bfloat16)

    def in_order(own, partner):
        left = jnp.where(first_core, own, partner)
        right = jnp.where(first_core, partner, own)
        return jnp.concatenate([left, right], axis=1)

    left, right = query_round[:, :half], query_round[:, half:]
    query_halves = [jnp.where(first_core, left, right), jnp.where(first_core, right, left)]
    score_part = sum(
        jnp.einsum("id,jd->ij", query, rows, preferred_element_type=jnp.float32)
        for query, rows in zip(query_halves, embed_halves)
    )
    passage_unit = ring_gather(units[1, :pass_dev]).transpose(1, 0, 2).reshape(pass_dev, width)
    scores = ring_sum(score_part) / SOFTMAX_TEMPER
    column = lax.iota(jnp.int32, dp * span)[None, :]
    is_passage = (column % span) // pairs_dev == 1
    own_ids = lax.iota(jnp.int32, pairs_dev)
    is_label = column == lax.axis_index(DP) * span + pairs_dev + own_ids[:, None]
    hard_column = (hard_index // pairs_dev) * span + 2 * pairs_dev + hard_index % pairs_dev
    is_candidate = is_passage | (column == hard_column[:, None])
    masked = jnp.where(is_candidate, scores, -jnp.inf)
    row_top = jnp.max(masked, axis=1)
    exps = jnp.exp(masked - row_top[:, None])
    exp_total = jnp.sum(exps, axis=1)
    per_query = row_top + jnp.log(exp_total) - jnp.sum(jnp.where(is_label, scores, 0.0), axis=1)
    local_total = jnp.sum(per_query)
    score_gradient = (
        (exps / exp_total[:, None] - is_label.astype(jnp.float32)) / SOFTMAX_TEMPER
    ).astype(jnp.bfloat16)
    by_owner = score_gradient.reshape(pairs_dev, dp, span).transpose(1, 0, 2)
    own_columns = lax.all_to_all(by_owner, DP, 0, 0, tiled=True)
    own_columns = jnp.pad(own_columns, ((0, 0), (0, span - pairs_dev), (0, 0)))
    own_columns = own_columns.reshape(dp * span, span)
    query_grad = in_order(
        *[
            jnp.einsum("ij,jd->id", score_gradient, rows, preferred_element_type=jnp.float32)
            for rows in embed_halves
        ]
    )
    both_grads = in_order(
        *[
            jnp.einsum("jc,jd->cd", own_columns, rows, preferred_element_type=jnp.float32)
            for rows in embed_halves
        ]
    )
    passage_grad = both_grads[pairs_dev : pairs_dev + pass_dev]
    passage_grad = ring_gather(passage_grad).transpose(1, 0, 2).reshape(pass_dev, width)
    passage_inner = jnp.sum(passage_grad * passage_unit, axis=1, keepdims=True)
    cotangent = (passage_grad - passage_inner * passage_unit) / embed_len[1, :pass_dev]
    grads = jnp.concatenate([query_grad, both_grads[pairs_dev:]], axis=0).reshape(units.shape)
    inner_sums = ring_sum(jnp.sum(grads * units, axis=2))[:, :, None]
    embed_grads = (grads - inner_sums * units) / embed_len

    gain_in = in_gain.astype(jnp.float32)
    gain_out = out_gain.astype(jnp.float32)
    x_float = layer_input.astype(jnp.float32)
    inv_rms = lax.rsqrt(jnp.mean(x_float * x_float, axis=-1, keepdims=True) + EPSILON)
    normed = (x_float * inv_rms * gain_in).astype(jnp.bfloat16)
    last_pos = lengths - 1
    n_last = jnp.take_along_axis(normed, last_pos[:, None, None], axis=1)[:, 0]
    x_last = jnp.take_along_axis(layer_input, last_pos[:, None, None], axis=1)[:, 0].astype(
        jnp.float32
    )
    value_lowrank = jnp.einsum(
        "pld,dr->plr", normed, down_value, preferred_element_type=jnp.float32
    ).astype(jnp.bfloat16)
    query_lowrank = jnp.dot(n_last, down_query, preferred_element_type=jnp.float32).astype(
        jnp.bfloat16
    )
    group_size = q_cols // kv_cols
    score_scale = HD ** (-0.5)
    cosine, sine = angle_table(seq_len, HD)
    kv_pre = jnp.einsum("pld,dc->plc", normed, kv_groups[0], preferred_element_type=jnp.float32)
    value_rows = (
        kv_pre[:, :, kv_cols:]
        + ADAPTER_SCALE
        * jnp.einsum(
            "plr,rc->plc", value_lowrank, value_up_weight, preferred_element_type=jnp.float32
        )
    ).astype(jnp.bfloat16)
    key_rows = rotate(kv_pre[:, :, :kv_cols], cosine[None], sine[None]).astype(jnp.bfloat16)
    query_before_rotation = jnp.dot(
        n_last, query_full, preferred_element_type=jnp.float32
    ) + ADAPTER_SCALE * jnp.dot(
        query_lowrank, query_up_weight, preferred_element_type=jnp.float32
    )
    cos_last = cosine[last_pos][:, None, :]
    sin_last = sine[last_pos][:, None, :]
    query_rot = rotate(
        query_before_rotation.reshape(pass_dev, group_size, HD), cos_last, sin_last
    ).astype(jnp.bfloat16)
    logits = (
        jnp.einsum("pgd,pld->pgl", query_rot, key_rows, preferred_element_type=jnp.float32)
        * score_scale
    )
    visible = lax.iota(jnp.int32, seq_len)[None, :] <= last_pos[:, None]
    logits = jnp.where(visible[:, None, :], logits, -1e30)
    row_peak = jnp.max(logits, axis=-1, keepdims=True)
    exponent_att = jnp.exp(logits - row_peak)
    attention = exponent_att / jnp.sum(exponent_att, axis=-1, keepdims=True)
    attention_round = attention.astype(jnp.bfloat16)
    mixed_heads = (
        jnp.einsum("pgl,pld->pgd", attention_round, value_rows, preferred_element_type=jnp.float32)
        .astype(jnp.bfloat16)
        .reshape(pass_dev, q_cols)
    )
    out_part = jnp.einsum("pc,dc->pd", mixed_heads, out_t, preferred_element_type=jnp.float32)
    hidden = x_last + ring_sum(out_part)

    inv_hidden = lax.rsqrt(jnp.mean(hidden * hidden, axis=-1, keepdims=True) + EPSILON)
    scaled = gain_out * cotangent
    d_hidden = scaled * inv_hidden - hidden * inv_hidden**3 * jnp.mean(
        hidden * scaled, axis=-1, keepdims=True
    )
    d_mixed = jnp.dot(
        d_hidden.astype(jnp.bfloat16), out_t, preferred_element_type=jnp.float32
    ).reshape(pass_dev, group_size, HD)
    value_float = value_rows.astype(jnp.float32)
    key_float = key_rows.astype(jnp.float32)
    d_attention = jnp.einsum("pgd,pld->pgl", d_mixed, value_float, precision=MATMUL_ACCURACY)
    d_logits = attention * (d_attention - jnp.sum(attention * d_attention, axis=-1, keepdims=True))
    d_values = jnp.einsum(
        "pgl,pgd->pld", attention_round.astype(jnp.float32), d_mixed, precision=MATMUL_ACCURACY
    )
    d_query = (
        jnp.einsum("pgl,pld->pgd", d_logits, key_float, precision=MATMUL_ACCURACY) * score_scale
    )
    d_keys = (
        jnp.einsum(
            "pgl,pgd->pld", d_logits, query_rot.astype(jnp.float32), precision=MATMUL_ACCURACY
        )
        * score_scale
    )
    d_query_pre = rotate(d_query, cos_last, -sin_last).reshape(pass_dev, q_cols)
    d_keys_pre = rotate(d_keys, cosine[None], -sine[None])

    tok_span = seq_len // mp
    first_tok = place * tok_span
    d_kv = jnp.concatenate([d_keys_pre, d_values], axis=2).astype(jnp.bfloat16)
    d_kv = d_kv.reshape(pass_dev, mp, tok_span, group_cols)
    d_kv_own = [
        lax.dynamic_index_in_dim(d_kv, (place + k) % mp, axis=1, keepdims=False) for k in range(mp)
    ]
    d_kv_own = [d_kv_own[0]] + [shifted(d_kv_own[k], "mp", k) for k in range(1, mp)]
    du_query_part = jnp.einsum(
        "rc,pc->rp",
        query_up_weight.astype(jnp.float32),
        d_query_pre,
        precision=MATMUL_ACCURACY,
    )
    du_value_part = jnp.einsum(
        "rc,nc->rn",
        value_up_weight.astype(jnp.float32),
        d_values.reshape(pass_dev * seq_len, kv_cols),
        precision=MATMUL_ACCURACY,
    )
    du_parts = jnp.pad(
        jnp.concatenate([du_value_part, du_query_part], axis=1), ((0, 0), (0, 128 - pass_dev))
    )
    du = (ADAPTER_SCALE * ring_sum(du_parts)).astype(jnp.bfloat16)
    d_query_round, du = lax.optimization_barrier((d_query_pre.astype(jnp.bfloat16), du))
    query_back = jnp.einsum(
        "pc,dc->pd", d_query_round, query_full, preferred_element_type=jnp.float32
    )
    query_back_all = ring_parts(query_back)
    rank = du.shape[0]
    n_tokens = pass_dev * seq_len
    du_value = du[:, :n_tokens]
    du_query = du[:, n_tokens : n_tokens + pass_dev]
    up_query_part = ADAPTER_SCALE * jnp.einsum(
        "pr,pc->rc", query_lowrank.astype(jnp.float32), d_query_pre, precision=MATMUL_ACCURACY
    )
    up_value_part = ADAPTER_SCALE * jnp.einsum(
        "plr,plc->rc", value_lowrank.astype(jnp.float32), d_values, precision=MATMUL_ACCURACY
    )

    quarter = width // mp
    first_feature = place * quarter
    normed_quarter = lax.dynamic_slice_in_dim(
        normed.reshape(n_tokens, width), first_feature, quarter, 1
    )
    last_quarter = lax.dynamic_slice_in_dim(n_last, first_feature, quarter, 1)
    down_value_part = jnp.einsum(
        "rn,nd->rd", du_value, normed_quarter, preferred_element_type=jnp.float32
    )
    down_query_part = jnp.einsum(
        "rp,pd->rd", du_query, last_quarter, preferred_element_type=jnp.float32
    )
    down_part = jnp.concatenate([down_query_part, down_value_part], axis=0).reshape(dp, -1)
    head_part = jnp.concatenate(
        [up_query_part.reshape(dp, -1), up_value_part.reshape(dp, -1)], axis=1
    )
    loss_part = jnp.broadcast_to(local_total / dp, (dp, 1))
    parts = jnp.concatenate([down_part, head_part, loss_part], axis=1)
    n_down = down_part.shape[1]
    n_head = head_part.shape[1]
    padded = -(-parts.shape[1] // 128) * 128
    parts = jnp.pad(parts, ((0, 0), (0, padded - parts.shape[1]))).reshape(dp, 1, padded)
    reduced = jnp.sum(lax.all_to_all(parts, DP, 0, 0, tiled=True), axis=0)
    totals = spread(reduced, (*DP, "mp")).reshape(dp, mp, padded)
    grad_down = (
        totals[:, :, :n_down]
        .reshape(2 * rank, dp // (2 * rank), mp, n_down)
        .transpose(0, 2, 1, 3)
        .reshape(2 * rank, width)
    )
    grad_down_query = grad_down[:rank].T
    grad_down_value = grad_down[rank:].T
    own = lax.dynamic_index_in_dim(totals, place, axis=1, keepdims=False)
    n_up_query = q_cols * rank // dp
    grad_up_query = own[:, n_down : n_down + n_up_query].reshape(rank, q_cols)
    grad_up_value = own[:, n_down + n_up_query : n_down + n_head].reshape(rank, kv_cols)
    loss = jnp.sum(totals[:, 0, n_down + n_head]) / total_pairs

    x_local = lax.dynamic_slice_in_dim(layer_input, first_tok, tok_span, 1).astype(jnp.float32)
    rms_local = lax.dynamic_slice_in_dim(inv_rms, first_tok, tok_span, 1)
    du_local = lax.dynamic_slice_in_dim(
        du_value.reshape(rank, pass_dev, seq_len), first_tok, tok_span, 2
    )
    tok_ids = first_tok + lax.iota(jnp.int32, tok_span)
    at_local = (tok_ids[None, :] == last_pos[:, None])[:, :, None]
    d_normed = jnp.einsum(
        "rpt,dr->ptd", du_local, down_value, preferred_element_type=jnp.float32
    )
    query_adapter = jnp.einsum(
        "rp,dr->pd", du_query, down_query, preferred_element_type=jnp.float32
    )
    d_normed = d_normed + jnp.where(at_local, query_adapter[:, None, :], 0.0)
    for group in range(mp):
        term = jnp.einsum(
            "ptc,dc->ptd",
            d_kv_own[group],
            kv_groups[group],
            preferred_element_type=jnp.float32,
        )
        term = term + jnp.where(at_local, query_back_all[group][:, None, :], 0.0)
        d_normed = d_normed + term.astype(jnp.bfloat16).astype(jnp.float32)
    d_input = gain_in * d_normed * rms_local - x_local * rms_local**3 * jnp.mean(
        x_local * gain_in * d_normed, axis=-1, keepdims=True
    )
    d_input = d_input + jnp.where(at_local, d_hidden[:, None, :], 0.0)
    grad_input = d_input.astype(jnp.bfloat16)
    return (
        loss,
        embed_grads[0],
        embed_grads[1],
        embed_grads[2],
        grad_input,
        grad_down_query,
        grad_up_query,
        grad_down_value,
        grad_up_value,
    )


def solution(mesh):
    staged = Mesh(mesh.devices.reshape(4, 4, 2, 2, 4), (*DP, "mp"))
    in_specs = (
        P(DP, "mp"),
        P(DP, "mp"),
        P(DP, "mp"),
        P(DP),
        P(DP, None, None),
        P(DP),
        P(),
        P(),
        P(DP, "mp"),
        P(DP, "mp"),
        P(DP, "mp"),
        P("mp", DP),
        P(),
        P(None, "mp"),
        P(),
        P(None, "mp"),
    )
    out_specs = (
        P(),
        P(DP, "mp"),
        P(DP, "mp"),
        P(DP, "mp"),
        P(DP, "mp", None),
        P(),
        P(None, "mp"),
        P(),
        P(None, "mp"),
    )
    return jax.shard_map(
        on_device, mesh=staged, in_specs=in_specs, out_specs=out_specs, check_vma=False
    )
```

```python
import jax
import jax.numpy as jnp
from jax import lax
from jax.sharding import Mesh
from jax.sharding import PartitionSpec as P

HD = 128
DP = ("y", "x", "zh", "core")


EPSILON = 1e-05
SOFTMAX_TEMPER = 0.01
ADAPTER_SCALE = 2.0
ROPE_BASE = 10000.0
MATMUL_ACCURACY = lax.Precision.HIGHEST


def angle_table(seq_len, head_dim):
    half_dim = head_dim // 2
    frequency = ROPE_BASE ** (-(jnp.arange(half_dim, dtype=jnp.float32) * 2.0 / head_dim))
    angles = jnp.arange(seq_len, dtype=jnp.float32)[:, None] * frequency[None, :]
    return (jnp.cos(angles), jnp.sin(angles))


def rotate(field, cosine, sine):
    half_dim = field.shape[-1] // 2
    leading = field[..., :half_dim]
    trailing = field[..., half_dim:]
    return jnp.concatenate(
        [leading * cosine - trailing * sine, trailing * cosine + leading * sine], axis=-1
    )


def shifted(value, axis_name, shift):
    size = lax.axis_size(axis_name)
    return lax.ppermute(value, axis_name, [(i, (i + shift) % size) for i in range(size)])


def ring_sum(value):
    one, two, three = (shifted(value, "mp", k) for k in (1, 2, 3))
    return (value + two) + (one + three)


def ring_parts(value):
    return [value] + [shifted(value, "mp", k) for k in (1, 2, 3)]


def ring_gather(value):
    parts = jnp.stack(ring_parts(value))
    place = lax.axis_index("mp")
    order = (place - lax.iota(jnp.int32, 4)) % 4
    return jnp.take(parts, order, axis=0)


def spread(value, axis_name):
    size = lax.axis_size(axis_name)
    return lax.all_to_all(
        jnp.broadcast_to(value[None], (size,) + value.shape), axis_name, 0, 0, tiled=True
    )


def pair_gather(value, axis_name):
    other = lax.ppermute(value, axis_name, [(0, 1), (1, 0)])
    at_first = lax.axis_index(axis_name) == 0
    return jnp.stack([jnp.where(at_first, value, other), jnp.where(at_first, other, value)])


def after(value, *first):
    return lax.optimization_barrier((value, *first))[0]


def core_halves(value):
    half = value.shape[1] // 2
    at_first = lax.axis_index("core") == 0
    left, right = value[:, :half], value[:, half:]
    kept = jnp.where(at_first, left, right)
    other = lax.ppermute(jnp.where(at_first, right, left), "core", [(0, 1), (1, 0)])
    return jnp.stack([jnp.where(at_first, kept, other), jnp.where(at_first, other, kept)])


def on_device(
    queries,
    passages,
    negatives,
    hard_index,
    layer_input,
    lengths,
    in_gain,
    out_gain,
    w_query,
    w_key,
    w_value,
    w_out,
    down_query,
    query_up_weight,
    down_value,
    value_up_weight,
):
    dp = lax.axis_size(DP)
    mp = lax.axis_size("mp")
    place = lax.axis_index("mp")
    pairs_dev, feature_dev = queries.shape
    total_pairs = pairs_dev * dp
    pass_dev, seq_len, width = layer_input.shape
    kv_cols = w_key.shape[1]
    q_cols = w_query.shape[1]
    group_cols = 2 * kv_cols

    kv_shard = jnp.concatenate([w_key, w_value], axis=1)
    weights = lax.all_gather(
        jnp.concatenate([w_query, w_out.T, kv_shard], axis=1), DP, axis=0, tiled=True
    )
    query_full = weights[:, :q_cols]
    out_t = weights[:, q_cols : 2 * q_cols]

    half = feature_dev // 2
    span = 3 * pairs_dev
    first_core = lax.axis_index("core") == 0
    embeds = jnp.stack([queries, passages, negatives])
    by_core = core_halves(embeds.reshape(span, feature_dev))
    by_chip = pair_gather(by_core, "zh")
    layer_input = after(layer_input, by_chip)
    mine = spread(by_chip, ("y", "x")).reshape(dp * span, half)
    theirs = lax.ppermute(mine, "core", [(0, 1), (1, 0)])
    kv_shards = ring_parts(after(kv_shard, theirs))
    others = lax.all_gather(jnp.concatenate(kv_shards[1:], axis=1), DP, axis=0, tiled=True)
    raw_halves = [rows.astype(jnp.float32) for rows in (mine, theirs)]
    square_sums = ring_sum(sum(jnp.sum(rows * rows, axis=1) for rows in raw_halves))
    all_len = jnp.sqrt(square_sums)
    embed_halves = [(rows / all_len[:, None]).astype(jnp.bfloat16) for rows in raw_halves]
    embed_len = lax.dynamic_slice_in_dim(all_len, lax.axis_index(DP) * span, span)
    embed_len = embed_len.reshape(3, pairs_dev, 1)
    units = embeds.astype(jnp.float32) / embed_len
    query_round = units[0].astype(jnp.bfloat16)

    def in_order(own, partner):
        left = jnp.where(first_core, own, partner)
        right = jnp.where(first_core, partner, own)
        return jnp.concatenate([left, right], axis=1)

    left, right = query_round[:, :half], query_round[:, half:]
    query_halves = [jnp.where(first_core, left, right), jnp.where(first_core, right, left)]
    score_part = sum(
        jnp.einsum("id,jd->ij", query, rows, preferred_element_type=jnp.float32)
        for query, rows in zip(query_halves, embed_halves)
    )
    scores = ring_sum(score_part) / SOFTMAX_TEMPER
    column = lax.iota(jnp.int32, dp * span)[None, :]
    is_passage = (column % span) // pairs_dev == 1
    own_ids = lax.iota(jnp.int32, pairs_dev)
    is_label = column == lax.axis_index(DP) * span + pairs_dev + own_ids[:, None]
    hard_column = (hard_index // pairs_dev) * span + 2 * pairs_dev + hard_index % pairs_dev
    is_candidate = is_passage | (column == hard_column[:, None])
    masked = jnp.where(is_candidate, scores, -jnp.inf)
    row_top = jnp.max(masked, axis=1)
    exps = jnp.exp(masked - row_top[:, None])
    exp_total = jnp.sum(exps, axis=1)
    per_query = row_top + jnp.log(exp_total) - jnp.sum(jnp.where(is_label, scores, 0.0), axis=1)
    local_total = jnp.sum(per_query)
    score_gradient = (
        (exps / exp_total[:, None] - is_label.astype(jnp.float32)) / SOFTMAX_TEMPER
    ).astype(jnp.bfloat16)
    passage_unit = ring_gather(after(units[1, :pass_dev], score_gradient))
    passage_unit = passage_unit.transpose(1, 0, 2).reshape(pass_dev, width)
    by_owner = score_gradient.reshape(pairs_dev, dp, span).transpose(1, 0, 2)
    own_columns = lax.all_to_all(by_owner, DP, 0, 0, tiled=True)
    own_columns = jnp.pad(own_columns, ((0, 0), (0, span - pairs_dev), (0, 0)))
    own_columns = own_columns.reshape(dp * span, span)
    query_grad = in_order(
        *[
            jnp.einsum("ij,jd->id", score_gradient, rows, preferred_element_type=jnp.float32)
            for rows in embed_halves
        ]
    )
    both_grads = in_order(
        *[
            jnp.einsum("jc,jd->cd", own_columns, rows, preferred_element_type=jnp.float32)
            for rows in embed_halves
        ]
    )
    passage_grad = both_grads[pairs_dev : pairs_dev + pass_dev]
    passage_grad = ring_gather(passage_grad).transpose(1, 0, 2).reshape(pass_dev, width)
    passage_inner = jnp.sum(passage_grad * passage_unit, axis=1, keepdims=True)
    cotangent = (passage_grad - passage_inner * passage_unit) / embed_len[1, :pass_dev]
    grads = jnp.concatenate([query_grad, both_grads[pairs_dev:]], axis=0).reshape(units.shape)
    grads = after(grads, cotangent)
    inner_sums = ring_sum(jnp.sum(grads * units, axis=2))[:, :, None]
    embed_grads = (grads - inner_sums * units) / embed_len

    gain_in = in_gain.astype(jnp.float32)
    gain_out = out_gain.astype(jnp.float32)
    x_float = layer_input.astype(jnp.float32)
    inv_rms = lax.rsqrt(jnp.mean(x_float * x_float, axis=-1, keepdims=True) + EPSILON)
    normed = (x_float * inv_rms * gain_in).astype(jnp.bfloat16)
    last_pos = lengths - 1
    n_last = jnp.take_along_axis(normed, last_pos[:, None, None], axis=1)[:, 0]
    x_last = jnp.take_along_axis(layer_input, last_pos[:, None, None], axis=1)[:, 0].astype(
        jnp.float32
    )
    value_lowrank = jnp.einsum(
        "pld,dr->plr", normed, down_value, preferred_element_type=jnp.float32
    ).astype(jnp.bfloat16)
    query_lowrank = jnp.dot(n_last, down_query, preferred_element_type=jnp.float32).astype(
        jnp.bfloat16
    )
    group_size = q_cols // kv_cols
    score_scale = HD ** (-0.5)
    cosine, sine = angle_table(seq_len, HD)
    kv_pre = jnp.einsum("pld,dc->plc", normed, weights[:, 2 * q_cols :], preferred_element_type=jnp.float32)
    value_rows = (
        kv_pre[:, :, kv_cols:]
        + ADAPTER_SCALE
        * jnp.einsum(
            "plr,rc->plc", value_lowrank, value_up_weight, preferred_element_type=jnp.float32
        )
    ).astype(jnp.bfloat16)
    key_rows = rotate(kv_pre[:, :, :kv_cols], cosine[None], sine[None]).astype(jnp.bfloat16)
    query_before_rotation = jnp.dot(
        n_last, query_full, preferred_element_type=jnp.float32
    ) + ADAPTER_SCALE * jnp.dot(
        query_lowrank, query_up_weight, preferred_element_type=jnp.float32
    )
    cos_last = cosine[last_pos][:, None, :]
    sin_last = sine[last_pos][:, None, :]
    query_rot = rotate(
        query_before_rotation.reshape(pass_dev, group_size, HD), cos_last, sin_last
    ).astype(jnp.bfloat16)
    logits = (
        jnp.einsum("pgd,pld->pgl", query_rot, key_rows, preferred_element_type=jnp.float32)
        * score_scale
    )
    visible = lax.iota(jnp.int32, seq_len)[None, :] <= last_pos[:, None]
    logits = jnp.where(visible[:, None, :], logits, -1e30)
    row_peak = jnp.max(logits, axis=-1, keepdims=True)
    exponent_att = jnp.exp(logits - row_peak)
    attention = exponent_att / jnp.sum(exponent_att, axis=-1, keepdims=True)
    attention_round = attention.astype(jnp.bfloat16)
    mixed_heads = (
        jnp.einsum("pgl,pld->pgd", attention_round, value_rows, preferred_element_type=jnp.float32)
        .astype(jnp.bfloat16)
        .reshape(pass_dev, q_cols)
    )
    out_part = jnp.einsum("pc,dc->pd", mixed_heads, out_t, preferred_element_type=jnp.float32)
    hidden = x_last + ring_sum(out_part)

    inv_hidden = lax.rsqrt(jnp.mean(hidden * hidden, axis=-1, keepdims=True) + EPSILON)
    scaled = gain_out * cotangent
    d_hidden = scaled * inv_hidden - hidden * inv_hidden**3 * jnp.mean(
        hidden * scaled, axis=-1, keepdims=True
    )
    d_mixed = jnp.dot(
        d_hidden.astype(jnp.bfloat16), out_t, preferred_element_type=jnp.float32
    ).reshape(pass_dev, group_size, HD)
    value_float = value_rows.astype(jnp.float32)
    key_float = key_rows.astype(jnp.float32)
    d_attention = jnp.einsum("pgd,pld->pgl", d_mixed, value_float, precision=MATMUL_ACCURACY)
    d_logits = attention * (d_attention - jnp.sum(attention * d_attention, axis=-1, keepdims=True))
    d_values = jnp.einsum(
        "pgl,pgd->pld", attention_round.astype(jnp.float32), d_mixed, precision=MATMUL_ACCURACY
    )
    d_query = (
        jnp.einsum("pgl,pld->pgd", d_logits, key_float, precision=MATMUL_ACCURACY) * score_scale
    )
    d_keys = (
        jnp.einsum(
            "pgl,pgd->pld", d_logits, query_rot.astype(jnp.float32), precision=MATMUL_ACCURACY
        )
        * score_scale
    )
    d_query_pre = rotate(d_query, cos_last, -sin_last).reshape(pass_dev, q_cols)
    d_keys_pre = rotate(d_keys, cosine[None], -sine[None])

    tok_span = seq_len // mp
    first_tok = place * tok_span
    d_kv = jnp.concatenate([d_keys_pre, d_values], axis=2).astype(jnp.bfloat16)
    d_kv = d_kv.reshape(pass_dev, mp, tok_span, group_cols)
    d_kv_own = [
        lax.dynamic_index_in_dim(d_kv, (place + k) % mp, axis=1, keepdims=False) for k in range(mp)
    ]
    d_kv_own = [d_kv_own[0]] + [shifted(d_kv_own[k], "mp", k) for k in range(1, mp)]
    du_query_part = jnp.einsum(
        "rc,pc->rp",
        query_up_weight.astype(jnp.float32),
        d_query_pre,
        precision=MATMUL_ACCURACY,
    )
    du_value_part = jnp.einsum(
        "rc,nc->rn",
        value_up_weight.astype(jnp.float32),
        d_values.reshape(pass_dev * seq_len, kv_cols),
        precision=MATMUL_ACCURACY,
    )
    du_parts = jnp.pad(
        jnp.concatenate([du_value_part, du_query_part], axis=1), ((0, 0), (0, 128 - pass_dev))
    )
    du = (ADAPTER_SCALE * ring_sum(du_parts)).astype(jnp.bfloat16)
    rank = du.shape[0]
    n_tokens = pass_dev * seq_len
    du_value = du[:, :n_tokens]
    du_query = du[:, n_tokens : n_tokens + pass_dev]
    up_query_part = ADAPTER_SCALE * jnp.einsum(
        "pr,pc->rc", query_lowrank.astype(jnp.float32), d_query_pre, precision=MATMUL_ACCURACY
    )
    up_value_part = ADAPTER_SCALE * jnp.einsum(
        "plr,plc->rc", value_lowrank.astype(jnp.float32), d_values, precision=MATMUL_ACCURACY
    )

    quarter = width // mp
    first_feature = place * quarter
    normed_quarter = lax.dynamic_slice_in_dim(
        normed.reshape(n_tokens, width), first_feature, quarter, 1
    )
    last_quarter = lax.dynamic_slice_in_dim(n_last, first_feature, quarter, 1)
    down_value_part = jnp.einsum(
        "rn,nd->rd", du_value, normed_quarter, preferred_element_type=jnp.float32
    )
    down_query_part = jnp.einsum(
        "rp,pd->rd", du_query, last_quarter, preferred_element_type=jnp.float32
    )
    down_part = jnp.concatenate([down_query_part, down_value_part], axis=0).reshape(dp, -1)
    head_part = jnp.concatenate(
        [up_query_part.reshape(dp, -1), up_value_part.reshape(dp, -1)], axis=1
    )
    loss_part = jnp.broadcast_to(local_total / dp, (dp, 1))
    parts = jnp.concatenate([down_part, head_part, loss_part], axis=1)
    n_down = down_part.shape[1]
    n_head = head_part.shape[1]
    padded = -(-parts.shape[1] // 128) * 128
    parts = jnp.pad(parts, ((0, 0), (0, padded - parts.shape[1]))).reshape(dp, 1, padded)
    query_back = jnp.einsum(
        "pc,dc->pd",
        after(d_query_pre.astype(jnp.bfloat16), parts),
        query_full,
        preferred_element_type=jnp.float32,
    )
    query_back_all = ring_parts(query_back)
    reduced = jnp.sum(lax.all_to_all(parts, DP, 0, 0, tiled=True), axis=0)
    totals = spread(reduced, (*DP, "mp")).reshape(dp, mp, padded)
    grad_down = (
        totals[:, :, :n_down]
        .reshape(2 * rank, dp // (2 * rank), mp, n_down)
        .transpose(0, 2, 1, 3)
        .reshape(2 * rank, width)
    )
    grad_down_query = grad_down[:rank].T
    grad_down_value = grad_down[rank:].T
    own = lax.dynamic_index_in_dim(totals, place, axis=1, keepdims=False)
    n_up_query = q_cols * rank // dp
    grad_up_query = own[:, n_down : n_down + n_up_query].reshape(rank, q_cols)
    grad_up_value = own[:, n_down + n_up_query : n_down + n_head].reshape(rank, kv_cols)
    loss = jnp.sum(totals[:, 0, n_down + n_head]) / total_pairs

    d_kv_own = [d_kv_own[0]] + [after(blocks, reduced) for blocks in d_kv_own[1:]]
    kv_groups = [weights[:, 2 * q_cols :]]
    kv_groups += [others[:, k * group_cols : (k + 1) * group_cols] for k in range(mp - 1)]
    x_local = lax.dynamic_slice_in_dim(layer_input, first_tok, tok_span, 1).astype(jnp.float32)
    rms_local = lax.dynamic_slice_in_dim(inv_rms, first_tok, tok_span, 1)
    du_local = lax.dynamic_slice_in_dim(
        du_value.reshape(rank, pass_dev, seq_len), first_tok, tok_span, 2
    )
    tok_ids = first_tok + lax.iota(jnp.int32, tok_span)
    at_local = (tok_ids[None, :] == last_pos[:, None])[:, :, None]
    d_normed = jnp.einsum(
        "rpt,dr->ptd", du_local, down_value, preferred_element_type=jnp.float32
    )
    query_adapter = jnp.einsum(
        "rp,dr->pd", du_query, down_query, preferred_element_type=jnp.float32
    )
    d_normed = d_normed + jnp.where(at_local, query_adapter[:, None, :], 0.0)
    for group in range(mp):
        term = jnp.einsum(
            "ptc,dc->ptd",
            d_kv_own[group],
            kv_groups[group],
            preferred_element_type=jnp.float32,
        )
        term = term + jnp.where(at_local, query_back_all[group][:, None, :], 0.0)
        d_normed = d_normed + term.astype(jnp.bfloat16).astype(jnp.float32)
    d_input = gain_in * d_normed * rms_local - x_local * rms_local**3 * jnp.mean(
        x_local * gain_in * d_normed, axis=-1, keepdims=True
    )
    d_input = d_input + jnp.where(at_local, d_hidden[:, None, :], 0.0)
    grad_input = d_input.astype(jnp.bfloat16)
    return (
        loss,
        embed_grads[0],
        embed_grads[1],
        embed_grads[2],
        grad_input,
        grad_down_query,
        grad_up_query,
        grad_down_value,
        grad_up_value,
    )


def solution(mesh):
    staged = Mesh(mesh.devices.reshape(4, 4, 2, 2, 4), (*DP, "mp"))
    in_specs = (
        P(DP, "mp"),
        P(DP, "mp"),
        P(DP, "mp"),
        P(DP),
        P(DP, None, None),
        P(DP),
        P(),
        P(),
        P(DP, "mp"),
        P(DP, "mp"),
        P(DP, "mp"),
        P("mp", DP),
        P(),
        P(None, "mp"),
        P(),
        P(None, "mp"),
    )
    out_specs = (
        P(),
        P(DP, "mp"),
        P(DP, "mp"),
        P(DP, "mp"),
        P(DP, "mp", None),
        P(),
        P(None, "mp"),
        P(),
        P(None, "mp"),
    )
    return jax.shard_map(
        on_device, mesh=staged, in_specs=in_specs, out_specs=out_specs, check_vma=False
    )
```

```python
import jax
import jax.numpy as jnp
from jax import lax
from jax.sharding import Mesh
from jax.sharding import PartitionSpec as P

HD = 128
DP = ("y", "x", "zh", "core")


EPSILON = 1e-05
SOFTMAX_TEMPER = 0.01
ADAPTER_SCALE = 2.0
ROPE_BASE = 10000.0
MATMUL_ACCURACY = lax.Precision.HIGHEST


def angle_table(seq_len, head_dim):
    half_dim = head_dim // 2
    frequency = ROPE_BASE ** (-(jnp.arange(half_dim, dtype=jnp.float32) * 2.0 / head_dim))
    angles = jnp.arange(seq_len, dtype=jnp.float32)[:, None] * frequency[None, :]
    return (jnp.cos(angles), jnp.sin(angles))


def rotate(field, cosine, sine):
    half_dim = field.shape[-1] // 2
    leading = field[..., :half_dim]
    trailing = field[..., half_dim:]
    return jnp.concatenate(
        [leading * cosine - trailing * sine, trailing * cosine + leading * sine], axis=-1
    )


def shifted(value, axis_name, shift):
    size = lax.axis_size(axis_name)
    return lax.ppermute(value, axis_name, [(i, (i + shift) % size) for i in range(size)])


def ring_sum(value):
    one, two, three = (shifted(value, "mp", k) for k in (1, 2, 3))
    return (value + two) + (one + three)


def ring_parts(value):
    return [value] + [shifted(value, "mp", k) for k in (1, 2, 3)]


def ring_gather(value):
    parts = jnp.stack(ring_parts(value))
    place = lax.axis_index("mp")
    order = (place - lax.iota(jnp.int32, 4)) % 4
    return jnp.take(parts, order, axis=0)


def spread(value, axis_name):
    size = lax.axis_size(axis_name)
    return lax.all_to_all(
        jnp.broadcast_to(value[None], (size,) + value.shape), axis_name, 0, 0, tiled=True
    )


def pair_gather(value, axis_name):
    other = lax.ppermute(value, axis_name, [(0, 1), (1, 0)])
    at_first = lax.axis_index(axis_name) == 0
    return jnp.stack([jnp.where(at_first, value, other), jnp.where(at_first, other, value)])


def after(value, *first):
    return lax.optimization_barrier((value, *first))[0]


def core_halves(value):
    half = value.shape[1] // 2
    at_first = lax.axis_index("core") == 0
    left, right = value[:, :half], value[:, half:]
    kept = jnp.where(at_first, left, right)
    other = lax.ppermute(jnp.where(at_first, right, left), "core", [(0, 1), (1, 0)])
    return jnp.stack([jnp.where(at_first, kept, other), jnp.where(at_first, other, kept)])


def gather_rows(shard):
    pair = pair_gather(shard, "core").reshape(2 * shard.shape[0], shard.shape[1])
    moved = lax.ppermute(pair, ("zh", "core"), [(0, 2), (3, 1)])
    pair = jnp.where(lax.axis_index("zh") == lax.axis_index("core"), pair, moved)
    return lax.all_gather(pair, ("y", "x", "core"), axis=0, tiled=True)


def on_device(
    queries,
    passages,
    negatives,
    hard_index,
    layer_input,
    lengths,
    in_gain,
    out_gain,
    w_query,
    w_key,
    w_value,
    w_out,
    down_query,
    query_up_weight,
    down_value,
    value_up_weight,
):
    dp = lax.axis_size(DP)
    mp = lax.axis_size("mp")
    place = lax.axis_index("mp")
    pairs_dev, feature_dev = queries.shape
    total_pairs = pairs_dev * dp
    pass_dev, seq_len, width = layer_input.shape
    kv_cols = w_key.shape[1]
    q_cols = w_query.shape[1]
    group_cols = 2 * kv_cols

    kv_shard = jnp.concatenate([w_key, w_value], axis=1)
    weights = gather_rows(jnp.concatenate([w_query, w_out.T, kv_shard], axis=1))
    query_full = weights[:, :q_cols]
    out_t = weights[:, q_cols : 2 * q_cols]

    half = feature_dev // 2
    span = 3 * pairs_dev
    first_core = lax.axis_index("core") == 0
    embeds = jnp.stack([queries, passages, negatives])
    by_core = core_halves(embeds.reshape(span, feature_dev))
    by_chip = pair_gather(by_core, "zh")
    layer_input = after(layer_input, by_chip)
    mine = spread(by_chip, ("y", "x")).reshape(dp * span, half)
    theirs = lax.ppermute(mine, "core", [(0, 1), (1, 0)])
    kv_shards = ring_parts(after(kv_shard, theirs))
    others = gather_rows(jnp.concatenate(kv_shards[1:], axis=1))
    raw_halves = [rows.astype(jnp.float32) for rows in (mine, theirs)]
    square_sums = ring_sum(sum(jnp.sum(rows * rows, axis=1) for rows in raw_halves))
    all_len = jnp.sqrt(square_sums)
    embed_halves = [(rows / all_len[:, None]).astype(jnp.bfloat16) for rows in raw_halves]
    embed_len = lax.dynamic_slice_in_dim(all_len, lax.axis_index(DP) * span, span)
    embed_len = embed_len.reshape(3, pairs_dev, 1)
    units = embeds.astype(jnp.float32) / embed_len
    query_round = units[0].astype(jnp.bfloat16)

    def in_order(own, partner):
        left = jnp.where(first_core, own, partner)
        right = jnp.where(first_core, partner, own)
        return jnp.concatenate([left, right], axis=1)

    left, right = query_round[:, :half], query_round[:, half:]
    query_halves = [jnp.where(first_core, left, right), jnp.where(first_core, right, left)]
    score_part = sum(
        jnp.einsum("id,jd->ij", query, rows, preferred_element_type=jnp.float32)
        for query, rows in zip(query_halves, embed_halves)
    )
    scores = ring_sum(score_part) / SOFTMAX_TEMPER
    column = lax.iota(jnp.int32, dp * span)[None, :]
    is_passage = (column % span) // pairs_dev == 1
    own_ids = lax.iota(jnp.int32, pairs_dev)
    is_label = column == lax.axis_index(DP) * span + pairs_dev + own_ids[:, None]
    hard_column = (hard_index // pairs_dev) * span + 2 * pairs_dev + hard_index % pairs_dev
    is_candidate = is_passage | (column == hard_column[:, None])
    masked = jnp.where(is_candidate, scores, -jnp.inf)
    row_top = jnp.max(masked, axis=1)
    exps = jnp.exp(masked - row_top[:, None])
    exp_total = jnp.sum(exps, axis=1)
    per_query = row_top + jnp.log(exp_total) - jnp.sum(jnp.where(is_label, scores, 0.0), axis=1)
    local_total = jnp.sum(per_query)
    score_gradient = (
        (exps / exp_total[:, None] - is_label.astype(jnp.float32)) / SOFTMAX_TEMPER
    ).astype(jnp.bfloat16)
    passage_unit = ring_gather(after(units[1, :pass_dev], score_gradient))
    passage_unit = passage_unit.transpose(1, 0, 2).reshape(pass_dev, width)
    by_owner = score_gradient.reshape(pairs_dev, dp, span).transpose(1, 0, 2)
    own_columns = lax.all_to_all(by_owner, DP, 0, 0, tiled=True)
    own_columns = jnp.pad(own_columns, ((0, 0), (0, span - pairs_dev), (0, 0)))
    own_columns = own_columns.reshape(dp * span, span)
    query_grad = in_order(
        *[
            jnp.einsum("ij,jd->id", score_gradient, rows, preferred_element_type=jnp.float32)
            for rows in embed_halves
        ]
    )
    both_grads = in_order(
        *[
            jnp.einsum("jc,jd->cd", own_columns, rows, preferred_element_type=jnp.float32)
            for rows in embed_halves
        ]
    )
    passage_grad = both_grads[pairs_dev : pairs_dev + pass_dev]
    passage_grad = ring_gather(passage_grad).transpose(1, 0, 2).reshape(pass_dev, width)
    passage_inner = jnp.sum(passage_grad * passage_unit, axis=1, keepdims=True)
    cotangent = (passage_grad - passage_inner * passage_unit) / embed_len[1, :pass_dev]
    grads = jnp.concatenate([query_grad, both_grads[pairs_dev:]], axis=0).reshape(units.shape)
    grads = after(grads, cotangent)
    inner_sums = ring_sum(jnp.sum(grads * units, axis=2))[:, :, None]
    embed_grads = (grads - inner_sums * units) / embed_len

    gain_in = in_gain.astype(jnp.float32)
    gain_out = out_gain.astype(jnp.float32)
    x_float = layer_input.astype(jnp.float32)
    inv_rms = lax.rsqrt(jnp.mean(x_float * x_float, axis=-1, keepdims=True) + EPSILON)
    normed = (x_float * inv_rms * gain_in).astype(jnp.bfloat16)
    last_pos = lengths - 1
    n_last = jnp.take_along_axis(normed, last_pos[:, None, None], axis=1)[:, 0]
    x_last = jnp.take_along_axis(layer_input, last_pos[:, None, None], axis=1)[:, 0].astype(
        jnp.float32
    )
    value_lowrank = jnp.einsum(
        "pld,dr->plr", normed, down_value, preferred_element_type=jnp.float32
    ).astype(jnp.bfloat16)
    query_lowrank = jnp.dot(n_last, down_query, preferred_element_type=jnp.float32).astype(
        jnp.bfloat16
    )
    group_size = q_cols // kv_cols
    score_scale = HD ** (-0.5)
    cosine, sine = angle_table(seq_len, HD)
    kv_pre = jnp.einsum("pld,dc->plc", normed, weights[:, 2 * q_cols :], preferred_element_type=jnp.float32)
    value_rows = (
        kv_pre[:, :, kv_cols:]
        + ADAPTER_SCALE
        * jnp.einsum(
            "plr,rc->plc", value_lowrank, value_up_weight, preferred_element_type=jnp.float32
        )
    ).astype(jnp.bfloat16)
    key_rows = rotate(kv_pre[:, :, :kv_cols], cosine[None], sine[None]).astype(jnp.bfloat16)
    query_before_rotation = jnp.dot(
        n_last, query_full, preferred_element_type=jnp.float32
    ) + ADAPTER_SCALE * jnp.dot(
        query_lowrank, query_up_weight, preferred_element_type=jnp.float32
    )
    cos_last = cosine[last_pos][:, None, :]
    sin_last = sine[last_pos][:, None, :]
    query_rot = rotate(
        query_before_rotation.reshape(pass_dev, group_size, HD), cos_last, sin_last
    ).astype(jnp.bfloat16)
    logits = (
        jnp.einsum("pgd,pld->pgl", query_rot, key_rows, preferred_element_type=jnp.float32)
        * score_scale
    )
    visible = lax.iota(jnp.int32, seq_len)[None, :] <= last_pos[:, None]
    logits = jnp.where(visible[:, None, :], logits, -1e30)
    row_peak = jnp.max(logits, axis=-1, keepdims=True)
    exponent_att = jnp.exp(logits - row_peak)
    attention = exponent_att / jnp.sum(exponent_att, axis=-1, keepdims=True)
    attention_round = attention.astype(jnp.bfloat16)
    mixed_heads = (
        jnp.einsum("pgl,pld->pgd", attention_round, value_rows, preferred_element_type=jnp.float32)
        .astype(jnp.bfloat16)
        .reshape(pass_dev, q_cols)
    )
    out_part = jnp.einsum("pc,dc->pd", mixed_heads, out_t, preferred_element_type=jnp.float32)
    hidden = x_last + ring_sum(out_part)

    inv_hidden = lax.rsqrt(jnp.mean(hidden * hidden, axis=-1, keepdims=True) + EPSILON)
    scaled = gain_out * cotangent
    d_hidden = scaled * inv_hidden - hidden * inv_hidden**3 * jnp.mean(
        hidden * scaled, axis=-1, keepdims=True
    )
    d_mixed = jnp.dot(
        d_hidden.astype(jnp.bfloat16), out_t, preferred_element_type=jnp.float32
    ).reshape(pass_dev, group_size, HD)
    value_float = value_rows.astype(jnp.float32)
    key_float = key_rows.astype(jnp.float32)
    d_attention = jnp.einsum("pgd,pld->pgl", d_mixed, value_float, precision=MATMUL_ACCURACY)
    d_logits = attention * (d_attention - jnp.sum(attention * d_attention, axis=-1, keepdims=True))
    d_values = jnp.einsum(
        "pgl,pgd->pld", attention_round.astype(jnp.float32), d_mixed, precision=MATMUL_ACCURACY
    )
    d_query = (
        jnp.einsum("pgl,pld->pgd", d_logits, key_float, precision=MATMUL_ACCURACY) * score_scale
    )
    d_keys = (
        jnp.einsum(
            "pgl,pgd->pld", d_logits, query_rot.astype(jnp.float32), precision=MATMUL_ACCURACY
        )
        * score_scale
    )
    d_query_pre = rotate(d_query, cos_last, -sin_last).reshape(pass_dev, q_cols)
    d_keys_pre = rotate(d_keys, cosine[None], -sine[None])

    tok_span = seq_len // mp
    first_tok = place * tok_span
    d_kv = jnp.concatenate([d_keys_pre, d_values], axis=2).astype(jnp.bfloat16)
    d_kv = d_kv.reshape(pass_dev, mp, tok_span, group_cols)
    d_kv_own = [
        lax.dynamic_index_in_dim(d_kv, (place + k) % mp, axis=1, keepdims=False) for k in range(mp)
    ]
    d_kv_own = [d_kv_own[0]] + [shifted(d_kv_own[k], "mp", k) for k in range(1, mp)]
    du_query_part = jnp.einsum(
        "rc,pc->rp",
        query_up_weight.astype(jnp.float32),
        d_query_pre,
        precision=MATMUL_ACCURACY,
    )
    du_value_part = jnp.einsum(
        "rc,nc->rn",
        value_up_weight.astype(jnp.float32),
        d_values.reshape(pass_dev * seq_len, kv_cols),
        precision=MATMUL_ACCURACY,
    )
    du_parts = jnp.pad(
        jnp.concatenate([du_value_part, du_query_part], axis=1), ((0, 0), (0, 128 - pass_dev))
    )
    du = (ADAPTER_SCALE * ring_sum(du_parts)).astype(jnp.bfloat16)
    rank = du.shape[0]
    n_tokens = pass_dev * seq_len
    du_value = du[:, :n_tokens]
    du_query = du[:, n_tokens : n_tokens + pass_dev]
    up_query_part = ADAPTER_SCALE * jnp.einsum(
        "pr,pc->rc", query_lowrank.astype(jnp.float32), d_query_pre, precision=MATMUL_ACCURACY
    )
    up_value_part = ADAPTER_SCALE * jnp.einsum(
        "plr,plc->rc", value_lowrank.astype(jnp.float32), d_values, precision=MATMUL_ACCURACY
    )

    quarter = width // mp
    first_feature = place * quarter
    normed_quarter = lax.dynamic_slice_in_dim(
        normed.reshape(n_tokens, width), first_feature, quarter, 1
    )
    last_quarter = lax.dynamic_slice_in_dim(n_last, first_feature, quarter, 1)
    down_value_part = jnp.einsum(
        "rn,nd->rd", du_value, normed_quarter, preferred_element_type=jnp.float32
    )
    down_query_part = jnp.einsum(
        "rp,pd->rd", du_query, last_quarter, preferred_element_type=jnp.float32
    )
    down_part = jnp.concatenate([down_query_part, down_value_part], axis=0).reshape(dp, -1)
    head_part = jnp.concatenate(
        [up_query_part.reshape(dp, -1), up_value_part.reshape(dp, -1)], axis=1
    )
    loss_part = jnp.broadcast_to(local_total / dp, (dp, 1))
    parts = jnp.concatenate([down_part, head_part, loss_part], axis=1)
    n_down = down_part.shape[1]
    n_head = head_part.shape[1]
    padded = -(-parts.shape[1] // 128) * 128
    parts = jnp.pad(parts, ((0, 0), (0, padded - parts.shape[1]))).reshape(dp, 1, padded)
    query_back = jnp.einsum(
        "pc,dc->pd",
        after(d_query_pre.astype(jnp.bfloat16), parts),
        query_full,
        preferred_element_type=jnp.float32,
    )
    query_back_all = ring_parts(query_back)
    reduced = jnp.sum(lax.all_to_all(parts, DP, 0, 0, tiled=True), axis=0)
    totals = spread(reduced, (*DP, "mp")).reshape(dp, mp, padded)
    grad_down = (
        totals[:, :, :n_down]
        .reshape(2 * rank, dp // (2 * rank), mp, n_down)
        .transpose(0, 2, 1, 3)
        .reshape(2 * rank, width)
    )
    grad_down_query = grad_down[:rank].T
    grad_down_value = grad_down[rank:].T
    own = lax.dynamic_index_in_dim(totals, place, axis=1, keepdims=False)
    n_up_query = q_cols * rank // dp
    grad_up_query = own[:, n_down : n_down + n_up_query].reshape(rank, q_cols)
    grad_up_value = own[:, n_down + n_up_query : n_down + n_head].reshape(rank, kv_cols)
    loss = jnp.sum(totals[:, 0, n_down + n_head]) / total_pairs

    d_kv_own = [d_kv_own[0]] + [after(blocks, reduced) for blocks in d_kv_own[1:]]
    kv_groups = [weights[:, 2 * q_cols :]]
    kv_groups += [others[:, k * group_cols : (k + 1) * group_cols] for k in range(mp - 1)]
    x_local = lax.dynamic_slice_in_dim(layer_input, first_tok, tok_span, 1).astype(jnp.float32)
    rms_local = lax.dynamic_slice_in_dim(inv_rms, first_tok, tok_span, 1)
    du_local = lax.dynamic_slice_in_dim(
        du_value.reshape(rank, pass_dev, seq_len), first_tok, tok_span, 2
    )
    tok_ids = first_tok + lax.iota(jnp.int32, tok_span)
    at_local = (tok_ids[None, :] == last_pos[:, None])[:, :, None]
    d_normed = jnp.einsum(
        "rpt,dr->ptd", du_local, down_value, preferred_element_type=jnp.float32
    )
    query_adapter = jnp.einsum(
        "rp,dr->pd", du_query, down_query, preferred_element_type=jnp.float32
    )
    d_normed = d_normed + jnp.where(at_local, query_adapter[:, None, :], 0.0)
    for group in range(mp):
        term = jnp.einsum(
            "ptc,dc->ptd",
            d_kv_own[group],
            kv_groups[group],
            preferred_element_type=jnp.float32,
        )
        term = term + jnp.where(at_local, query_back_all[group][:, None, :], 0.0)
        d_normed = d_normed + term.astype(jnp.bfloat16).astype(jnp.float32)
    d_input = gain_in * d_normed * rms_local - x_local * rms_local**3 * jnp.mean(
        x_local * gain_in * d_normed, axis=-1, keepdims=True
    )
    d_input = d_input + jnp.where(at_local, d_hidden[:, None, :], 0.0)
    grad_input = d_input.astype(jnp.bfloat16)
    return (
        loss,
        embed_grads[0],
        embed_grads[1],
        embed_grads[2],
        grad_input,
        grad_down_query,
        grad_up_query,
        grad_down_value,
        grad_up_value,
    )


def solution(mesh):
    staged = Mesh(mesh.devices.reshape(4, 4, 2, 2, 4), (*DP, "mp"))
    in_specs = (
        P(DP, "mp"),
        P(DP, "mp"),
        P(DP, "mp"),
        P(DP),
        P(DP, None, None),
        P(DP),
        P(),
        P(),
        P(DP, "mp"),
        P(DP, "mp"),
        P(DP, "mp"),
        P("mp", DP),
        P(),
        P(None, "mp"),
        P(),
        P(None, "mp"),
    )
    out_specs = (
        P(),
        P(DP, "mp"),
        P(DP, "mp"),
        P(DP, "mp"),
        P(DP, "mp", None),
        P(),
        P(None, "mp"),
        P(),
        P(None, "mp"),
    )
    return jax.shard_map(
        on_device, mesh=staged, in_specs=in_specs, out_specs=out_specs, check_vma=False
    )
```

```python
import jax
import jax.numpy as jnp
from jax import lax
from jax.sharding import Mesh
from jax.sharding import PartitionSpec as P

HD = 128
DP = ("y", "x", "zh", "core")


EPSILON = 1e-05
SOFTMAX_TEMPER = 0.01
ADAPTER_SCALE = 2.0
ROPE_BASE = 10000.0
MATMUL_ACCURACY = lax.Precision.HIGHEST


def angle_table(seq_len, head_dim):
    half_dim = head_dim // 2
    frequency = ROPE_BASE ** (-(jnp.arange(half_dim, dtype=jnp.float32) * 2.0 / head_dim))
    angles = jnp.arange(seq_len, dtype=jnp.float32)[:, None] * frequency[None, :]
    return (jnp.cos(angles), jnp.sin(angles))


def rotate(field, cosine, sine):
    half_dim = field.shape[-1] // 2
    leading = field[..., :half_dim]
    trailing = field[..., half_dim:]
    return jnp.concatenate(
        [leading * cosine - trailing * sine, trailing * cosine + leading * sine], axis=-1
    )


def shifted(value, axis_name, shift):
    size = lax.axis_size(axis_name)
    return lax.ppermute(value, axis_name, [(i, (i + shift) % size) for i in range(size)])


def ring_sum(value):
    one, two, three = (shifted(value, "mp", k) for k in (1, 2, 3))
    return (value + two) + (one + three)


def ring_parts(value):
    return [value] + [shifted(value, "mp", k) for k in (1, 2, 3)]


def ring_gather(value):
    parts = jnp.stack(ring_parts(value))
    place = lax.axis_index("mp")
    order = (place - lax.iota(jnp.int32, 4)) % 4
    return jnp.take(parts, order, axis=0)


def spread(value, axis_name):
    size = lax.axis_size(axis_name)
    return lax.all_to_all(
        jnp.broadcast_to(value[None], (size,) + value.shape), axis_name, 0, 0, tiled=True
    )


def pair_gather(value, axis_name):
    other = lax.ppermute(value, axis_name, [(0, 1), (1, 0)])
    at_first = lax.axis_index(axis_name) == 0
    return jnp.stack([jnp.where(at_first, value, other), jnp.where(at_first, other, value)])


def after(value, *first):
    return lax.optimization_barrier((value, *first))[0]


def core_halves(value):
    half = value.shape[1] // 2
    at_first = lax.axis_index("core") == 0
    left, right = value[:, :half], value[:, half:]
    kept = jnp.where(at_first, left, right)
    other = lax.ppermute(jnp.where(at_first, right, left), "core", [(0, 1), (1, 0)])
    return jnp.stack([jnp.where(at_first, kept, other), jnp.where(at_first, other, kept)])


def gather_rows(shard, *first):
    pair = pair_gather(shard, "core").reshape(2 * shard.shape[0], shard.shape[1])
    pair = after(pair, *first)
    moved = lax.ppermute(pair, ("zh", "core"), [(0, 2), (3, 1)])
    pair = jnp.where(lax.axis_index("zh") == lax.axis_index("core"), pair, moved)
    return lax.all_gather(pair, ("y", "x", "core"), axis=0, tiled=True)


def on_device(
    queries,
    passages,
    negatives,
    hard_index,
    layer_input,
    lengths,
    in_gain,
    out_gain,
    w_query,
    w_key,
    w_value,
    w_out,
    down_query,
    query_up_weight,
    down_value,
    value_up_weight,
):
    dp = lax.axis_size(DP)
    mp = lax.axis_size("mp")
    place = lax.axis_index("mp")
    pairs_dev, feature_dev = queries.shape
    total_pairs = pairs_dev * dp
    pass_dev, seq_len, width = layer_input.shape
    kv_cols = w_key.shape[1]
    q_cols = w_query.shape[1]
    group_cols = 2 * kv_cols

    half = feature_dev // 2
    span = 3 * pairs_dev
    first_core = lax.axis_index("core") == 0
    embeds = jnp.stack([queries, passages, negatives])
    by_core = core_halves(embeds.reshape(span, feature_dev))
    by_chip = pair_gather(by_core, "zh")
    layer_input = after(layer_input, by_chip)
    mine = spread(by_chip, ("y", "x")).reshape(dp * span, half)
    theirs = lax.ppermute(mine, "core", [(0, 1), (1, 0)])

    kv_shards = ring_parts(jnp.concatenate([w_key, w_value], axis=1))
    query_kv = gather_rows(jnp.concatenate([w_query, kv_shards[0]], axis=1), by_core)
    query_full, kv_own = query_kv[:, :q_cols], query_kv[:, q_cols:]
    out_t = gather_rows(w_out.T, by_chip)
    others = gather_rows(jnp.concatenate(kv_shards[1:], axis=1), mine)

    raw_halves = [rows.astype(jnp.float32) for rows in (mine, theirs)]
    square_sums = ring_sum(sum(jnp.sum(rows * rows, axis=1) for rows in raw_halves))
    all_len = jnp.sqrt(square_sums)
    embed_halves = [(rows / all_len[:, None]).astype(jnp.bfloat16) for rows in raw_halves]
    embed_len = lax.dynamic_slice_in_dim(all_len, lax.axis_index(DP) * span, span)
    embed_len = embed_len.reshape(3, pairs_dev, 1)
    units = embeds.astype(jnp.float32) / embed_len
    query_round = units[0].astype(jnp.bfloat16)

    def in_order(own, partner):
        left = jnp.where(first_core, own, partner)
        right = jnp.where(first_core, partner, own)
        return jnp.concatenate([left, right], axis=1)

    left, right = query_round[:, :half], query_round[:, half:]
    query_halves = [jnp.where(first_core, left, right), jnp.where(first_core, right, left)]
    score_part = sum(
        jnp.einsum("id,jd->ij", query, rows, preferred_element_type=jnp.float32)
        for query, rows in zip(query_halves, embed_halves)
    )
    scores = ring_sum(score_part) / SOFTMAX_TEMPER
    column = lax.iota(jnp.int32, dp * span)[None, :]
    is_passage = (column % span) // pairs_dev == 1
    own_ids = lax.iota(jnp.int32, pairs_dev)
    is_label = column == lax.axis_index(DP) * span + pairs_dev + own_ids[:, None]
    hard_column = (hard_index // pairs_dev) * span + 2 * pairs_dev + hard_index % pairs_dev
    is_candidate = is_passage | (column == hard_column[:, None])
    masked = jnp.where(is_candidate, scores, -jnp.inf)
    row_top = jnp.max(masked, axis=1)
    exps = jnp.exp(masked - row_top[:, None])
    exp_total = jnp.sum(exps, axis=1)
    per_query = row_top + jnp.log(exp_total) - jnp.sum(jnp.where(is_label, scores, 0.0), axis=1)
    local_total = jnp.sum(per_query)
    score_gradient = (
        (exps / exp_total[:, None] - is_label.astype(jnp.float32)) / SOFTMAX_TEMPER
    ).astype(jnp.bfloat16)
    by_owner = score_gradient.reshape(pairs_dev, dp, span).transpose(1, 0, 2)
    own_columns = lax.all_to_all(by_owner, DP, 0, 0, tiled=True)

    gain_in = in_gain.astype(jnp.float32)
    gain_out = out_gain.astype(jnp.float32)
    x_float = layer_input.astype(jnp.float32)
    inv_rms = lax.rsqrt(jnp.mean(x_float * x_float, axis=-1, keepdims=True) + EPSILON)
    normed = (x_float * inv_rms * gain_in).astype(jnp.bfloat16)
    last_pos = lengths - 1
    n_last = jnp.take_along_axis(normed, last_pos[:, None, None], axis=1)[:, 0]
    x_last = jnp.take_along_axis(layer_input, last_pos[:, None, None], axis=1)[:, 0].astype(
        jnp.float32
    )
    value_lowrank = jnp.einsum(
        "pld,dr->plr", normed, down_value, preferred_element_type=jnp.float32
    ).astype(jnp.bfloat16)
    query_lowrank = jnp.dot(n_last, down_query, preferred_element_type=jnp.float32).astype(
        jnp.bfloat16
    )
    group_size = q_cols // kv_cols
    score_scale = HD ** (-0.5)
    cosine, sine = angle_table(seq_len, HD)
    kv_pre = jnp.einsum("pld,dc->plc", normed, kv_own, preferred_element_type=jnp.float32)
    value_rows = (
        kv_pre[:, :, kv_cols:]
        + ADAPTER_SCALE
        * jnp.einsum(
            "plr,rc->plc", value_lowrank, value_up_weight, preferred_element_type=jnp.float32
        )
    ).astype(jnp.bfloat16)
    key_rows = rotate(kv_pre[:, :, :kv_cols], cosine[None], sine[None]).astype(jnp.bfloat16)
    query_before_rotation = jnp.dot(
        n_last, query_full, preferred_element_type=jnp.float32
    ) + ADAPTER_SCALE * jnp.dot(
        query_lowrank, query_up_weight, preferred_element_type=jnp.float32
    )
    cos_last = cosine[last_pos][:, None, :]
    sin_last = sine[last_pos][:, None, :]
    query_rot = rotate(
        query_before_rotation.reshape(pass_dev, group_size, HD), cos_last, sin_last
    ).astype(jnp.bfloat16)
    logits = (
        jnp.einsum("pgd,pld->pgl", query_rot, key_rows, preferred_element_type=jnp.float32)
        * score_scale
    )
    visible = lax.iota(jnp.int32, seq_len)[None, :] <= last_pos[:, None]
    logits = jnp.where(visible[:, None, :], logits, -1e30)
    row_peak = jnp.max(logits, axis=-1, keepdims=True)
    exponent_att = jnp.exp(logits - row_peak)
    attention = exponent_att / jnp.sum(exponent_att, axis=-1, keepdims=True)
    attention_round = attention.astype(jnp.bfloat16)
    mixed_heads = (
        jnp.einsum("pgl,pld->pgd", attention_round, value_rows, preferred_element_type=jnp.float32)
        .astype(jnp.bfloat16)
        .reshape(pass_dev, q_cols)
    )

    passage_unit = ring_gather(after(units[1, :pass_dev], mixed_heads))
    passage_unit = passage_unit.transpose(1, 0, 2).reshape(pass_dev, width)
    own_columns = jnp.pad(after(own_columns, mixed_heads), ((0, 0), (0, span - pairs_dev), (0, 0)))
    own_columns = own_columns.reshape(dp * span, span)
    query_grad = in_order(
        *[
            jnp.einsum("ij,jd->id", score_gradient, rows, preferred_element_type=jnp.float32)
            for rows in embed_halves
        ]
    )
    both_grads = in_order(
        *[
            jnp.einsum("jc,jd->cd", own_columns, rows, preferred_element_type=jnp.float32)
            for rows in embed_halves
        ]
    )
    passage_grad = both_grads[pairs_dev : pairs_dev + pass_dev]
    passage_grad = ring_gather(passage_grad).transpose(1, 0, 2).reshape(pass_dev, width)
    passage_inner = jnp.sum(passage_grad * passage_unit, axis=1, keepdims=True)
    cotangent = (passage_grad - passage_inner * passage_unit) / embed_len[1, :pass_dev]

    out_part = jnp.einsum("pc,dc->pd", mixed_heads, out_t, preferred_element_type=jnp.float32)
    hidden = x_last + ring_sum(out_part)

    inv_hidden = lax.rsqrt(jnp.mean(hidden * hidden, axis=-1, keepdims=True) + EPSILON)
    scaled = gain_out * cotangent
    d_hidden = scaled * inv_hidden - hidden * inv_hidden**3 * jnp.mean(
        hidden * scaled, axis=-1, keepdims=True
    )
    d_mixed = jnp.dot(
        d_hidden.astype(jnp.bfloat16), out_t, preferred_element_type=jnp.float32
    ).reshape(pass_dev, group_size, HD)
    value_float = value_rows.astype(jnp.float32)
    key_float = key_rows.astype(jnp.float32)
    d_attention = jnp.einsum("pgd,pld->pgl", d_mixed, value_float, precision=MATMUL_ACCURACY)
    d_logits = attention * (d_attention - jnp.sum(attention * d_attention, axis=-1, keepdims=True))
    d_values = jnp.einsum(
        "pgl,pgd->pld", attention_round.astype(jnp.float32), d_mixed, precision=MATMUL_ACCURACY
    )
    d_query = (
        jnp.einsum("pgl,pld->pgd", d_logits, key_float, precision=MATMUL_ACCURACY) * score_scale
    )
    d_keys = (
        jnp.einsum(
            "pgl,pgd->pld", d_logits, query_rot.astype(jnp.float32), precision=MATMUL_ACCURACY
        )
        * score_scale
    )
    d_query_pre = rotate(d_query, cos_last, -sin_last).reshape(pass_dev, q_cols)
    d_keys_pre = rotate(d_keys, cosine[None], -sine[None])

    tok_span = seq_len // mp
    first_tok = place * tok_span
    d_kv = jnp.concatenate([d_keys_pre, d_values], axis=2).astype(jnp.bfloat16)
    d_kv = d_kv.reshape(pass_dev, mp, tok_span, group_cols)
    d_kv_own = [
        lax.dynamic_index_in_dim(d_kv, (place + k) % mp, axis=1, keepdims=False) for k in range(mp)
    ]
    d_kv_own = [d_kv_own[0]] + [shifted(d_kv_own[k], "mp", k) for k in range(1, mp)]
    du_query_part = jnp.einsum(
        "rc,pc->rp",
        query_up_weight.astype(jnp.float32),
        d_query_pre,
        precision=MATMUL_ACCURACY,
    )
    du_value_part = jnp.einsum(
        "rc,nc->rn",
        value_up_weight.astype(jnp.float32),
        d_values.reshape(pass_dev * seq_len, kv_cols),
        precision=MATMUL_ACCURACY,
    )
    du_parts = jnp.pad(
        jnp.concatenate([du_value_part, du_query_part], axis=1), ((0, 0), (0, 128 - pass_dev))
    )
    du = (ADAPTER_SCALE * ring_sum(du_parts)).astype(jnp.bfloat16)
    rank = du.shape[0]
    n_tokens = pass_dev * seq_len
    du_value = du[:, :n_tokens]
    du_query = du[:, n_tokens : n_tokens + pass_dev]
    up_query_part = ADAPTER_SCALE * jnp.einsum(
        "pr,pc->rc", query_lowrank.astype(jnp.float32), d_query_pre, precision=MATMUL_ACCURACY
    )
    up_value_part = ADAPTER_SCALE * jnp.einsum(
        "plr,plc->rc", value_lowrank.astype(jnp.float32), d_values, precision=MATMUL_ACCURACY
    )

    quarter = width // mp
    first_feature = place * quarter
    normed_quarter = lax.dynamic_slice_in_dim(
        normed.reshape(n_tokens, width), first_feature, quarter, 1
    )
    last_quarter = lax.dynamic_slice_in_dim(n_last, first_feature, quarter, 1)
    down_value_part = jnp.einsum(
        "rn,nd->rd", du_value, normed_quarter, preferred_element_type=jnp.float32
    )
    down_query_part = jnp.einsum(
        "rp,pd->rd", du_query, last_quarter, preferred_element_type=jnp.float32
    )
    down_part = jnp.concatenate([down_query_part, down_value_part], axis=0).reshape(dp, -1)
    head_part = jnp.concatenate(
        [up_query_part.reshape(dp, -1), up_value_part.reshape(dp, -1)], axis=1
    )
    loss_part = jnp.broadcast_to(local_total / dp, (dp, 1))
    parts = jnp.concatenate([down_part, head_part, loss_part], axis=1)
    n_down = down_part.shape[1]
    n_head = head_part.shape[1]
    padded = -(-parts.shape[1] // 128) * 128
    parts = jnp.pad(parts, ((0, 0), (0, padded - parts.shape[1]))).reshape(dp, 1, padded)
    grads = jnp.concatenate([query_grad, both_grads[pairs_dev:]], axis=0).reshape(units.shape)
    grads = after(grads, parts)
    inner_sums = ring_sum(jnp.sum(grads * units, axis=2))[:, :, None]
    embed_grads = (grads - inner_sums * units) / embed_len
    query_back = jnp.einsum(
        "pc,dc->pd",
        after(d_query_pre.astype(jnp.bfloat16), parts),
        query_full,
        preferred_element_type=jnp.float32,
    )
    query_back_all = ring_parts(query_back)
    reduced = jnp.sum(lax.all_to_all(parts, DP, 0, 0, tiled=True), axis=0)
    totals = spread(reduced, (*DP, "mp")).reshape(dp, mp, padded)
    grad_down = (
        totals[:, :, :n_down]
        .reshape(2 * rank, dp // (2 * rank), mp, n_down)
        .transpose(0, 2, 1, 3)
        .reshape(2 * rank, width)
    )
    grad_down_query = grad_down[:rank].T
    grad_down_value = grad_down[rank:].T
    own = lax.dynamic_index_in_dim(totals, place, axis=1, keepdims=False)
    n_up_query = q_cols * rank // dp
    grad_up_query = own[:, n_down : n_down + n_up_query].reshape(rank, q_cols)
    grad_up_value = own[:, n_down + n_up_query : n_down + n_head].reshape(rank, kv_cols)
    loss = jnp.sum(totals[:, 0, n_down + n_head]) / total_pairs

    d_kv_own = [d_kv_own[0]] + [after(blocks, reduced) for blocks in d_kv_own[1:]]
    kv_groups = [kv_own]
    kv_groups += [others[:, k * group_cols : (k + 1) * group_cols] for k in range(mp - 1)]
    x_local = lax.dynamic_slice_in_dim(layer_input, first_tok, tok_span, 1).astype(jnp.float32)
    rms_local = lax.dynamic_slice_in_dim(inv_rms, first_tok, tok_span, 1)
    du_local = lax.dynamic_slice_in_dim(
        du_value.reshape(rank, pass_dev, seq_len), first_tok, tok_span, 2
    )
    tok_ids = first_tok + lax.iota(jnp.int32, tok_span)
    at_local = (tok_ids[None, :] == last_pos[:, None])[:, :, None]
    d_normed = jnp.einsum(
        "rpt,dr->ptd", du_local, down_value, preferred_element_type=jnp.float32
    )
    query_adapter = jnp.einsum(
        "rp,dr->pd", du_query, down_query, preferred_element_type=jnp.float32
    )
    d_normed = d_normed + jnp.where(at_local, query_adapter[:, None, :], 0.0)
    for group in range(mp):
        term = jnp.einsum(
            "ptc,dc->ptd",
            d_kv_own[group],
            kv_groups[group],
            preferred_element_type=jnp.float32,
        )
        term = term + jnp.where(at_local, query_back_all[group][:, None, :], 0.0)
        d_normed = d_normed + term.astype(jnp.bfloat16).astype(jnp.float32)
    d_input = gain_in * d_normed * rms_local - x_local * rms_local**3 * jnp.mean(
        x_local * gain_in * d_normed, axis=-1, keepdims=True
    )
    d_input = d_input + jnp.where(at_local, d_hidden[:, None, :], 0.0)
    grad_input = d_input.astype(jnp.bfloat16)
    return (
        loss,
        embed_grads[0],
        embed_grads[1],
        embed_grads[2],
        grad_input,
        grad_down_query,
        grad_up_query,
        grad_down_value,
        grad_up_value,
    )


def solution(mesh):
    staged = Mesh(mesh.devices.reshape(4, 4, 2, 2, 4), (*DP, "mp"))
    in_specs = (
        P(DP, "mp"),
        P(DP, "mp"),
        P(DP, "mp"),
        P(DP),
        P(DP, None, None),
        P(DP),
        P(),
        P(),
        P(DP, "mp"),
        P(DP, "mp"),
        P(DP, "mp"),
        P("mp", DP),
        P(),
        P(None, "mp"),
        P(),
        P(None, "mp"),
    )
    out_specs = (
        P(),
        P(DP, "mp"),
        P(DP, "mp"),
        P(DP, "mp"),
        P(DP, "mp", None),
        P(),
        P(None, "mp"),
        P(),
        P(None, "mp"),
    )
    return jax.shard_map(
        on_device, mesh=staged, in_specs=in_specs, out_specs=out_specs, check_vma=False
    )
```

```python
import jax
import jax.numpy as jnp
from jax import lax
from jax.sharding import Mesh
from jax.sharding import PartitionSpec as P

HD = 128
DP = ("y", "x", "zh", "core")


EPSILON = 1e-05
SOFTMAX_TEMPER = 0.01
ADAPTER_SCALE = 2.0
ROPE_BASE = 10000.0
MATMUL_ACCURACY = lax.Precision.HIGHEST


def angle_table(seq_len, head_dim):
    half_dim = head_dim // 2
    frequency = ROPE_BASE ** (-(jnp.arange(half_dim, dtype=jnp.float32) * 2.0 / head_dim))
    angles = jnp.arange(seq_len, dtype=jnp.float32)[:, None] * frequency[None, :]
    return (jnp.cos(angles), jnp.sin(angles))


def rotate(field, cosine, sine):
    half_dim = field.shape[-1] // 2
    leading = field[..., :half_dim]
    trailing = field[..., half_dim:]
    return jnp.concatenate(
        [leading * cosine - trailing * sine, trailing * cosine + leading * sine], axis=-1
    )


def shifted(value, axis_name, shift):
    size = lax.axis_size(axis_name)
    return lax.ppermute(value, axis_name, [(i, (i + shift) % size) for i in range(size)])


def ring_sum(value):
    one, two, three = (shifted(value, "mp", k) for k in (1, 2, 3))
    return (value + two) + (one + three)


def ring_parts(value):
    return [value] + [shifted(value, "mp", k) for k in (1, 2, 3)]


def ring_gather(value):
    parts = jnp.stack(ring_parts(value))
    place = lax.axis_index("mp")
    order = (place - lax.iota(jnp.int32, 4)) % 4
    return jnp.take(parts, order, axis=0)


def spread(value, axis_name):
    size = lax.axis_size(axis_name)
    return lax.all_to_all(
        jnp.broadcast_to(value[None], (size,) + value.shape), axis_name, 0, 0, tiled=True
    )


def pair_gather(value, axis_name):
    other = lax.ppermute(value, axis_name, [(0, 1), (1, 0)])
    at_first = lax.axis_index(axis_name) == 0
    return jnp.stack([jnp.where(at_first, value, other), jnp.where(at_first, other, value)])


def after(value, *first):
    return lax.optimization_barrier((value, *first))[0]


def core_halves(value):
    half = value.shape[1] // 2
    at_first = lax.axis_index("core") == 0
    left, right = value[:, :half], value[:, half:]
    kept = jnp.where(at_first, left, right)
    other = lax.ppermute(jnp.where(at_first, right, left), "core", [(0, 1), (1, 0)])
    return jnp.stack([jnp.where(at_first, kept, other), jnp.where(at_first, other, kept)])


def chip_pairs(shard):
    pair = pair_gather(shard, "core").reshape(2 * shard.shape[0], shard.shape[1])
    moved = lax.ppermute(pair, ("zh", "core"), [(0, 2), (3, 1)])
    return jnp.where(lax.axis_index("zh") == lax.axis_index("core"), pair, moved)


def gather_rows(pair, *first):
    return lax.all_gather(after(pair, *first), ("y", "x", "core"), axis=0, tiled=True)


def on_device(
    queries,
    passages,
    negatives,
    hard_index,
    layer_input,
    lengths,
    in_gain,
    out_gain,
    w_query,
    w_key,
    w_value,
    w_out,
    down_query,
    query_up_weight,
    down_value,
    value_up_weight,
):
    dp = lax.axis_size(DP)
    mp = lax.axis_size("mp")
    place = lax.axis_index("mp")
    pairs_dev, feature_dev = queries.shape
    total_pairs = pairs_dev * dp
    pass_dev, seq_len, width = layer_input.shape
    kv_cols = w_key.shape[1]
    q_cols = w_query.shape[1]
    group_cols = 2 * kv_cols

    half = feature_dev // 2
    span = 3 * pairs_dev
    first_core = lax.axis_index("core") == 0
    embeds = jnp.stack([queries, passages, negatives])
    by_core = core_halves(embeds.reshape(span, feature_dev))
    by_chip = pair_gather(by_core, "zh")
    layer_input = after(layer_input, by_chip)
    mine = spread(by_chip, ("y", "x")).reshape(dp * span, half)
    theirs = lax.ppermute(mine, "core", [(0, 1), (1, 0)])

    kv_shards = ring_parts(jnp.concatenate([w_key, w_value], axis=1))
    pairs = chip_pairs(jnp.concatenate([w_query, kv_shards[0], w_out.T], axis=1))
    other_pairs = chip_pairs(after(jnp.concatenate(kv_shards[1:], axis=1), by_chip))
    first_cols = q_cols + group_cols
    query_kv = gather_rows(pairs[:, :first_cols], mine)
    query_full, kv_own = query_kv[:, :q_cols], query_kv[:, q_cols:]
    out_t = gather_rows(pairs[:, first_cols:], mine)
    others = gather_rows(other_pairs, mine, pairs)

    raw_halves = [rows.astype(jnp.float32) for rows in (mine, theirs)]
    square_sums = ring_sum(sum(jnp.sum(rows * rows, axis=1) for rows in raw_halves))
    all_len = jnp.sqrt(square_sums)
    embed_halves = [(rows / all_len[:, None]).astype(jnp.bfloat16) for rows in raw_halves]
    embed_len = lax.dynamic_slice_in_dim(all_len, lax.axis_index(DP) * span, span)
    embed_len = embed_len.reshape(3, pairs_dev, 1)
    units = embeds.astype(jnp.float32) / embed_len
    query_round = units[0].astype(jnp.bfloat16)

    def in_order(own, partner):
        left = jnp.where(first_core, own, partner)
        right = jnp.where(first_core, partner, own)
        return jnp.concatenate([left, right], axis=1)

    left, right = query_round[:, :half], query_round[:, half:]
    query_halves = [jnp.where(first_core, left, right), jnp.where(first_core, right, left)]
    score_part = sum(
        jnp.einsum("id,jd->ij", query, rows, preferred_element_type=jnp.float32)
        for query, rows in zip(query_halves, embed_halves)
    )
    scores = ring_sum(score_part) / SOFTMAX_TEMPER
    column = lax.iota(jnp.int32, dp * span)[None, :]
    is_passage = (column % span) // pairs_dev == 1
    own_ids = lax.iota(jnp.int32, pairs_dev)
    is_label = column == lax.axis_index(DP) * span + pairs_dev + own_ids[:, None]
    hard_column = (hard_index // pairs_dev) * span + 2 * pairs_dev + hard_index % pairs_dev
    is_candidate = is_passage | (column == hard_column[:, None])
    masked = jnp.where(is_candidate, scores, -jnp.inf)
    row_top = jnp.max(masked, axis=1)
    exps = jnp.exp(masked - row_top[:, None])
    exp_total = jnp.sum(exps, axis=1)
    per_query = row_top + jnp.log(exp_total) - jnp.sum(jnp.where(is_label, scores, 0.0), axis=1)
    local_total = jnp.sum(per_query)
    score_gradient = (
        (exps / exp_total[:, None] - is_label.astype(jnp.float32)) / SOFTMAX_TEMPER
    ).astype(jnp.bfloat16)
    by_owner = score_gradient.reshape(pairs_dev, dp, span).transpose(1, 0, 2)
    own_columns = lax.all_to_all(by_owner, DP, 0, 0, tiled=True)

    gain_in = in_gain.astype(jnp.float32)
    gain_out = out_gain.astype(jnp.float32)
    x_float = layer_input.astype(jnp.float32)
    inv_rms = lax.rsqrt(jnp.mean(x_float * x_float, axis=-1, keepdims=True) + EPSILON)
    normed = (x_float * inv_rms * gain_in).astype(jnp.bfloat16)
    last_pos = lengths - 1
    n_last = jnp.take_along_axis(normed, last_pos[:, None, None], axis=1)[:, 0]
    x_last = jnp.take_along_axis(layer_input, last_pos[:, None, None], axis=1)[:, 0].astype(
        jnp.float32
    )
    value_lowrank = jnp.einsum(
        "pld,dr->plr", normed, down_value, preferred_element_type=jnp.float32
    ).astype(jnp.bfloat16)
    query_lowrank = jnp.dot(n_last, down_query, preferred_element_type=jnp.float32).astype(
        jnp.bfloat16
    )
    group_size = q_cols // kv_cols
    score_scale = HD ** (-0.5)
    cosine, sine = angle_table(seq_len, HD)
    kv_pre = jnp.einsum("pld,dc->plc", normed, kv_own, preferred_element_type=jnp.float32)
    value_rows = (
        kv_pre[:, :, kv_cols:]
        + ADAPTER_SCALE
        * jnp.einsum(
            "plr,rc->plc", value_lowrank, value_up_weight, preferred_element_type=jnp.float32
        )
    ).astype(jnp.bfloat16)
    key_rows = rotate(kv_pre[:, :, :kv_cols], cosine[None], sine[None]).astype(jnp.bfloat16)
    query_before_rotation = jnp.dot(
        n_last, query_full, preferred_element_type=jnp.float32
    ) + ADAPTER_SCALE * jnp.dot(
        query_lowrank, query_up_weight, preferred_element_type=jnp.float32
    )
    cos_last = cosine[last_pos][:, None, :]
    sin_last = sine[last_pos][:, None, :]
    query_rot = rotate(
        query_before_rotation.reshape(pass_dev, group_size, HD), cos_last, sin_last
    ).astype(jnp.bfloat16)
    logits = (
        jnp.einsum("pgd,pld->pgl", query_rot, key_rows, preferred_element_type=jnp.float32)
        * score_scale
    )
    visible = lax.iota(jnp.int32, seq_len)[None, :] <= last_pos[:, None]
    logits = jnp.where(visible[:, None, :], logits, -1e30)
    row_peak = jnp.max(logits, axis=-1, keepdims=True)
    exponent_att = jnp.exp(logits - row_peak)
    attention = exponent_att / jnp.sum(exponent_att, axis=-1, keepdims=True)
    attention_round = attention.astype(jnp.bfloat16)
    mixed_heads = (
        jnp.einsum("pgl,pld->pgd", attention_round, value_rows, preferred_element_type=jnp.float32)
        .astype(jnp.bfloat16)
        .reshape(pass_dev, q_cols)
    )

    passage_unit = ring_gather(after(units[1, :pass_dev], mixed_heads))
    passage_unit = passage_unit.transpose(1, 0, 2).reshape(pass_dev, width)
    own_columns = jnp.pad(after(own_columns, mixed_heads), ((0, 0), (0, span - pairs_dev), (0, 0)))
    own_columns = own_columns.reshape(dp * span, span)
    query_grad = in_order(
        *[
            jnp.einsum("ij,jd->id", score_gradient, rows, preferred_element_type=jnp.float32)
            for rows in embed_halves
        ]
    )
    both_grads = in_order(
        *[
            jnp.einsum("jc,jd->cd", own_columns, rows, preferred_element_type=jnp.float32)
            for rows in embed_halves
        ]
    )
    passage_grad = both_grads[pairs_dev : pairs_dev + pass_dev]
    passage_grad = ring_gather(passage_grad).transpose(1, 0, 2).reshape(pass_dev, width)
    passage_inner = jnp.sum(passage_grad * passage_unit, axis=1, keepdims=True)
    cotangent = (passage_grad - passage_inner * passage_unit) / embed_len[1, :pass_dev]

    out_part = jnp.einsum("pc,dc->pd", mixed_heads, out_t, preferred_element_type=jnp.float32)
    hidden = x_last + ring_sum(out_part)

    inv_hidden = lax.rsqrt(jnp.mean(hidden * hidden, axis=-1, keepdims=True) + EPSILON)
    scaled = gain_out * cotangent
    d_hidden = scaled * inv_hidden - hidden * inv_hidden**3 * jnp.mean(
        hidden * scaled, axis=-1, keepdims=True
    )
    d_mixed = jnp.dot(
        d_hidden.astype(jnp.bfloat16), out_t, preferred_element_type=jnp.float32
    ).reshape(pass_dev, group_size, HD)
    value_float = value_rows.astype(jnp.float32)
    key_float = key_rows.astype(jnp.float32)
    d_attention = jnp.einsum("pgd,pld->pgl", d_mixed, value_float, precision=MATMUL_ACCURACY)
    d_logits = attention * (d_attention - jnp.sum(attention * d_attention, axis=-1, keepdims=True))
    d_values = jnp.einsum(
        "pgl,pgd->pld", attention_round.astype(jnp.float32), d_mixed, precision=MATMUL_ACCURACY
    )
    d_query = (
        jnp.einsum("pgl,pld->pgd", d_logits, key_float, precision=MATMUL_ACCURACY) * score_scale
    )
    d_keys = (
        jnp.einsum(
            "pgl,pgd->pld", d_logits, query_rot.astype(jnp.float32), precision=MATMUL_ACCURACY
        )
        * score_scale
    )
    d_query_pre = rotate(d_query, cos_last, -sin_last).reshape(pass_dev, q_cols)
    d_keys_pre = rotate(d_keys, cosine[None], -sine[None])

    tok_span = seq_len // mp
    first_tok = place * tok_span
    d_kv = jnp.concatenate([d_keys_pre, d_values], axis=2).astype(jnp.bfloat16)
    d_kv = d_kv.reshape(pass_dev, mp, tok_span, group_cols)
    d_kv_own = [
        lax.dynamic_index_in_dim(d_kv, (place + k) % mp, axis=1, keepdims=False) for k in range(mp)
    ]
    d_kv_own = [d_kv_own[0]] + [shifted(d_kv_own[k], "mp", k) for k in range(1, mp)]
    du_query_part = jnp.einsum(
        "rc,pc->rp",
        query_up_weight.astype(jnp.float32),
        d_query_pre,
        precision=MATMUL_ACCURACY,
    )
    du_value_part = jnp.einsum(
        "rc,nc->rn",
        value_up_weight.astype(jnp.float32),
        d_values.reshape(pass_dev * seq_len, kv_cols),
        precision=MATMUL_ACCURACY,
    )
    du_parts = jnp.pad(
        jnp.concatenate([du_value_part, du_query_part], axis=1), ((0, 0), (0, 128 - pass_dev))
    )
    du = (ADAPTER_SCALE * ring_sum(du_parts)).astype(jnp.bfloat16)
    rank = du.shape[0]
    n_tokens = pass_dev * seq_len
    du_value = du[:, :n_tokens]
    du_query = du[:, n_tokens : n_tokens + pass_dev]
    up_query_part = ADAPTER_SCALE * jnp.einsum(
        "pr,pc->rc", query_lowrank.astype(jnp.float32), d_query_pre, precision=MATMUL_ACCURACY
    )
    up_value_part = ADAPTER_SCALE * jnp.einsum(
        "plr,plc->rc", value_lowrank.astype(jnp.float32), d_values, precision=MATMUL_ACCURACY
    )

    quarter = width // mp
    first_feature = place * quarter
    normed_quarter = lax.dynamic_slice_in_dim(
        normed.reshape(n_tokens, width), first_feature, quarter, 1
    )
    last_quarter = lax.dynamic_slice_in_dim(n_last, first_feature, quarter, 1)
    down_value_part = jnp.einsum(
        "rn,nd->rd", du_value, normed_quarter, preferred_element_type=jnp.float32
    )
    down_query_part = jnp.einsum(
        "rp,pd->rd", du_query, last_quarter, preferred_element_type=jnp.float32
    )
    down_part = jnp.concatenate([down_query_part, down_value_part], axis=0).reshape(dp, -1)
    head_part = jnp.concatenate(
        [up_query_part.reshape(dp, -1), up_value_part.reshape(dp, -1)], axis=1
    )
    loss_part = jnp.broadcast_to(local_total / dp, (dp, 1))
    parts = jnp.concatenate([down_part, head_part, loss_part], axis=1)
    n_down = down_part.shape[1]
    n_head = head_part.shape[1]
    padded = -(-parts.shape[1] // 128) * 128
    parts = jnp.pad(parts, ((0, 0), (0, padded - parts.shape[1]))).reshape(dp, 1, padded)
    grads = jnp.concatenate([query_grad, both_grads[pairs_dev:]], axis=0).reshape(units.shape)
    grads = after(grads, parts)
    inner_sums = ring_sum(jnp.sum(grads * units, axis=2))[:, :, None]
    embed_grads = (grads - inner_sums * units) / embed_len
    query_back = jnp.einsum(
        "pc,dc->pd",
        after(d_query_pre.astype(jnp.bfloat16), parts),
        query_full,
        preferred_element_type=jnp.float32,
    )
    query_back_all = ring_parts(query_back)
    reduced = jnp.sum(lax.all_to_all(parts, DP, 0, 0, tiled=True), axis=0)
    totals = spread(reduced, (*DP, "mp")).reshape(dp, mp, padded)
    grad_down = (
        totals[:, :, :n_down]
        .reshape(2 * rank, dp // (2 * rank), mp, n_down)
        .transpose(0, 2, 1, 3)
        .reshape(2 * rank, width)
    )
    grad_down_query = grad_down[:rank].T
    grad_down_value = grad_down[rank:].T
    own = lax.dynamic_index_in_dim(totals, place, axis=1, keepdims=False)
    n_up_query = q_cols * rank // dp
    grad_up_query = own[:, n_down : n_down + n_up_query].reshape(rank, q_cols)
    grad_up_value = own[:, n_down + n_up_query : n_down + n_head].reshape(rank, kv_cols)
    loss = jnp.sum(totals[:, 0, n_down + n_head]) / total_pairs

    d_kv_own = [d_kv_own[0]] + [after(blocks, reduced) for blocks in d_kv_own[1:]]
    kv_groups = [kv_own]
    kv_groups += [others[:, k * group_cols : (k + 1) * group_cols] for k in range(mp - 1)]
    x_local = lax.dynamic_slice_in_dim(layer_input, first_tok, tok_span, 1).astype(jnp.float32)
    rms_local = lax.dynamic_slice_in_dim(inv_rms, first_tok, tok_span, 1)
    du_local = lax.dynamic_slice_in_dim(
        du_value.reshape(rank, pass_dev, seq_len), first_tok, tok_span, 2
    )
    tok_ids = first_tok + lax.iota(jnp.int32, tok_span)
    at_local = (tok_ids[None, :] == last_pos[:, None])[:, :, None]
    d_normed = jnp.einsum(
        "rpt,dr->ptd", du_local, down_value, preferred_element_type=jnp.float32
    )
    query_adapter = jnp.einsum(
        "rp,dr->pd", du_query, down_query, preferred_element_type=jnp.float32
    )
    d_normed = d_normed + jnp.where(at_local, query_adapter[:, None, :], 0.0)
    for group in range(mp):
        term = jnp.einsum(
            "ptc,dc->ptd",
            d_kv_own[group],
            kv_groups[group],
            preferred_element_type=jnp.float32,
        )
        term = term + jnp.where(at_local, query_back_all[group][:, None, :], 0.0)
        d_normed = d_normed + term.astype(jnp.bfloat16).astype(jnp.float32)
    d_input = gain_in * d_normed * rms_local - x_local * rms_local**3 * jnp.mean(
        x_local * gain_in * d_normed, axis=-1, keepdims=True
    )
    d_input = d_input + jnp.where(at_local, d_hidden[:, None, :], 0.0)
    grad_input = d_input.astype(jnp.bfloat16)
    return (
        loss,
        embed_grads[0],
        embed_grads[1],
        embed_grads[2],
        grad_input,
        grad_down_query,
        grad_up_query,
        grad_down_value,
        grad_up_value,
    )


def solution(mesh):
    staged = Mesh(mesh.devices.reshape(4, 4, 2, 2, 4), (*DP, "mp"))
    in_specs = (
        P(DP, "mp"),
        P(DP, "mp"),
        P(DP, "mp"),
        P(DP),
        P(DP, None, None),
        P(DP),
        P(),
        P(),
        P(DP, "mp"),
        P(DP, "mp"),
        P(DP, "mp"),
        P("mp", DP),
        P(),
        P(None, "mp"),
        P(),
        P(None, "mp"),
    )
    out_specs = (
        P(),
        P(DP, "mp"),
        P(DP, "mp"),
        P(DP, "mp"),
        P(DP, "mp", None),
        P(),
        P(None, "mp"),
        P(),
        P(None, "mp"),
    )
    return jax.shard_map(
        on_device, mesh=staged, in_specs=in_specs, out_specs=out_specs, check_vma=False
    )
```

```python
import jax
import jax.numpy as jnp
from jax import lax
from jax.sharding import Mesh
from jax.sharding import PartitionSpec as P

HD = 128
DP = ("y", "x", "zh", "core")


EPSILON = 1e-05
SOFTMAX_TEMPER = 0.01
ADAPTER_SCALE = 2.0
ROPE_BASE = 10000.0
MATMUL_ACCURACY = lax.Precision.HIGHEST


def angle_table(seq_len, head_dim):
    half_dim = head_dim // 2
    frequency = ROPE_BASE ** (-(jnp.arange(half_dim, dtype=jnp.float32) * 2.0 / head_dim))
    angles = jnp.arange(seq_len, dtype=jnp.float32)[:, None] * frequency[None, :]
    return (jnp.cos(angles), jnp.sin(angles))


def rotate(field, cosine, sine):
    half_dim = field.shape[-1] // 2
    leading = field[..., :half_dim]
    trailing = field[..., half_dim:]
    return jnp.concatenate(
        [leading * cosine - trailing * sine, trailing * cosine + leading * sine], axis=-1
    )


def shifted(value, axis_name, shift):
    size = lax.axis_size(axis_name)
    return lax.ppermute(value, axis_name, [(i, (i + shift) % size) for i in range(size)])


def ring_sum(value):
    one, two, three = (shifted(value, "mp", k) for k in (1, 2, 3))
    return (value + two) + (one + three)


def ring_parts(value):
    return [value] + [shifted(value, "mp", k) for k in (1, 2, 3)]


def ring_gather(value):
    parts = jnp.stack(ring_parts(value))
    place = lax.axis_index("mp")
    order = (place - lax.iota(jnp.int32, 4)) % 4
    return jnp.take(parts, order, axis=0)


def spread(value, axis_name):
    size = lax.axis_size(axis_name)
    return lax.all_to_all(
        jnp.broadcast_to(value[None], (size,) + value.shape), axis_name, 0, 0, tiled=True
    )


def pair_gather(value, axis_name):
    other = lax.ppermute(value, axis_name, [(0, 1), (1, 0)])
    at_first = lax.axis_index(axis_name) == 0
    return jnp.stack([jnp.where(at_first, value, other), jnp.where(at_first, other, value)])


def after(value, *first):
    return lax.optimization_barrier((value, *first))[0]


def core_halves(value):
    half = value.shape[1] // 2
    at_first = lax.axis_index("core") == 0
    left, right = value[:, :half], value[:, half:]
    kept = jnp.where(at_first, left, right)
    other = lax.ppermute(jnp.where(at_first, right, left), "core", [(0, 1), (1, 0)])
    return jnp.stack([jnp.where(at_first, kept, other), jnp.where(at_first, other, kept)])


def chip_pairs(shard):
    pair = pair_gather(shard, "core").reshape(2 * shard.shape[0], shard.shape[1])
    moved = lax.ppermute(pair, ("zh", "core"), [(0, 2), (3, 1)])
    return jnp.where(lax.axis_index("zh") == lax.axis_index("core"), pair, moved)


def gather_rows(pair, *first):
    return lax.all_gather(after(pair, *first), ("y", "x", "core"), axis=0, tiled=True)


def on_device(
    queries,
    passages,
    negatives,
    hard_index,
    layer_input,
    lengths,
    in_gain,
    out_gain,
    w_query,
    w_key,
    w_value,
    w_out,
    down_query,
    query_up_weight,
    down_value,
    value_up_weight,
):
    dp = lax.axis_size(DP)
    mp = lax.axis_size("mp")
    place = lax.axis_index("mp")
    pairs_dev, feature_dev = queries.shape
    total_pairs = pairs_dev * dp
    pass_dev, seq_len, width = layer_input.shape
    kv_cols = w_key.shape[1]
    q_cols = w_query.shape[1]
    group_cols = 2 * kv_cols

    half = feature_dev // 2
    span = 3 * pairs_dev
    first_core = lax.axis_index("core") == 0
    embeds = jnp.stack([queries, passages, negatives])
    by_core = core_halves(embeds.reshape(span, feature_dev))
    by_chip = pair_gather(by_core, "zh")
    mine = spread(by_chip, ("y", "x")).reshape(dp * span, half)
    theirs = lax.ppermute(mine, "core", [(0, 1), (1, 0)])

    kv_shards = ring_parts(jnp.concatenate([w_key, w_value], axis=1))
    pairs = chip_pairs(jnp.concatenate([w_query, kv_shards[0], w_out.T], axis=1))
    other_pairs = chip_pairs(after(jnp.concatenate(kv_shards[1:], axis=1), by_chip))
    weights = gather_rows(pairs, mine)
    query_full, kv_own = weights[:, :q_cols], weights[:, q_cols : q_cols + group_cols]
    out_t = weights[:, q_cols + group_cols :]
    others = gather_rows(other_pairs, mine, pairs)

    raw_halves = [rows.astype(jnp.float32) for rows in (mine, theirs)]
    square_sums = ring_sum(sum(jnp.sum(rows * rows, axis=1) for rows in raw_halves))
    all_len = jnp.sqrt(square_sums)
    embed_halves = [(rows / all_len[:, None]).astype(jnp.bfloat16) for rows in raw_halves]
    embed_len = lax.dynamic_slice_in_dim(all_len, lax.axis_index(DP) * span, span)
    embed_len = embed_len.reshape(3, pairs_dev, 1)
    units = embeds.astype(jnp.float32) / embed_len
    query_round = units[0].astype(jnp.bfloat16)

    def in_order(own, partner):
        left = jnp.where(first_core, own, partner)
        right = jnp.where(first_core, partner, own)
        return jnp.concatenate([left, right], axis=1)

    left, right = query_round[:, :half], query_round[:, half:]
    query_halves = [jnp.where(first_core, left, right), jnp.where(first_core, right, left)]
    score_part = sum(
        jnp.einsum("id,jd->ij", query, rows, preferred_element_type=jnp.float32)
        for query, rows in zip(query_halves, embed_halves)
    )
    layer_input = after(layer_input, score_part)
    scores = ring_sum(score_part) / SOFTMAX_TEMPER
    column = lax.iota(jnp.int32, dp * span)[None, :]
    is_passage = (column % span) // pairs_dev == 1
    own_ids = lax.iota(jnp.int32, pairs_dev)
    is_label = column == lax.axis_index(DP) * span + pairs_dev + own_ids[:, None]
    hard_column = (hard_index // pairs_dev) * span + 2 * pairs_dev + hard_index % pairs_dev
    is_candidate = is_passage | (column == hard_column[:, None])
    masked = jnp.where(is_candidate, scores, -jnp.inf)
    row_top = jnp.max(masked, axis=1)
    exps = jnp.exp(masked - row_top[:, None])
    exp_total = jnp.sum(exps, axis=1)
    per_query = row_top + jnp.log(exp_total) - jnp.sum(jnp.where(is_label, scores, 0.0), axis=1)
    local_total = jnp.sum(per_query)
    score_gradient = (
        (exps / exp_total[:, None] - is_label.astype(jnp.float32)) / SOFTMAX_TEMPER
    ).astype(jnp.bfloat16)
    by_owner = score_gradient.reshape(pairs_dev, dp, span).transpose(1, 0, 2)
    own_columns = lax.all_to_all(by_owner, DP, 0, 0, tiled=True)

    gain_in = in_gain.astype(jnp.float32)
    gain_out = out_gain.astype(jnp.float32)
    x_float = layer_input.astype(jnp.float32)
    inv_rms = lax.rsqrt(jnp.mean(x_float * x_float, axis=-1, keepdims=True) + EPSILON)
    normed = (x_float * inv_rms * gain_in).astype(jnp.bfloat16)
    last_pos = lengths - 1
    n_last = jnp.take_along_axis(normed, last_pos[:, None, None], axis=1)[:, 0]
    x_last = jnp.take_along_axis(layer_input, last_pos[:, None, None], axis=1)[:, 0].astype(
        jnp.float32
    )
    value_lowrank = jnp.einsum(
        "pld,dr->plr", normed, down_value, preferred_element_type=jnp.float32
    ).astype(jnp.bfloat16)
    query_lowrank = jnp.dot(n_last, down_query, preferred_element_type=jnp.float32).astype(
        jnp.bfloat16
    )
    group_size = q_cols // kv_cols
    score_scale = HD ** (-0.5)
    cosine, sine = angle_table(seq_len, HD)
    kv_pre = jnp.einsum("pld,dc->plc", normed, kv_own, preferred_element_type=jnp.float32)
    value_rows = (
        kv_pre[:, :, kv_cols:]
        + ADAPTER_SCALE
        * jnp.einsum(
            "plr,rc->plc", value_lowrank, value_up_weight, preferred_element_type=jnp.float32
        )
    ).astype(jnp.bfloat16)
    key_rows = rotate(kv_pre[:, :, :kv_cols], cosine[None], sine[None]).astype(jnp.bfloat16)
    query_before_rotation = jnp.dot(
        n_last, query_full, preferred_element_type=jnp.float32
    ) + ADAPTER_SCALE * jnp.dot(
        query_lowrank, query_up_weight, preferred_element_type=jnp.float32
    )
    cos_last = cosine[last_pos][:, None, :]
    sin_last = sine[last_pos][:, None, :]
    query_rot = rotate(
        query_before_rotation.reshape(pass_dev, group_size, HD), cos_last, sin_last
    ).astype(jnp.bfloat16)
    logits = (
        jnp.einsum("pgd,pld->pgl", query_rot, key_rows, preferred_element_type=jnp.float32)
        * score_scale
    )
    visible = lax.iota(jnp.int32, seq_len)[None, :] <= last_pos[:, None]
    logits = jnp.where(visible[:, None, :], logits, -1e30)
    row_peak = jnp.max(logits, axis=-1, keepdims=True)
    exponent_att = jnp.exp(logits - row_peak)
    attention = exponent_att / jnp.sum(exponent_att, axis=-1, keepdims=True)
    attention_round = attention.astype(jnp.bfloat16)
    mixed_heads = (
        jnp.einsum("pgl,pld->pgd", attention_round, value_rows, preferred_element_type=jnp.float32)
        .astype(jnp.bfloat16)
        .reshape(pass_dev, q_cols)
    )

    own_columns = jnp.pad(own_columns, ((0, 0), (0, span - pairs_dev), (0, 0)))
    own_columns = own_columns.reshape(dp * span, span)
    query_grad = in_order(
        *[
            jnp.einsum("ij,jd->id", score_gradient, rows, preferred_element_type=jnp.float32)
            for rows in embed_halves
        ]
    )
    both_grads = in_order(
        *[
            jnp.einsum("jc,jd->cd", own_columns, rows, preferred_element_type=jnp.float32)
            for rows in embed_halves
        ]
    )
    passage_rows = ring_gather(
        jnp.concatenate([both_grads[pairs_dev : pairs_dev + pass_dev], units[1, :pass_dev]], axis=0)
    )
    passage_rows = passage_rows.transpose(1, 0, 2).reshape(2 * pass_dev, width)
    passage_grad, passage_unit = passage_rows[:pass_dev], passage_rows[pass_dev:]
    passage_inner = jnp.sum(passage_grad * passage_unit, axis=1, keepdims=True)
    cotangent = (passage_grad - passage_inner * passage_unit) / embed_len[1, :pass_dev]

    out_part = jnp.einsum("pc,dc->pd", mixed_heads, out_t, preferred_element_type=jnp.float32)
    hidden = x_last + ring_sum(out_part)

    inv_hidden = lax.rsqrt(jnp.mean(hidden * hidden, axis=-1, keepdims=True) + EPSILON)
    scaled = gain_out * cotangent
    d_hidden = scaled * inv_hidden - hidden * inv_hidden**3 * jnp.mean(
        hidden * scaled, axis=-1, keepdims=True
    )
    d_mixed = jnp.dot(
        d_hidden.astype(jnp.bfloat16), out_t, preferred_element_type=jnp.float32
    ).reshape(pass_dev, group_size, HD)
    value_float = value_rows.astype(jnp.float32)
    key_float = key_rows.astype(jnp.float32)
    d_attention = jnp.einsum("pgd,pld->pgl", d_mixed, value_float, precision=MATMUL_ACCURACY)
    d_logits = attention * (d_attention - jnp.sum(attention * d_attention, axis=-1, keepdims=True))
    d_values = jnp.einsum(
        "pgl,pgd->pld", attention_round.astype(jnp.float32), d_mixed, precision=MATMUL_ACCURACY
    )
    d_query = (
        jnp.einsum("pgl,pld->pgd", d_logits, key_float, precision=MATMUL_ACCURACY) * score_scale
    )
    d_keys = (
        jnp.einsum(
            "pgl,pgd->pld", d_logits, query_rot.astype(jnp.float32), precision=MATMUL_ACCURACY
        )
        * score_scale
    )
    d_query_pre = rotate(d_query, cos_last, -sin_last).reshape(pass_dev, q_cols)
    d_keys_pre = rotate(d_keys, cosine[None], -sine[None])

    tok_span = seq_len // mp
    first_tok = place * tok_span
    d_kv = jnp.concatenate([d_keys_pre, d_values], axis=2).astype(jnp.bfloat16)
    d_kv = d_kv.reshape(pass_dev, mp, tok_span, group_cols)
    d_kv_own = [
        lax.dynamic_index_in_dim(d_kv, (place + k) % mp, axis=1, keepdims=False) for k in range(mp)
    ]
    d_kv_own = [d_kv_own[0]] + [shifted(d_kv_own[k], "mp", k) for k in range(1, mp)]
    du_query_part = jnp.einsum(
        "rc,pc->rp",
        query_up_weight.astype(jnp.float32),
        d_query_pre,
        precision=MATMUL_ACCURACY,
    )
    du_value_part = jnp.einsum(
        "rc,nc->rn",
        value_up_weight.astype(jnp.float32),
        d_values.reshape(pass_dev * seq_len, kv_cols),
        precision=MATMUL_ACCURACY,
    )
    rank = du_query_part.shape[0]
    n_tokens = pass_dev * seq_len
    grads = jnp.concatenate([query_grad, both_grads[pairs_dev:]], axis=0).reshape(units.shape)
    inner_part = jnp.pad(jnp.sum(grads * units, axis=2).T, ((0, rank - pairs_dev), (0, 0)))
    mp_part = jnp.concatenate([du_value_part, du_query_part, inner_part], axis=1)
    spare = -mp_part.shape[1] % 128
    mp_sum = ring_sum(jnp.pad(mp_part, ((0, 0), (0, spare))))
    query_back = jnp.einsum(
        "pc,dc->pd",
        after(d_query_pre.astype(jnp.bfloat16), mp_part),
        query_full,
        preferred_element_type=jnp.float32,
    )
    query_back_all = ring_parts(query_back)
    du = (ADAPTER_SCALE * mp_sum[:, : n_tokens + pass_dev]).astype(jnp.bfloat16)
    inner_sums = mp_sum[:pairs_dev, n_tokens + pass_dev : n_tokens + pass_dev + 3].T[:, :, None]
    embed_grads = (grads - inner_sums * units) / embed_len
    du_value = du[:, :n_tokens]
    du_query = du[:, n_tokens : n_tokens + pass_dev]
    up_query_part = ADAPTER_SCALE * jnp.einsum(
        "pr,pc->rc", query_lowrank.astype(jnp.float32), d_query_pre, precision=MATMUL_ACCURACY
    )
    up_value_part = ADAPTER_SCALE * jnp.einsum(
        "plr,plc->rc", value_lowrank.astype(jnp.float32), d_values, precision=MATMUL_ACCURACY
    )

    quarter = width // mp
    first_feature = place * quarter
    normed_quarter = lax.dynamic_slice_in_dim(
        normed.reshape(n_tokens, width), first_feature, quarter, 1
    )
    last_quarter = lax.dynamic_slice_in_dim(n_last, first_feature, quarter, 1)
    down_value_part = jnp.einsum(
        "rn,nd->rd", du_value, normed_quarter, preferred_element_type=jnp.float32
    )
    down_query_part = jnp.einsum(
        "rp,pd->rd", du_query, last_quarter, preferred_element_type=jnp.float32
    )
    down_part = jnp.concatenate([down_query_part, down_value_part], axis=0).reshape(dp, -1)
    head_part = jnp.concatenate(
        [up_query_part.reshape(dp, -1), up_value_part.reshape(dp, -1)], axis=1
    )
    loss_part = jnp.broadcast_to(local_total / dp, (dp, 1))
    parts = jnp.concatenate([down_part, head_part, loss_part], axis=1)
    n_down = down_part.shape[1]
    n_head = head_part.shape[1]
    padded = -(-parts.shape[1] // 128) * 128
    parts = jnp.pad(parts, ((0, 0), (0, padded - parts.shape[1]))).reshape(dp, 1, padded)
    reduced = jnp.sum(lax.all_to_all(parts, DP, 0, 0, tiled=True), axis=0)
    totals = spread(reduced, (*DP, "mp")).reshape(dp, mp, padded)
    grad_down = (
        totals[:, :, :n_down]
        .reshape(2 * rank, dp // (2 * rank), mp, n_down)
        .transpose(0, 2, 1, 3)
        .reshape(2 * rank, width)
    )
    grad_down_query = grad_down[:rank].T
    grad_down_value = grad_down[rank:].T
    own = lax.dynamic_index_in_dim(totals, place, axis=1, keepdims=False)
    n_up_query = q_cols * rank // dp
    grad_up_query = own[:, n_down : n_down + n_up_query].reshape(rank, q_cols)
    grad_up_value = own[:, n_down + n_up_query : n_down + n_head].reshape(rank, kv_cols)
    loss = jnp.sum(totals[:, 0, n_down + n_head]) / total_pairs

    d_kv_own = [d_kv_own[0]] + [after(blocks, reduced) for blocks in d_kv_own[1:]]
    kv_groups = [kv_own]
    kv_groups += [others[:, k * group_cols : (k + 1) * group_cols] for k in range(mp - 1)]
    x_local = lax.dynamic_slice_in_dim(layer_input, first_tok, tok_span, 1).astype(jnp.float32)
    rms_local = lax.dynamic_slice_in_dim(inv_rms, first_tok, tok_span, 1)
    du_local = lax.dynamic_slice_in_dim(
        du_value.reshape(rank, pass_dev, seq_len), first_tok, tok_span, 2
    )
    tok_ids = first_tok + lax.iota(jnp.int32, tok_span)
    at_local = (tok_ids[None, :] == last_pos[:, None])[:, :, None]
    d_normed = jnp.einsum(
        "rpt,dr->ptd", du_local, down_value, preferred_element_type=jnp.float32
    )
    query_adapter = jnp.einsum(
        "rp,dr->pd", du_query, down_query, preferred_element_type=jnp.float32
    )
    d_normed = d_normed + jnp.where(at_local, query_adapter[:, None, :], 0.0)
    for group in range(mp):
        term = jnp.einsum(
            "ptc,dc->ptd",
            d_kv_own[group],
            kv_groups[group],
            preferred_element_type=jnp.float32,
        )
        term = term + jnp.where(at_local, query_back_all[group][:, None, :], 0.0)
        d_normed = d_normed + term.astype(jnp.bfloat16).astype(jnp.float32)
    d_input = gain_in * d_normed * rms_local - x_local * rms_local**3 * jnp.mean(
        x_local * gain_in * d_normed, axis=-1, keepdims=True
    )
    d_input = d_input + jnp.where(at_local, d_hidden[:, None, :], 0.0)
    grad_input = d_input.astype(jnp.bfloat16)
    return (
        loss,
        embed_grads[0],
        embed_grads[1],
        embed_grads[2],
        grad_input,
        grad_down_query,
        grad_up_query,
        grad_down_value,
        grad_up_value,
    )


def solution(mesh):
    staged = Mesh(mesh.devices.reshape(4, 4, 2, 2, 4), (*DP, "mp"))
    in_specs = (
        P(DP, "mp"),
        P(DP, "mp"),
        P(DP, "mp"),
        P(DP),
        P(DP, None, None),
        P(DP),
        P(),
        P(),
        P(DP, "mp"),
        P(DP, "mp"),
        P(DP, "mp"),
        P("mp", DP),
        P(),
        P(None, "mp"),
        P(),
        P(None, "mp"),
    )
    out_specs = (
        P(),
        P(DP, "mp"),
        P(DP, "mp"),
        P(DP, "mp"),
        P(DP, "mp", None),
        P(),
        P(None, "mp"),
        P(),
        P(None, "mp"),
    )
    return jax.shard_map(
        on_device, mesh=staged, in_specs=in_specs, out_specs=out_specs, check_vma=False
    )
```

```python
import jax
import jax.numpy as jnp
from jax import lax
from jax.sharding import Mesh
from jax.sharding import PartitionSpec as P

HD = 128
DP = ("y", "x", "zh", "core")


EPSILON = 1e-05
SOFTMAX_TEMPER = 0.01
ADAPTER_SCALE = 2.0
ROPE_BASE = 10000.0
MATMUL_ACCURACY = lax.Precision.HIGHEST


def angle_table(seq_len, head_dim):
    half_dim = head_dim // 2
    frequency = ROPE_BASE ** (-(jnp.arange(half_dim, dtype=jnp.float32) * 2.0 / head_dim))
    angles = jnp.arange(seq_len, dtype=jnp.float32)[:, None] * frequency[None, :]
    return (jnp.cos(angles), jnp.sin(angles))


def rotate(field, cosine, sine):
    half_dim = field.shape[-1] // 2
    leading = field[..., :half_dim]
    trailing = field[..., half_dim:]
    return jnp.concatenate(
        [leading * cosine - trailing * sine, trailing * cosine + leading * sine], axis=-1
    )


def shifted(value, axis_name, shift):
    size = lax.axis_size(axis_name)
    return lax.ppermute(value, axis_name, [(i, (i + shift) % size) for i in range(size)])


def ring_sum(value):
    one, two, three = (shifted(value, "mp", k) for k in (1, 2, 3))
    return (value + two) + (one + three)


def ring_parts(value):
    return [value] + [shifted(value, "mp", k) for k in (1, 2, 3)]


def ring_gather(value):
    parts = jnp.stack(ring_parts(value))
    place = lax.axis_index("mp")
    order = (place - lax.iota(jnp.int32, 4)) % 4
    return jnp.take(parts, order, axis=0)


def spread(value, axis_name):
    size = lax.axis_size(axis_name)
    return lax.all_to_all(
        jnp.broadcast_to(value[None], (size,) + value.shape), axis_name, 0, 0, tiled=True
    )


def pair_gather(value, axis_name):
    other = lax.ppermute(value, axis_name, [(0, 1), (1, 0)])
    at_first = lax.axis_index(axis_name) == 0
    return jnp.stack([jnp.where(at_first, value, other), jnp.where(at_first, other, value)])


def after(value, *first):
    return lax.optimization_barrier((value, *first))[0]


def core_halves(value):
    half = value.shape[1] // 2
    at_first = lax.axis_index("core") == 0
    left, right = value[:, :half], value[:, half:]
    kept = jnp.where(at_first, left, right)
    other = lax.ppermute(jnp.where(at_first, right, left), "core", [(0, 1), (1, 0)])
    return jnp.stack([jnp.where(at_first, kept, other), jnp.where(at_first, other, kept)])


def chip_pairs(shard):
    pair = pair_gather(shard, "core").reshape(2 * shard.shape[0], shard.shape[1])
    moved = lax.ppermute(pair, ("zh", "core"), [(0, 2), (3, 1)])
    return jnp.where(lax.axis_index("zh") == lax.axis_index("core"), pair, moved)


def gather_rows(pair, *first):
    return lax.all_gather(after(pair, *first), ("y", "x", "core"), axis=0, tiled=True)


def on_device(
    queries,
    passages,
    negatives,
    hard_index,
    layer_input,
    lengths,
    in_gain,
    out_gain,
    w_query,
    w_key,
    w_value,
    w_out,
    down_query,
    query_up_weight,
    down_value,
    value_up_weight,
):
    dp = lax.axis_size(DP)
    mp = lax.axis_size("mp")
    place = lax.axis_index("mp")
    pairs_dev, feature_dev = queries.shape
    total_pairs = pairs_dev * dp
    pass_dev, seq_len, width = layer_input.shape
    kv_cols = w_key.shape[1]
    q_cols = w_query.shape[1]
    group_cols = 2 * kv_cols

    half = feature_dev // 2
    span = 3 * pairs_dev
    first_core = lax.axis_index("core") == 0
    embeds = jnp.stack([queries, passages, negatives])
    by_core = core_halves(embeds.reshape(span, feature_dev))
    by_chip = pair_gather(by_core, "zh")
    mine = spread(by_chip, ("y", "x")).reshape(dp * span, half)
    theirs = lax.ppermute(mine, "core", [(0, 1), (1, 0)])

    layer_input = after(layer_input, by_chip)
    gain_in = in_gain.astype(jnp.float32)
    gain_out = out_gain.astype(jnp.float32)
    x_float = layer_input.astype(jnp.float32)
    inv_rms = lax.rsqrt(jnp.mean(x_float * x_float, axis=-1, keepdims=True) + EPSILON)
    normed = (x_float * inv_rms * gain_in).astype(jnp.bfloat16)

    kv_shard = jnp.concatenate([w_key, w_value], axis=1)
    pairs = chip_pairs(jnp.concatenate([w_query, kv_shard, w_out.T], axis=1))
    weights = gather_rows(pairs, mine, normed)
    query_full, kv_own = weights[:, :q_cols], weights[:, q_cols : q_cols + group_cols]
    out_t = weights[:, q_cols + group_cols :]

    raw_halves = [rows.astype(jnp.float32) for rows in (mine, theirs)]
    square_sums = ring_sum(sum(jnp.sum(rows * rows, axis=1) for rows in raw_halves))
    all_len = jnp.sqrt(square_sums)
    embed_halves = [(rows / all_len[:, None]).astype(jnp.bfloat16) for rows in raw_halves]
    embed_len = lax.dynamic_slice_in_dim(all_len, lax.axis_index(DP) * span, span)
    embed_len = embed_len.reshape(3, pairs_dev, 1)
    units = embeds.astype(jnp.float32) / embed_len
    query_round = units[0].astype(jnp.bfloat16)

    def in_order(own, partner):
        left = jnp.where(first_core, own, partner)
        right = jnp.where(first_core, partner, own)
        return jnp.concatenate([left, right], axis=1)

    left, right = query_round[:, :half], query_round[:, half:]
    query_halves = [jnp.where(first_core, left, right), jnp.where(first_core, right, left)]
    score_part = sum(
        jnp.einsum("id,jd->ij", query, rows, preferred_element_type=jnp.float32)
        for query, rows in zip(query_halves, embed_halves)
    )
    scores = ring_sum(score_part) / SOFTMAX_TEMPER
    column = lax.iota(jnp.int32, dp * span)[None, :]
    is_passage = (column % span) // pairs_dev == 1
    own_ids = lax.iota(jnp.int32, pairs_dev)
    is_label = column == lax.axis_index(DP) * span + pairs_dev + own_ids[:, None]
    hard_column = (hard_index // pairs_dev) * span + 2 * pairs_dev + hard_index % pairs_dev
    is_candidate = is_passage | (column == hard_column[:, None])
    masked = jnp.where(is_candidate, scores, -jnp.inf)
    row_top = jnp.max(masked, axis=1)
    exps = jnp.exp(masked - row_top[:, None])
    exp_total = jnp.sum(exps, axis=1)
    per_query = row_top + jnp.log(exp_total) - jnp.sum(jnp.where(is_label, scores, 0.0), axis=1)
    local_total = jnp.sum(per_query)
    score_gradient = (
        (exps / exp_total[:, None] - is_label.astype(jnp.float32)) / SOFTMAX_TEMPER
    ).astype(jnp.bfloat16)
    by_owner = score_gradient.reshape(pairs_dev, dp, span).transpose(1, 0, 2)
    own_columns = lax.all_to_all(by_owner, DP, 0, 0, tiled=True)

    kv_shards = ring_parts(after(kv_shard, own_columns))
    others = gather_rows(chip_pairs(jnp.concatenate(kv_shards[1:], axis=1)), pairs)

    normed, lengths = after(normed, score_gradient), after(lengths, score_gradient)
    last_pos = lengths - 1
    n_last = jnp.take_along_axis(normed, last_pos[:, None, None], axis=1)[:, 0]
    x_last = jnp.take_along_axis(layer_input, last_pos[:, None, None], axis=1)[:, 0].astype(
        jnp.float32
    )
    value_lowrank = jnp.einsum(
        "pld,dr->plr", normed, down_value, preferred_element_type=jnp.float32
    ).astype(jnp.bfloat16)
    query_lowrank = jnp.dot(n_last, down_query, preferred_element_type=jnp.float32).astype(
        jnp.bfloat16
    )
    group_size = q_cols // kv_cols
    score_scale = HD ** (-0.5)
    cosine, sine = angle_table(seq_len, HD)
    kv_pre = jnp.einsum("pld,dc->plc", normed, kv_own, preferred_element_type=jnp.float32)
    value_rows = (
        kv_pre[:, :, kv_cols:]
        + ADAPTER_SCALE
        * jnp.einsum(
            "plr,rc->plc", value_lowrank, value_up_weight, preferred_element_type=jnp.float32
        )
    ).astype(jnp.bfloat16)
    key_rows = rotate(kv_pre[:, :, :kv_cols], cosine[None], sine[None]).astype(jnp.bfloat16)
    query_before_rotation = jnp.dot(
        n_last, query_full, preferred_element_type=jnp.float32
    ) + ADAPTER_SCALE * jnp.dot(
        query_lowrank, query_up_weight, preferred_element_type=jnp.float32
    )
    cos_last = cosine[last_pos][:, None, :]
    sin_last = sine[last_pos][:, None, :]
    query_rot = rotate(
        query_before_rotation.reshape(pass_dev, group_size, HD), cos_last, sin_last
    ).astype(jnp.bfloat16)
    logits = (
        jnp.einsum("pgd,pld->pgl", query_rot, key_rows, preferred_element_type=jnp.float32)
        * score_scale
    )
    visible = lax.iota(jnp.int32, seq_len)[None, :] <= last_pos[:, None]
    logits = jnp.where(visible[:, None, :], logits, -1e30)
    row_peak = jnp.max(logits, axis=-1, keepdims=True)
    exponent_att = jnp.exp(logits - row_peak)
    attention = exponent_att / jnp.sum(exponent_att, axis=-1, keepdims=True)
    attention_round = attention.astype(jnp.bfloat16)
    mixed_heads = (
        jnp.einsum("pgl,pld->pgd", attention_round, value_rows, preferred_element_type=jnp.float32)
        .astype(jnp.bfloat16)
        .reshape(pass_dev, q_cols)
    )

    own_columns = jnp.pad(own_columns, ((0, 0), (0, span - pairs_dev), (0, 0)))
    own_columns = own_columns.reshape(dp * span, span)
    query_grad = in_order(
        *[
            jnp.einsum("ij,jd->id", score_gradient, rows, preferred_element_type=jnp.float32)
            for rows in embed_halves
        ]
    )
    both_grads = in_order(
        *[
            jnp.einsum("jc,jd->cd", own_columns, rows, preferred_element_type=jnp.float32)
            for rows in embed_halves
        ]
    )
    passage_rows = ring_gather(
        jnp.concatenate([both_grads[pairs_dev : pairs_dev + pass_dev], units[1, :pass_dev]], axis=0)
    )
    passage_rows = passage_rows.transpose(1, 0, 2).reshape(2 * pass_dev, width)
    passage_grad, passage_unit = passage_rows[:pass_dev], passage_rows[pass_dev:]
    passage_inner = jnp.sum(passage_grad * passage_unit, axis=1, keepdims=True)
    cotangent = (passage_grad - passage_inner * passage_unit) / embed_len[1, :pass_dev]

    out_part = jnp.einsum("pc,dc->pd", mixed_heads, out_t, preferred_element_type=jnp.float32)
    hidden = x_last + ring_sum(out_part)

    inv_hidden = lax.rsqrt(jnp.mean(hidden * hidden, axis=-1, keepdims=True) + EPSILON)
    scaled = gain_out * cotangent
    d_hidden = scaled * inv_hidden - hidden * inv_hidden**3 * jnp.mean(
        hidden * scaled, axis=-1, keepdims=True
    )
    d_mixed = jnp.dot(
        d_hidden.astype(jnp.bfloat16), out_t, preferred_element_type=jnp.float32
    ).reshape(pass_dev, group_size, HD)
    value_float = value_rows.astype(jnp.float32)
    key_float = key_rows.astype(jnp.float32)
    d_attention = jnp.einsum("pgd,pld->pgl", d_mixed, value_float, precision=MATMUL_ACCURACY)
    d_logits = attention * (d_attention - jnp.sum(attention * d_attention, axis=-1, keepdims=True))
    d_values = jnp.einsum(
        "pgl,pgd->pld", attention_round.astype(jnp.float32), d_mixed, precision=MATMUL_ACCURACY
    )
    d_query = (
        jnp.einsum("pgl,pld->pgd", d_logits, key_float, precision=MATMUL_ACCURACY) * score_scale
    )
    d_keys = (
        jnp.einsum(
            "pgl,pgd->pld", d_logits, query_rot.astype(jnp.float32), precision=MATMUL_ACCURACY
        )
        * score_scale
    )
    d_query_pre = rotate(d_query, cos_last, -sin_last).reshape(pass_dev, q_cols)
    d_keys_pre = rotate(d_keys, cosine[None], -sine[None])

    tok_span = seq_len // mp
    first_tok = place * tok_span
    d_kv = jnp.concatenate([d_keys_pre, d_values], axis=2).astype(jnp.bfloat16)
    d_kv = d_kv.reshape(pass_dev, mp, tok_span, group_cols)
    d_kv_own = [
        lax.dynamic_index_in_dim(d_kv, (place + k) % mp, axis=1, keepdims=False) for k in range(mp)
    ]
    d_kv_own = [d_kv_own[0]] + [shifted(d_kv_own[k], "mp", k) for k in range(1, mp)]
    du_query_part = jnp.einsum(
        "rc,pc->rp",
        query_up_weight.astype(jnp.float32),
        d_query_pre,
        precision=MATMUL_ACCURACY,
    )
    du_value_part = jnp.einsum(
        "rc,nc->rn",
        value_up_weight.astype(jnp.float32),
        d_values.reshape(pass_dev * seq_len, kv_cols),
        precision=MATMUL_ACCURACY,
    )
    rank = du_query_part.shape[0]
    n_tokens = pass_dev * seq_len
    grads = jnp.concatenate([query_grad, both_grads[pairs_dev:]], axis=0).reshape(units.shape)
    inner_part = jnp.pad(jnp.sum(grads * units, axis=2).T, ((0, rank - pairs_dev), (0, 0)))
    mp_part = jnp.concatenate([du_value_part, du_query_part, inner_part], axis=1)
    spare = -mp_part.shape[1] % 128
    mp_sum = ring_sum(jnp.pad(mp_part, ((0, 0), (0, spare))))
    query_back = jnp.einsum(
        "pc,dc->pd",
        after(d_query_pre.astype(jnp.bfloat16), mp_part),
        query_full,
        preferred_element_type=jnp.float32,
    )
    query_back_all = ring_parts(query_back)
    du = (ADAPTER_SCALE * mp_sum[:, : n_tokens + pass_dev]).astype(jnp.bfloat16)
    inner_sums = mp_sum[:pairs_dev, n_tokens + pass_dev : n_tokens + pass_dev + 3].T[:, :, None]
    embed_grads = (grads - inner_sums * units) / embed_len
    du_value = du[:, :n_tokens]
    du_query = du[:, n_tokens : n_tokens + pass_dev]
    up_query_part = ADAPTER_SCALE * jnp.einsum(
        "pr,pc->rc", query_lowrank.astype(jnp.float32), d_query_pre, precision=MATMUL_ACCURACY
    )
    up_value_part = ADAPTER_SCALE * jnp.einsum(
        "plr,plc->rc", value_lowrank.astype(jnp.float32), d_values, precision=MATMUL_ACCURACY
    )

    quarter = width // mp
    first_feature = place * quarter
    normed_quarter = lax.dynamic_slice_in_dim(
        normed.reshape(n_tokens, width), first_feature, quarter, 1
    )
    last_quarter = lax.dynamic_slice_in_dim(n_last, first_feature, quarter, 1)
    down_value_part = jnp.einsum(
        "rn,nd->rd", du_value, normed_quarter, preferred_element_type=jnp.float32
    )
    down_query_part = jnp.einsum(
        "rp,pd->rd", du_query, last_quarter, preferred_element_type=jnp.float32
    )
    down_part = jnp.concatenate([down_query_part, down_value_part], axis=0).reshape(dp, -1)
    head_part = jnp.concatenate(
        [up_query_part.reshape(dp, -1), up_value_part.reshape(dp, -1)], axis=1
    )
    loss_part = jnp.broadcast_to(local_total / dp, (dp, 1))
    parts = jnp.concatenate([down_part, head_part, loss_part], axis=1)
    n_down = down_part.shape[1]
    n_head = head_part.shape[1]
    padded = -(-parts.shape[1] // 128) * 128
    parts = jnp.pad(parts, ((0, 0), (0, padded - parts.shape[1]))).reshape(dp, 1, padded)
    reduced = jnp.sum(lax.all_to_all(parts, DP, 0, 0, tiled=True), axis=0)
    totals = spread(reduced, (*DP, "mp")).reshape(dp, mp, padded)
    grad_down = (
        totals[:, :, :n_down]
        .reshape(2 * rank, dp // (2 * rank), mp, n_down)
        .transpose(0, 2, 1, 3)
        .reshape(2 * rank, width)
    )
    grad_down_query = grad_down[:rank].T
    grad_down_value = grad_down[rank:].T
    own = lax.dynamic_index_in_dim(totals, place, axis=1, keepdims=False)
    n_up_query = q_cols * rank // dp
    grad_up_query = own[:, n_down : n_down + n_up_query].reshape(rank, q_cols)
    grad_up_value = own[:, n_down + n_up_query : n_down + n_head].reshape(rank, kv_cols)
    loss = jnp.sum(totals[:, 0, n_down + n_head]) / total_pairs

    d_kv_own = [d_kv_own[0]] + [after(blocks, reduced) for blocks in d_kv_own[1:]]
    kv_groups = [kv_own]
    kv_groups += [others[:, k * group_cols : (k + 1) * group_cols] for k in range(mp - 1)]
    x_local = lax.dynamic_slice_in_dim(layer_input, first_tok, tok_span, 1).astype(jnp.float32)
    rms_local = lax.dynamic_slice_in_dim(inv_rms, first_tok, tok_span, 1)
    du_local = lax.dynamic_slice_in_dim(
        du_value.reshape(rank, pass_dev, seq_len), first_tok, tok_span, 2
    )
    tok_ids = first_tok + lax.iota(jnp.int32, tok_span)
    at_local = (tok_ids[None, :] == last_pos[:, None])[:, :, None]
    d_normed = jnp.einsum(
        "rpt,dr->ptd", du_local, down_value, preferred_element_type=jnp.float32
    )
    query_adapter = jnp.einsum(
        "rp,dr->pd", du_query, down_query, preferred_element_type=jnp.float32
    )
    d_normed = d_normed + jnp.where(at_local, query_adapter[:, None, :], 0.0)
    for group in range(mp):
        term = jnp.einsum(
            "ptc,dc->ptd",
            d_kv_own[group],
            kv_groups[group],
            preferred_element_type=jnp.float32,
        )
        term = term + jnp.where(at_local, query_back_all[group][:, None, :], 0.0)
        d_normed = d_normed + term.astype(jnp.bfloat16).astype(jnp.float32)
    d_input = gain_in * d_normed * rms_local - x_local * rms_local**3 * jnp.mean(
        x_local * gain_in * d_normed, axis=-1, keepdims=True
    )
    d_input = d_input + jnp.where(at_local, d_hidden[:, None, :], 0.0)
    grad_input = d_input.astype(jnp.bfloat16)
    return (
        loss,
        embed_grads[0],
        embed_grads[1],
        embed_grads[2],
        grad_input,
        grad_down_query,
        grad_up_query,
        grad_down_value,
        grad_up_value,
    )


def solution(mesh):
    staged = Mesh(mesh.devices.reshape(4, 4, 2, 2, 4), (*DP, "mp"))
    in_specs = (
        P(DP, "mp"),
        P(DP, "mp"),
        P(DP, "mp"),
        P(DP),
        P(DP, None, None),
        P(DP),
        P(),
        P(),
        P(DP, "mp"),
        P(DP, "mp"),
        P(DP, "mp"),
        P("mp", DP),
        P(),
        P(None, "mp"),
        P(),
        P(None, "mp"),
    )
    out_specs = (
        P(),
        P(DP, "mp"),
        P(DP, "mp"),
        P(DP, "mp"),
        P(DP, "mp", None),
        P(),
        P(None, "mp"),
        P(),
        P(None, "mp"),
    )
    return jax.shard_map(
        on_device, mesh=staged, in_specs=in_specs, out_specs=out_specs, check_vma=False
    )
```

```python
import jax
import jax.numpy as jnp
from jax import lax
from jax.sharding import Mesh
from jax.sharding import PartitionSpec as P

HD = 128
DP = ("y", "x", "zh", "core")


EPSILON = 1e-05
SOFTMAX_TEMPER = 0.01
ADAPTER_SCALE = 2.0
ROPE_BASE = 10000.0
MATMUL_ACCURACY = lax.Precision.HIGHEST


def angle_table(seq_len, head_dim):
    half_dim = head_dim // 2
    frequency = ROPE_BASE ** (-(jnp.arange(half_dim, dtype=jnp.float32) * 2.0 / head_dim))
    angles = jnp.arange(seq_len, dtype=jnp.float32)[:, None] * frequency[None, :]
    return (jnp.cos(angles), jnp.sin(angles))


def rotate(field, cosine, sine):
    half_dim = field.shape[-1] // 2
    leading = field[..., :half_dim]
    trailing = field[..., half_dim:]
    return jnp.concatenate(
        [leading * cosine - trailing * sine, trailing * cosine + leading * sine], axis=-1
    )


def shifted(value, axis_name, shift):
    size = lax.axis_size(axis_name)
    return lax.ppermute(value, axis_name, [(i, (i + shift) % size) for i in range(size)])


def ring_sum(value):
    one, two, three = (shifted(value, "mp", k) for k in (1, 2, 3))
    return (value + two) + (one + three)


def ring_parts(value):
    return [value] + [shifted(value, "mp", k) for k in (1, 2, 3)]


def ring_gather(value):
    parts = jnp.stack(ring_parts(value))
    place = lax.axis_index("mp")
    order = (place - lax.iota(jnp.int32, 4)) % 4
    return jnp.take(parts, order, axis=0)


def spread(value, axis_name):
    size = lax.axis_size(axis_name)
    return lax.all_to_all(
        jnp.broadcast_to(value[None], (size,) + value.shape), axis_name, 0, 0, tiled=True
    )


def pair_gather(value, axis_name):
    other = lax.ppermute(value, axis_name, [(0, 1), (1, 0)])
    at_first = lax.axis_index(axis_name) == 0
    return jnp.stack([jnp.where(at_first, value, other), jnp.where(at_first, other, value)])


def after(value, *first):
    return lax.optimization_barrier((value, *first))[0]


def core_halves(value):
    half = value.shape[1] // 2
    at_first = lax.axis_index("core") == 0
    left, right = value[:, :half], value[:, half:]
    kept = jnp.where(at_first, left, right)
    other = lax.ppermute(jnp.where(at_first, right, left), "core", [(0, 1), (1, 0)])
    return jnp.stack([jnp.where(at_first, kept, other), jnp.where(at_first, other, kept)])


def chip_pairs(shard):
    pair = pair_gather(shard, "core").reshape(2 * shard.shape[0], shard.shape[1])
    moved = lax.ppermute(pair, ("zh", "core"), [(0, 2), (3, 1)])
    return jnp.where(lax.axis_index("zh") == lax.axis_index("core"), pair, moved)


def gather_rows(pair, *first):
    return lax.all_gather(after(pair, *first), ("y", "x", "core"), axis=0, tiled=True)


def on_device(
    queries,
    passages,
    negatives,
    hard_index,
    layer_input,
    lengths,
    in_gain,
    out_gain,
    w_query,
    w_key,
    w_value,
    w_out,
    down_query,
    query_up_weight,
    down_value,
    value_up_weight,
):
    dp = lax.axis_size(DP)
    mp = lax.axis_size("mp")
    place = lax.axis_index("mp")
    pairs_dev, feature_dev = queries.shape
    total_pairs = pairs_dev * dp
    pass_dev, seq_len, width = layer_input.shape
    kv_cols = w_key.shape[1]
    q_cols = w_query.shape[1]
    group_cols = 2 * kv_cols

    half = feature_dev // 2
    span = 3 * pairs_dev
    first_core = lax.axis_index("core") == 0
    embeds = jnp.stack([queries, passages, negatives])
    by_core = core_halves(embeds.reshape(span, feature_dev))
    by_chip = pair_gather(by_core, "zh")
    mine = spread(by_chip, ("y", "x")).reshape(dp * span, half)
    theirs = lax.ppermute(mine, "core", [(0, 1), (1, 0)])

    layer_input = after(layer_input, by_chip)
    gain_in = in_gain.astype(jnp.float32)
    gain_out = out_gain.astype(jnp.float32)
    x_float = layer_input.astype(jnp.float32)
    inv_rms = lax.rsqrt(jnp.mean(x_float * x_float, axis=-1, keepdims=True) + EPSILON)
    normed = (x_float * inv_rms * gain_in).astype(jnp.bfloat16)

    kv_shard = jnp.concatenate([w_key, w_value], axis=1)
    pairs = chip_pairs(jnp.concatenate([w_query, kv_shard, w_out.T], axis=1))
    weights = gather_rows(pairs, mine, normed)
    kv_shards = ring_parts(after(kv_shard, mine))
    others = gather_rows(chip_pairs(jnp.concatenate(kv_shards[1:], axis=1)), pairs)
    query_full, kv_own = weights[:, :q_cols], weights[:, q_cols : q_cols + group_cols]
    out_t = weights[:, q_cols + group_cols :]

    raw_halves = [rows.astype(jnp.float32) for rows in (mine, theirs)]
    square_sums = ring_sum(sum(jnp.sum(rows * rows, axis=1) for rows in raw_halves))
    all_len = jnp.sqrt(square_sums)
    embed_halves = [(rows / all_len[:, None]).astype(jnp.bfloat16) for rows in raw_halves]
    embed_len = lax.dynamic_slice_in_dim(all_len, lax.axis_index(DP) * span, span)
    embed_len = embed_len.reshape(3, pairs_dev, 1)
    units = embeds.astype(jnp.float32) / embed_len
    query_round = units[0].astype(jnp.bfloat16)

    def in_order(own, partner):
        left = jnp.where(first_core, own, partner)
        right = jnp.where(first_core, partner, own)
        return jnp.concatenate([left, right], axis=1)

    left, right = query_round[:, :half], query_round[:, half:]
    query_halves = [jnp.where(first_core, left, right), jnp.where(first_core, right, left)]
    score_part = sum(
        jnp.einsum("id,jd->ij", query, rows, preferred_element_type=jnp.float32)
        for query, rows in zip(query_halves, embed_halves)
    )
    scores = ring_sum(score_part) / SOFTMAX_TEMPER
    column = lax.iota(jnp.int32, dp * span)[None, :]
    is_passage = (column % span) // pairs_dev == 1
    own_ids = lax.iota(jnp.int32, pairs_dev)
    is_label = column == lax.axis_index(DP) * span + pairs_dev + own_ids[:, None]
    hard_column = (hard_index // pairs_dev) * span + 2 * pairs_dev + hard_index % pairs_dev
    is_candidate = is_passage | (column == hard_column[:, None])
    masked = jnp.where(is_candidate, scores, -jnp.inf)
    row_top = jnp.max(masked, axis=1)
    exps = jnp.exp(masked - row_top[:, None])
    exp_total = jnp.sum(exps, axis=1)
    per_query = row_top + jnp.log(exp_total) - jnp.sum(jnp.where(is_label, scores, 0.0), axis=1)
    local_total = jnp.sum(per_query)
    score_gradient = (
        (exps / exp_total[:, None] - is_label.astype(jnp.float32)) / SOFTMAX_TEMPER
    ).astype(jnp.bfloat16)
    by_owner = score_gradient.reshape(pairs_dev, dp, span).transpose(1, 0, 2)
    own_columns = lax.all_to_all(by_owner, DP, 0, 0, tiled=True)

    own_columns = jnp.pad(own_columns, ((0, 0), (0, span - pairs_dev), (0, 0)))
    own_columns = own_columns.reshape(dp * span, span)
    query_grad = in_order(
        *[
            jnp.einsum("ij,jd->id", score_gradient, rows, preferred_element_type=jnp.float32)
            for rows in embed_halves
        ]
    )
    both_grads = in_order(
        *[
            jnp.einsum("jc,jd->cd", own_columns, rows, preferred_element_type=jnp.float32)
            for rows in embed_halves
        ]
    )
    passage_rows = ring_gather(
        jnp.concatenate([both_grads[pairs_dev : pairs_dev + pass_dev], units[1, :pass_dev]], axis=0)
    )
    passage_rows = passage_rows.transpose(1, 0, 2).reshape(2 * pass_dev, width)
    passage_grad, passage_unit = passage_rows[:pass_dev], passage_rows[pass_dev:]
    passage_inner = jnp.sum(passage_grad * passage_unit, axis=1, keepdims=True)
    cotangent = (passage_grad - passage_inner * passage_unit) / embed_len[1, :pass_dev]

    normed, lengths = after(normed, score_gradient), after(lengths, both_grads)
    last_pos = lengths - 1
    n_last = jnp.take_along_axis(normed, last_pos[:, None, None], axis=1)[:, 0]
    x_last = jnp.take_along_axis(layer_input, last_pos[:, None, None], axis=1)[:, 0].astype(
        jnp.float32
    )
    value_lowrank = jnp.einsum(
        "pld,dr->plr", normed, down_value, preferred_element_type=jnp.float32
    ).astype(jnp.bfloat16)
    query_lowrank = jnp.dot(n_last, down_query, preferred_element_type=jnp.float32).astype(
        jnp.bfloat16
    )
    group_size = q_cols // kv_cols
    score_scale = HD ** (-0.5)
    cosine, sine = angle_table(seq_len, HD)
    kv_pre = jnp.einsum("pld,dc->plc", normed, kv_own, preferred_element_type=jnp.float32)
    value_rows = (
        kv_pre[:, :, kv_cols:]
        + ADAPTER_SCALE
        * jnp.einsum(
            "plr,rc->plc", value_lowrank, value_up_weight, preferred_element_type=jnp.float32
        )
    ).astype(jnp.bfloat16)
    key_rows = rotate(kv_pre[:, :, :kv_cols], cosine[None], sine[None]).astype(jnp.bfloat16)
    query_before_rotation = jnp.dot(
        n_last, query_full, preferred_element_type=jnp.float32
    ) + ADAPTER_SCALE * jnp.dot(
        query_lowrank, query_up_weight, preferred_element_type=jnp.float32
    )
    cos_last = cosine[last_pos][:, None, :]
    sin_last = sine[last_pos][:, None, :]
    query_rot = rotate(
        query_before_rotation.reshape(pass_dev, group_size, HD), cos_last, sin_last
    ).astype(jnp.bfloat16)
    logits = (
        jnp.einsum("pgd,pld->pgl", query_rot, key_rows, preferred_element_type=jnp.float32)
        * score_scale
    )
    visible = lax.iota(jnp.int32, seq_len)[None, :] <= last_pos[:, None]
    logits = jnp.where(visible[:, None, :], logits, -1e30)
    row_peak = jnp.max(logits, axis=-1, keepdims=True)
    exponent_att = jnp.exp(logits - row_peak)
    attention = exponent_att / jnp.sum(exponent_att, axis=-1, keepdims=True)
    attention_round = attention.astype(jnp.bfloat16)
    mixed_heads = (
        jnp.einsum("pgl,pld->pgd", attention_round, value_rows, preferred_element_type=jnp.float32)
        .astype(jnp.bfloat16)
        .reshape(pass_dev, q_cols)
    )

    out_part = jnp.einsum("pc,dc->pd", mixed_heads, out_t, preferred_element_type=jnp.float32)
    hidden = x_last + ring_sum(out_part)

    inv_hidden = lax.rsqrt(jnp.mean(hidden * hidden, axis=-1, keepdims=True) + EPSILON)
    scaled = gain_out * cotangent
    d_hidden = scaled * inv_hidden - hidden * inv_hidden**3 * jnp.mean(
        hidden * scaled, axis=-1, keepdims=True
    )
    d_mixed = jnp.dot(
        d_hidden.astype(jnp.bfloat16), out_t, preferred_element_type=jnp.float32
    ).reshape(pass_dev, group_size, HD)
    value_float = value_rows.astype(jnp.float32)
    key_float = key_rows.astype(jnp.float32)
    d_attention = jnp.einsum("pgd,pld->pgl", d_mixed, value_float, precision=MATMUL_ACCURACY)
    d_logits = attention * (d_attention - jnp.sum(attention * d_attention, axis=-1, keepdims=True))
    d_values = jnp.einsum(
        "pgl,pgd->pld", attention_round.astype(jnp.float32), d_mixed, precision=MATMUL_ACCURACY
    )
    d_query = (
        jnp.einsum("pgl,pld->pgd", d_logits, key_float, precision=MATMUL_ACCURACY) * score_scale
    )
    d_keys = (
        jnp.einsum(
            "pgl,pgd->pld", d_logits, query_rot.astype(jnp.float32), precision=MATMUL_ACCURACY
        )
        * score_scale
    )
    d_query_pre = rotate(d_query, cos_last, -sin_last).reshape(pass_dev, q_cols)
    d_keys_pre = rotate(d_keys, cosine[None], -sine[None])

    tok_span = seq_len // mp
    first_tok = place * tok_span
    d_kv = jnp.concatenate([d_keys_pre, d_values], axis=2).astype(jnp.bfloat16)
    d_kv = d_kv.reshape(pass_dev, mp, tok_span, group_cols)
    d_kv_own = [
        lax.dynamic_index_in_dim(d_kv, (place + k) % mp, axis=1, keepdims=False) for k in range(mp)
    ]
    d_kv_own = [d_kv_own[0]] + [shifted(d_kv_own[k], "mp", k) for k in range(1, mp)]
    du_query_part = jnp.einsum(
        "rc,pc->rp",
        query_up_weight.astype(jnp.float32),
        d_query_pre,
        precision=MATMUL_ACCURACY,
    )
    du_value_part = jnp.einsum(
        "rc,nc->rn",
        value_up_weight.astype(jnp.float32),
        d_values.reshape(pass_dev * seq_len, kv_cols),
        precision=MATMUL_ACCURACY,
    )
    rank = du_query_part.shape[0]
    n_tokens = pass_dev * seq_len
    grads = jnp.concatenate([query_grad, both_grads[pairs_dev:]], axis=0).reshape(units.shape)
    inner_part = jnp.pad(jnp.sum(grads * units, axis=2).T, ((0, rank - pairs_dev), (0, 0)))
    mp_part = jnp.concatenate([du_value_part, du_query_part, inner_part], axis=1)
    spare = -mp_part.shape[1] % 128
    mp_sum = ring_sum(jnp.pad(mp_part, ((0, 0), (0, spare))))
    query_back = jnp.einsum(
        "pc,dc->pd",
        after(d_query_pre.astype(jnp.bfloat16), mp_part),
        query_full,
        preferred_element_type=jnp.float32,
    )
    query_back_all = ring_parts(query_back)
    du = (ADAPTER_SCALE * mp_sum[:, : n_tokens + pass_dev]).astype(jnp.bfloat16)
    inner_sums = mp_sum[:pairs_dev, n_tokens + pass_dev : n_tokens + pass_dev + 3].T[:, :, None]
    embed_grads = (grads - inner_sums * units) / embed_len
    du_value = du[:, :n_tokens]
    du_query = du[:, n_tokens : n_tokens + pass_dev]
    up_query_part = ADAPTER_SCALE * jnp.einsum(
        "pr,pc->rc", query_lowrank.astype(jnp.float32), d_query_pre, precision=MATMUL_ACCURACY
    )
    up_value_part = ADAPTER_SCALE * jnp.einsum(
        "plr,plc->rc", value_lowrank.astype(jnp.float32), d_values, precision=MATMUL_ACCURACY
    )

    quarter = width // mp
    first_feature = place * quarter
    normed_quarter = lax.dynamic_slice_in_dim(
        normed.reshape(n_tokens, width), first_feature, quarter, 1
    )
    last_quarter = lax.dynamic_slice_in_dim(n_last, first_feature, quarter, 1)
    down_value_part = jnp.einsum(
        "rn,nd->rd", du_value, normed_quarter, preferred_element_type=jnp.float32
    )
    down_query_part = jnp.einsum(
        "rp,pd->rd", du_query, last_quarter, preferred_element_type=jnp.float32
    )
    down_part = jnp.concatenate([down_query_part, down_value_part], axis=0).reshape(dp, -1)
    head_part = jnp.concatenate(
        [up_query_part.reshape(dp, -1), up_value_part.reshape(dp, -1)], axis=1
    )
    loss_part = jnp.broadcast_to(local_total / dp, (dp, 1))
    parts = jnp.concatenate([down_part, head_part, loss_part], axis=1)
    n_down = down_part.shape[1]
    n_head = head_part.shape[1]
    padded = -(-parts.shape[1] // 128) * 128
    parts = jnp.pad(parts, ((0, 0), (0, padded - parts.shape[1]))).reshape(dp, 1, padded)
    reduced = jnp.sum(lax.all_to_all(parts, DP, 0, 0, tiled=True), axis=0)
    totals = spread(reduced, (*DP, "mp")).reshape(dp, mp, padded)
    grad_down = (
        totals[:, :, :n_down]
        .reshape(2 * rank, dp // (2 * rank), mp, n_down)
        .transpose(0, 2, 1, 3)
        .reshape(2 * rank, width)
    )
    grad_down_query = grad_down[:rank].T
    grad_down_value = grad_down[rank:].T
    own = lax.dynamic_index_in_dim(totals, place, axis=1, keepdims=False)
    n_up_query = q_cols * rank // dp
    grad_up_query = own[:, n_down : n_down + n_up_query].reshape(rank, q_cols)
    grad_up_value = own[:, n_down + n_up_query : n_down + n_head].reshape(rank, kv_cols)
    loss = jnp.sum(totals[:, 0, n_down + n_head]) / total_pairs

    d_kv_own = [d_kv_own[0]] + [after(blocks, reduced) for blocks in d_kv_own[1:]]
    kv_groups = [kv_own]
    kv_groups += [others[:, k * group_cols : (k + 1) * group_cols] for k in range(mp - 1)]
    x_local = lax.dynamic_slice_in_dim(layer_input, first_tok, tok_span, 1).astype(jnp.float32)
    rms_local = lax.dynamic_slice_in_dim(inv_rms, first_tok, tok_span, 1)
    du_local = lax.dynamic_slice_in_dim(
        du_value.reshape(rank, pass_dev, seq_len), first_tok, tok_span, 2
    )
    tok_ids = first_tok + lax.iota(jnp.int32, tok_span)
    at_local = (tok_ids[None, :] == last_pos[:, None])[:, :, None]
    d_normed = jnp.einsum(
        "rpt,dr->ptd", du_local, down_value, preferred_element_type=jnp.float32
    )
    query_adapter = jnp.einsum(
        "rp,dr->pd", du_query, down_query, preferred_element_type=jnp.float32
    )
    d_normed = d_normed + jnp.where(at_local, query_adapter[:, None, :], 0.0)
    for group in range(mp):
        term = jnp.einsum(
            "ptc,dc->ptd",
            d_kv_own[group],
            kv_groups[group],
            preferred_element_type=jnp.float32,
        )
        term = term + jnp.where(at_local, query_back_all[group][:, None, :], 0.0)
        d_normed = d_normed + term.astype(jnp.bfloat16).astype(jnp.float32)
    d_input = gain_in * d_normed * rms_local - x_local * rms_local**3 * jnp.mean(
        x_local * gain_in * d_normed, axis=-1, keepdims=True
    )
    d_input = d_input + jnp.where(at_local, d_hidden[:, None, :], 0.0)
    grad_input = d_input.astype(jnp.bfloat16)
    return (
        loss,
        embed_grads[0],
        embed_grads[1],
        embed_grads[2],
        grad_input,
        grad_down_query,
        grad_up_query,
        grad_down_value,
        grad_up_value,
    )


def solution(mesh):
    staged = Mesh(mesh.devices.reshape(4, 4, 2, 2, 4), (*DP, "mp"))
    in_specs = (
        P(DP, "mp"),
        P(DP, "mp"),
        P(DP, "mp"),
        P(DP),
        P(DP, None, None),
        P(DP),
        P(),
        P(),
        P(DP, "mp"),
        P(DP, "mp"),
        P(DP, "mp"),
        P("mp", DP),
        P(),
        P(None, "mp"),
        P(),
        P(None, "mp"),
    )
    out_specs = (
        P(),
        P(DP, "mp"),
        P(DP, "mp"),
        P(DP, "mp"),
        P(DP, "mp", None),
        P(),
        P(None, "mp"),
        P(),
        P(None, "mp"),
    )
    return jax.shard_map(
        on_device, mesh=staged, in_specs=in_specs, out_specs=out_specs, check_vma=False
    )
```
